32 devices in a mesh: groups: 2 (over y), tensor: 8 (over z, x), tokens: 2 (over core).
Axes of the slice: x: 2, y: 2, z: 4, core: 2. Of those that a mesh axis runs over, the one named last changes fastest.
Arguments:
- att_queries: bfloat16 [1024, 16384], P(('groups', 'tokens'), 'tensor'), parts along dimension 0, may hold values from -4.5 to 4.5
- att_keys: bfloat16 [1024, 8, 128], P(('groups', 'tokens')), parts along dimension 0, may hold values from -4.5 to 4.5
- att_values: bfloat16 [1024, 8, 128], P(('groups', 'tokens')), parts along dimension 0, may hold values from -4 to 4
- out_weight: bfloat16 [16384, 16384], P('tensor', 'tokens'), may hold values from -0.0625 to 0.0625
- residual: bfloat16 [1024, 16384], P(('groups', 'tokens'), 'tensor'), parts along dimension 0, may hold values from -4 to 4
- norm_gain: bfloat16 [16384], P('tensor'), may hold values from 0.25 to 1.75
- next_weight: bfloat16 [16384, 16384], P('tokens', 'tensor'), may hold values from -0.046875 to 0.046875
Outputs:
- resid_out: bfloat16 [1024, 16384], P(('groups', 'tokens'), 'tensor'), parts along dimension 0
- next_queries: bfloat16 [1024, 16384], P(('groups', 'tokens'), 'tensor'), parts along dimension 0
The draws below stay inside these ranges and needn't reach their ends.
There are 2 independent parts, one for each index of `groups`. The reference program is written for one: setup_inputs(seed, part) draws one part's arguments, and reference() takes and returns one part's arrays. A program takes and returns all parts, laid end to end along the dimension named above; an argument that names none is the same for every part. Nothing has to cross between parts.
All inputs are finite; a program needn't handle non-finite values. Where the reference program divides by a largest or mean magnitude, that divisor is 1e-20 or more.
Results may differ from the reference program's by a relative error of at most 0.013.
Values may be sent and summed in bfloat16 or wider, within the bound.
No kernel may reach another device: no remote copies, remote signals or barrier semaphores. Data moves between devices by JAX's collectives and lax.ppermute only.
A program may use at most 384 MiB of HBM per device.

```python
import math
import jax
import jax.numpy as jnp
from jax import lax

D = 16384
H = 128
KVH = 8
HD = 128
G = 128
SEQ = 512
N_TENSOR = 8


def draw_att_keys(key, part):
    key = jax.random.fold_in(key, 11)
    base = jnp.clip(jax.random.normal(key, (SEQ, KVH, HD), jnp.float32), -4.5, 4.5)
    return base.astype(jnp.bfloat16)


def draw_att_queries(key, part):
    key = jax.random.fold_in(key, 12)
    base = jnp.clip(jax.random.normal(key, (SEQ, H, HD), jnp.float32), -4.5, 4.5)
    return base.reshape(SEQ, H * HD).astype(jnp.bfloat16)


def draw_residual(key, part):
    key = jax.random.fold_in(key, 13)
    row_key = jax.random.fold_in(key, 0)
    noise_key = jax.random.fold_in(key, 1)
    jitter_key = jax.random.fold_in(key, 3)
    row_scale = 0.1 * jnp.exp(jax.random.uniform(row_key, (SEQ, 1), jnp.float32, 0.0, math.log(10.0)))
    jitter = jnp.exp(jax.random.uniform(jitter_key, (1, D), jnp.float32, -0.35, 0.35))
    ramp = jnp.arange(D, dtype=jnp.float32)[None, :] / D
    col_scale = jnp.exp((ramp - 1.0) * math.log(10.0)) * jitter
    noise = jnp.clip(jax.random.normal(noise_key, (SEQ, D), jnp.float32), -4.0, 4.0)
    values_drawn = jnp.clip(row_scale * col_scale * noise, -4.0, 4.0)
    return values_drawn.astype(jnp.bfloat16)


def strengthened(drawn, own_key, source, target, blocks, factor):
    def block_of(position):
        return (jnp.arange(drawn.shape[position]) // (drawn.shape[position] // blocks)).reshape((-1,) + (1,) * (drawn.ndim - 1 - position))

    first = jax.random.permutation(own_key, blocks)[block_of(target)]
    far = (block_of(target) + blocks // 2) % blocks
    return jnp.where((block_of(source) == first) | (block_of(source) == far), factor * drawn, drawn)


def level_of(own_key, extent, cuts, least, largest):
    level = 1.0
    for position, blocks in cuts:
        draws = jax.random.uniform(jax.random.fold_in(jax.random.fold_in(own_key, 6), position), (blocks,), jnp.float32, least / len(cuts), largest / len(cuts))
        level = level * jnp.repeat(jnp.exp(draws), extent[position] // blocks).reshape((-1,) + (1,) * (len(extent) - 1 - position))
    return level


def normal_values(stream_key, dims, deviation, reach, shards=(), kind=jnp.bfloat16):
    drawn = jax.random.normal(stream_key, dims, jnp.float32) * deviation
    if len(shards) > 0:
        drawn = level_of(stream_key, dims, shards, -0.22, 0.18) * drawn
    return jnp.clip(drawn, min=-reach, max=reach).astype(kind)


def noise_with(rng, dims, spread, most, cuts, heavy, held_as=jnp.bfloat16):
    array = spread * jax.random.normal(rng, dims, jnp.float32)
    if cuts:
        array = array * level_of(rng, dims, cuts, -0.22, 0.18)
    return jnp.clip(strengthened(array, jax.random.fold_in(rng, 3), *heavy), -most, most).astype(held_as)


def setup_inputs(seed: int = 0, part: int = 0) -> dict:
    key_list = jax.random.split(jax.random.key(seed), 8)
    part_splits = jax.random.split(jax.random.fold_in(key_list[7], part), 8)
    att_queries = draw_att_queries(jax.random.fold_in(jax.random.fold_in(key_list[7], part), 71), part)
    att_keys = draw_att_keys(jax.random.fold_in(jax.random.fold_in(key_list[7], part), 71), part)
    att_values = normal_values(part_splits[2], (SEQ, KVH, HD), 1.0, 4.0, ((0, 2),))
    out_weight = noise_with(key_list[3], (H * HD, D), (H * HD) ** -0.5, 0.0625, ((0, 8), (1, 2)), (0, 1, 8, 2.0))
    residual = draw_residual(jax.random.fold_in(jax.random.fold_in(key_list[7], part), 71), part)
    norm_gain = jnp.clip(1.0 + 0.15 * jax.random.normal(key_list[5], (D,), jnp.float32), 0.25, 1.75).astype(jnp.bfloat16)
    next_weight = normal_values(key_list[6], (D, H * HD), D ** -0.5, 0.046875, ((0, 2), (1, 8)))
    return dict(att_queries=att_queries, att_keys=att_keys, att_values=att_values, out_weight=out_weight, residual=residual, norm_gain=norm_gain, next_weight=next_weight)


def group_code(matrix):
    lead = matrix.shape[:-1]
    grouped = matrix.reshape(lead + (matrix.shape[-1] // G, G))
    scales = (lax.optimization_barrier(jnp.max(jnp.abs(grouped), axis=-1, keepdims=True)) + 1e-06).astype(jnp.bfloat16)
    coded = (grouped / scales.astype(jnp.float32)).astype(jnp.bfloat16)
    return (coded, scales)

def reference(att_queries, att_keys, att_values, out_weight, residual, norm_gain, next_weight):
    group_heads = H // KVH
    positions = jnp.arange(SEQ, dtype=jnp.int32)
    visible = positions[None, :] <= positions[:, None]
    inv_root = 1.0 / math.sqrt(HD)

    def one_head(head_index):
        kv_index = head_index // group_heads
        query = lax.dynamic_slice_in_dim(att_queries, (head_index * HD).astype(jnp.int32), HD, 1)
        key_rows = lax.dynamic_index_in_dim(att_keys, kv_index.astype(jnp.int32), 1, keepdims=False)
        value_rows = lax.dynamic_index_in_dim(att_values, kv_index.astype(jnp.int32), 1, keepdims=False)
        scores = jnp.dot(query, key_rows.T, preferred_element_type=jnp.float32) * inv_root
        scores = jnp.where(visible, scores, -1e+30)
        top = lax.optimization_barrier(jnp.max(scores, axis=1, keepdims=True))
        weights = jnp.where(visible, jnp.exp(scores - top), 0.0)
        total = lax.optimization_barrier(jnp.sum(weights, axis=1, keepdims=True))
        mixed_head = jnp.dot(weights.astype(jnp.bfloat16), value_rows, preferred_element_type=jnp.float32)
        return mixed_head / total
    heads_out = lax.map(one_head, jnp.arange(H, dtype=jnp.int32))
    attention = jnp.transpose(heads_out, (1, 0, 2)).reshape(SEQ, H * HD).astype(jnp.bfloat16)
    block_width = H * HD // N_TENSOR

    def accumulate(total, block):
        start = (block * block_width).astype(jnp.int32)
        rows = lax.dynamic_slice_in_dim(attention, start, block_width, 1)
        weight_rows = lax.dynamic_slice_in_dim(out_weight, start, block_width, 0)
        partial_value = jnp.dot(rows, weight_rows, preferred_element_type=jnp.float32)
        coded, scales = group_code(partial_value)
        return (total + coded.astype(jnp.float32) * scales.astype(jnp.float32), None)
    attn_out, _ = lax.scan(accumulate, jnp.zeros((SEQ, D // G, G), jnp.float32), jnp.arange(N_TENSOR, dtype=jnp.int32))
    mixed = residual.astype(jnp.float32) + attn_out.reshape(SEQ, D)
    resid_out = mixed.astype(jnp.bfloat16)
    mean_square = lax.optimization_barrier(jnp.mean(mixed * mixed, axis=1, keepdims=True))
    normed = mixed / jnp.sqrt(mean_square + 1e-05) * norm_gain.astype(jnp.float32)
    coded_n, scale_n = group_code(normed)
    inputs_next = (coded_n.astype(jnp.float32) * scale_n.astype(jnp.float32)).astype(jnp.bfloat16).reshape(SEQ, D)
    next_queries = jnp.dot(inputs_next, next_weight, preferred_element_type=jnp.float32).astype(jnp.bfloat16)
    return (resid_out, next_queries)
```

```python
import functools
import math

import jax
import jax.numpy as jnp
import numpy as np
from jax import lax
from jax.experimental import pallas as pl
from jax.experimental.pallas import tpu as pltpu
from jax.sharding import PartitionSpec as P

D = 16384
H = 128
KVH = 8
HD = 128
EPS_NORM = 1e-05
BF16 = jnp.bfloat16
F32 = jnp.float32
RING_LIMIT = 16
MIB = 1024 * 1024


def dot(a, b):
    return jnp.dot(a, b, preferred_element_type=F32)


def attention_kernel(heads, core_ref, q_ref, k_ref, v_ref, pk_ref, pv_ref, o_ref):
    rows = q_ref.shape[0]
    inv_root = 1.0 / math.sqrt(HD)
    query_pos = lax.broadcasted_iota(jnp.int32, (rows, rows), 0)
    key_pos = lax.broadcasted_iota(jnp.int32, (rows, rows), 1)
    visible = key_pos <= query_pos
    peer_visible = core_ref[0] == 1
    contract = (((1,), (1,)), ((), ()))
    for head in range(heads):
        columns = slice(head * HD, (head + 1) * HD)
        query = q_ref[:, columns]
        own = lax.dot_general(query, k_ref[...], contract, preferred_element_type=F32) * inv_root
        far = lax.dot_general(query, pk_ref[...], contract, preferred_element_type=F32) * inv_root
        own = jnp.where(visible, own, -1e30)
        far = jnp.where(peer_visible, far, -1e30)
        top = jnp.maximum(jnp.max(own, axis=1, keepdims=True), jnp.max(far, axis=1, keepdims=True))
        own = jnp.exp(own - top)
        far = jnp.exp(far - top)
        total = jnp.sum(own, axis=1, keepdims=True) + jnp.sum(far, axis=1, keepdims=True)
        mixed = dot(own.astype(BF16), v_ref[...]) + dot(far.astype(BF16), pv_ref[...])
        o_ref[:, columns] = (mixed / total).astype(BF16)


def attention(core, queries, keys, values, peer_keys, peer_values):
    rows, width = queries.shape
    heads = min(4, width // HD)
    whole = pl.BlockSpec((rows, HD), lambda h, s: (0, 0))
    part = pl.BlockSpec((rows, heads * HD), lambda h, s: (0, h))
    return pl.pallas_call(
        functools.partial(attention_kernel, heads),
        grid_spec=pltpu.PrefetchScalarGridSpec(
            num_scalar_prefetch=1,
            grid=(width // (heads * HD),),
            in_specs=[part, whole, whole, whole, whole],
            out_specs=part,
        ),
        out_shape=jax.ShapeDtypeStruct((rows, width), BF16),
        compiler_params=pltpu.CompilerParams(vmem_limit_bytes=24 * MIB),
        cost_estimate=pl.CostEstimate(
            flops=8 * rows * rows * width, bytes_accessed=4 * rows * width, transcendentals=2 * rows * rows * width // HD
        ),
        name="attention",
    )(core, queries, keys, values, peer_keys, peer_values)


def project_kernel(info_ref, x_ref, w_ref, own_ref, peer_ref):
    rows = own_ref.shape[0]
    result = dot(x_ref[...], w_ref[...]).astype(BF16)
    own_ref[...] = result[:rows]
    peer_ref[...] = result[rows:]


def project(info, pair, both, weight, width):
    depth = both.shape[1]
    rows = both.shape[0] // 2
    tile = min(512, width)
    tiles = width // tile
    out = pl.BlockSpec((rows, tile), lambda j, s: (0, j))
    return pl.pallas_call(
        project_kernel,
        grid_spec=pltpu.PrefetchScalarGridSpec(
            num_scalar_prefetch=1,
            grid=(tiles,),
            in_specs=[
                pl.BlockSpec((2 * rows, depth), lambda j, s: (0, 0)),
                pl.BlockSpec((depth, tile), lambda j, s: (0, s[pair] * tiles + j)),
            ],
            out_specs=[out, out],
        ),
        out_shape=[jax.ShapeDtypeStruct((rows, width), BF16)] * 2,
        compiler_params=pltpu.CompilerParams(vmem_limit_bytes=24 * MIB),
        cost_estimate=pl.CostEstimate(
            flops=4 * rows * depth * width, bytes_accessed=2 * depth * width, transcendentals=0
        ),
        name="project",
    )(info, both, weight)


def query_kernel(pieces, pair, half, first, info_ref, *refs):
    one, other, far = refs[:pieces], refs[pieces : 2 * pieces], refs[2 * pieces : 3 * pieces]
    w_ref = refs[3 * pieces]
    acc_refs = refs[3 * pieces + 1 : -3]
    own_ref, peer_ref, x_ref = refs[-3:]
    rows = own_ref.shape[0]
    width = one[0].shape[1]

    @pl.when(pl.program_id(0) == 0)
    def _():
        for piece in range(pieces):
            columns = slice(piece * width, (piece + 1) * width)

            @pl.when(info_ref[half + pair] == 1)
            def _():
                x_ref[:rows, columns] = one[piece][...]

            @pl.when(info_ref[half + pair] == 0)
            def _():
                x_ref[:rows, columns] = other[piece][...]

            x_ref[rows:, columns] = far[piece][...]

    result = dot(x_ref[...], w_ref[...])
    if first:
        own_ref[...] = result[:rows]
        peer_ref[...] = result[rows:].astype(peer_ref.dtype)
    else:
        own_ref[...] = acc_refs[0][...] + result[:rows]
        peer_ref[...] = (acc_refs[1][...] + result[rows:]).astype(peer_ref.dtype)


def query_block(info, pair, half, one, other, far, weight, acc, last):
    pieces = len(one)
    rows, piece_width = one[0].shape
    depth = pieces * piece_width
    width = weight.shape[1]
    tile = min(512, width)
    whole = pl.BlockSpec((rows, piece_width), lambda j, s: (0, 0))
    out = pl.BlockSpec((rows, tile), lambda j, s: (0, j))
    first = acc is None
    acc = () if first else acc
    return pl.pallas_call(
        functools.partial(query_kernel, pieces, pair, half, first),
        grid_spec=pltpu.PrefetchScalarGridSpec(
            num_scalar_prefetch=1,
            grid=(width // tile,),
            in_specs=[whole] * (3 * pieces)
            + [pl.BlockSpec((depth, tile), lambda j, s: (s[pair], j))]
            + [out] * len(acc),
            out_specs=[out, out],
            scratch_shapes=[pltpu.VMEM((2 * rows, depth), BF16)],
        ),
        out_shape=[
            jax.ShapeDtypeStruct((rows, width), F32),
            jax.ShapeDtypeStruct((rows, width), BF16 if last else F32),
        ],
        compiler_params=pltpu.CompilerParams(vmem_limit_bytes=32 * MIB),
        cost_estimate=pl.CostEstimate(
            flops=4 * rows * depth * width, bytes_accessed=2 * depth * width + 16 * rows * width, transcendentals=0
        ),
        name="next_query",
    )(info, *one, *other, *far, weight, *acc)


def ring_of(n):
    return [2 * p for p in range(n // 2)] + [2 * p + 1 for p in reversed(range(n // 2))]


def on_ring(n, att_queries, att_keys, att_values, out_weight, residual, norm_gain, next_weight):
    half = n // 2
    ring = ring_of(n)
    place = {chip: p for p, chip in enumerate(ring)}
    up = [(ring[p], ring[(p + 1) % n]) for p in range(n)]
    down = [(b, a) for a, b in up]
    swap = [(0, 1), (1, 0)]
    chip = lax.axis_index("tensor")
    core = lax.axis_index("tokens")
    rows, width = att_queries.shape
    pieces = 2 if width >= 256 else 1
    piece_width = residual.shape[1] // pieces

    table = np.zeros((n, 2, n), np.int32)
    for c in range(n):
        for k in range(half):
            near, far = ring[(place[c] + k) % n], ring[(place[c] + k + half) % n]
            for h in range(2):
                mine = near // half == h
                assert mine != (far // half == h)
                table[c, h, k] = (near if mine else far) - h * half
                table[c, h, half + k] = mine
    info = lax.dynamic_index_in_dim(jnp.asarray(table.reshape(2 * n, n)), chip * 2 + core, 0, keepdims=False)
    near_mine = [info[half + k] == 1 for k in range(half)]

    heads_here = width // HD
    kv_head = chip * heads_here // (H // KVH)
    own_keys = lax.dynamic_index_in_dim(att_keys, kv_head, 1, keepdims=False)
    own_values = lax.dynamic_index_in_dim(att_values, kv_head, 1, keepdims=False)
    peer_keys = lax.ppermute(own_keys, "tokens", swap)
    peer_values = lax.ppermute(own_values, "tokens", swap)
    attended = attention(core[None], att_queries, own_keys, own_values, peer_keys, peer_values)
    both = jnp.concatenate([attended, lax.ppermute(attended, "tokens", swap)], axis=0)

    mine, swapped = {}, {}
    order = [0] + [k for j in range(1, half) for k in (half - j, j) if k not in range(0, 1)]
    order = list(dict.fromkeys(order))
    for k in order:
        mine[k], outgoing = project(info, k, both, out_weight, residual.shape[1])
        swapped[k] = lax.ppermute(outgoing, "tokens", swap)

    def columns_of(array, piece):
        return array[:, piece * piece_width : (piece + 1) * piece_width]

    def block(q, piece):
        k = q % half
        near = near_mine[k] if q == k else jnp.logical_not(near_mine[k])
        return jnp.where(near, columns_of(mine[k], piece), columns_of(swapped[k], piece)).astype(F32)

    hops = [(half, half - 1) if piece % 2 == 0 else (half - 1, half) for piece in range(pieces)]
    arrived = {}
    for step in range(1, half + 1):
        for piece in range(pieces):
            for way, pairs in ((0, up), (1, down)):
                length = hops[piece][way]
                if step > length:
                    continue
                q = length - step + 1
                value = block(q if way == 0 else -q, piece)
                if step > 1:
                    value = value + arrived[piece, way].astype(F32)
                arrived[piece, way] = lax.ppermute(value.astype(BF16), "tensor", pairs)

    resid, scaled = [], []
    squares = jnp.zeros((rows,), F32)
    for piece in range(pieces):
        mixed = columns_of(residual, piece).astype(F32) + block(0, piece)
        for way in range(2):
            if hops[piece][way]:
                mixed = mixed + arrived[piece, way].astype(F32)
        resid.append(mixed.astype(BF16))
        gain = norm_gain[piece * piece_width : (piece + 1) * piece_width].astype(F32)
        scaled.append((mixed * gain).astype(BF16))
        squares = squares + jnp.sum(mixed * mixed, axis=1)
    resid_out = jnp.concatenate(resid, axis=1)

    held = {(piece, 0): scaled[piece] for piece in range(pieces)}
    for step in range(1, half + 1):
        for piece in range(pieces):
            for way, pairs in ((0, up), (1, down)):
                if step > hops[piece][way]:
                    continue
                sign = -1 if way == 0 else 1
                source = (piece, sign * (step - 1))
                target = sign * step
                value = lax.ppermute(held[source], "tensor", pairs)
                held[piece, target] = value
                if abs(target) == half:
                    held[piece, half] = held[piece, -half] = value
    distance = half
    while distance >= 1:
        shifted = [(ring[p], ring[(p + distance) % n]) for p in range(n)]
        squares = squares + lax.ppermute(squares, "tensor", shifted)
        distance //= 2

    acc = None
    when = sorted(range(half), key=lambda k: max(k, half - k))
    for k in when:
        one = [held[piece, k] for piece in range(pieces)]
        other = [held[piece, k - half] for piece in range(pieces)]
        far = [
            lax.ppermute(jnp.where(near_mine[k], other[piece], one[piece]), "tokens", swap) for piece in range(pieces)
        ]
        acc = query_block(info, k, half, one, other, far, next_weight, acc, k == when[-1])
    query_sum = acc[0] + lax.ppermute(acc[1], "tokens", swap).astype(F32)
    factor = 1.0 / jnp.sqrt(squares / D + EPS_NORM)
    return (resid_out, (query_sum * factor[:, None]).astype(BF16))


def on_mesh(n, att_queries, att_keys, att_values, out_weight, residual, norm_gain, next_weight):
    rows, width = att_queries.shape
    swap = [(0, 1), (1, 0)]
    chip = lax.axis_index("tensor")
    core = lax.axis_index("tokens")
    kv_head = chip * (width // HD) // (H // KVH)
    own_keys = lax.dynamic_index_in_dim(att_keys, kv_head, 1, keepdims=False)
    own_values = lax.dynamic_index_in_dim(att_values, kv_head, 1, keepdims=False)
    peer_keys = lax.ppermute(own_keys, "tokens", swap)
    peer_values = lax.ppermute(own_values, "tokens", swap)
    attended = attention(core[None], att_queries, own_keys, own_values, peer_keys, peer_values)
    both = lax.all_gather(attended, "tokens", axis=0, tiled=True)
    partial = dot(both, out_weight).astype(BF16)
    partial = lax.all_to_all(partial, "tokens", split_axis=0, concat_axis=1, tiled=True)
    attn_out = lax.psum_scatter(partial.astype(F32), "tensor", scatter_dimension=1, tiled=True)
    mixed = residual.astype(F32) + attn_out
    total_squares = lax.psum(jnp.sum(mixed * mixed, axis=1), "tensor")
    factor = 1.0 / jnp.sqrt(total_squares / D + EPS_NORM)
    normed = (mixed * factor[:, None] * norm_gain.astype(F32)).astype(BF16)
    gathered = lax.all_gather(normed, "tensor", axis=1, tiled=True)
    halves = lax.all_to_all(gathered, "tokens", split_axis=1, concat_axis=0, tiled=True)
    query_sum = lax.psum_scatter(dot(halves, next_weight), "tokens", scatter_dimension=0, tiled=True)
    return (mixed.astype(BF16), query_sum.astype(BF16))


def solution(mesh):
    n = mesh.shape["tensor"]
    in_specs = (
        P(("groups", "tokens"), "tensor"),
        P(("groups", "tokens"), None, None),
        P(("groups", "tokens"), None, None),
        P("tensor", "tokens"),
        P(("groups", "tokens"), "tensor"),
        P("tensor"),
        P("tokens", "tensor"),
    )
    out_specs = (P(("groups", "tokens"), "tensor"), P(("groups", "tokens"), "tensor"))
    body = functools.partial(on_ring if n <= RING_LIMIT else on_mesh, n)
    return jax.shard_map(body, mesh=mesh, in_specs=in_specs, out_specs=out_specs, check_vma=False)
```

```python
import functools
import math

import jax
import jax.numpy as jnp
import numpy as np
from jax import lax
from jax.experimental import pallas as pl
from jax.experimental.pallas import tpu as pltpu
from jax.sharding import PartitionSpec as P

D = 16384
H = 128
KVH = 8
HD = 128
EPS_NORM = 1e-05
BF16 = jnp.bfloat16
F32 = jnp.float32
RING_LIMIT = 16
MIB = 1024 * 1024


def dot(a, b):
    return jnp.dot(a, b, preferred_element_type=F32)


def attention_kernel(heads, core_ref, q_ref, k_ref, v_ref, pk_ref, pv_ref, *refs):
    o_ref = refs[-1]
    rows = q_ref.shape[0]
    inv_root = 1.0 / math.sqrt(HD)
    query_pos = lax.broadcasted_iota(jnp.int32, (rows, rows), 0)
    key_pos = lax.broadcasted_iota(jnp.int32, (rows, rows), 1)
    visible = key_pos <= query_pos
    peer_visible = core_ref[0] == 1
    contract = (((1,), (1,)), ((), ()))
    for head in range(heads):
        columns = slice(head * HD, (head + 1) * HD)
        query = q_ref[:, columns]
        own = lax.dot_general(query, k_ref[...], contract, preferred_element_type=F32) * inv_root
        far = lax.dot_general(query, pk_ref[...], contract, preferred_element_type=F32) * inv_root
        own = jnp.where(visible, own, -1e30)
        far = jnp.where(peer_visible, far, -1e30)
        top = jnp.maximum(jnp.max(own, axis=1, keepdims=True), jnp.max(far, axis=1, keepdims=True))
        own = jnp.exp(own - top)
        far = jnp.exp(far - top)
        total = jnp.sum(own, axis=1, keepdims=True) + jnp.sum(far, axis=1, keepdims=True)
        mixed = dot(own.astype(BF16), v_ref[...]) + dot(far.astype(BF16), pv_ref[...])
        o_ref[:, columns] = (mixed / total).astype(BF16)


def attention(core, queries, keys, values, peer_keys, peer_values, after=()):
    queries, index, count = queries
    rows, width = queries.shape
    width = width // count
    heads = min(4, width // HD)
    first = index * width // (heads * HD)
    whole = pl.BlockSpec((rows, HD), lambda h, s: (0, 0))
    wanted = pl.BlockSpec((rows, heads * HD), lambda h, s: (0, first + h))
    part = pl.BlockSpec((rows, heads * HD), lambda h, s: (0, h))
    return pl.pallas_call(
        functools.partial(attention_kernel, heads),
        grid_spec=pltpu.PrefetchScalarGridSpec(
            num_scalar_prefetch=1,
            grid=(width // (heads * HD),),
            in_specs=[wanted, whole, whole, whole, whole] + [pl.BlockSpec(memory_space=pl.ANY)] * len(after),
            out_specs=part,
        ),
        out_shape=jax.ShapeDtypeStruct((rows, width), BF16),
        compiler_params=pltpu.CompilerParams(vmem_limit_bytes=24 * MIB),
        cost_estimate=pl.CostEstimate(
            flops=8 * rows * rows * width, bytes_accessed=4 * rows * width, transcendentals=2 * rows * rows * width // HD
        ),
        name="attention",
    )(core, queries, keys, values, peer_keys, peer_values, *after)


def project_kernel(parts, info_ref, *refs):
    own, peer = refs[:parts], refs[parts : 2 * parts]
    w_ref = refs[2 * parts]
    own_ref, peer_ref, x_ref, sum_ref = refs[-4:]
    rows = own_ref.shape[0]
    width = own[0].shape[1]
    depth = w_ref.shape[0]
    step = pl.program_id(0)

    @pl.when(step == 0)
    def _():
        for part in range(parts):
            columns = slice(part * width, (part + 1) * width)
            x_ref[:rows, columns] = own[part][...]
            x_ref[rows:, columns] = peer[part][...]

    chunk = x_ref[:, pl.ds(pl.multiple_of(step * depth, depth), depth)]
    result = dot(chunk, w_ref[...])

    @pl.when(step == 0)
    def _():
        sum_ref[...] = result

    @pl.when(step > 0)
    def _():
        total = (sum_ref[...] + result).astype(BF16)
        own_ref[...] = total[:rows]
        peer_ref[...] = total[rows:]


def project(info, pair, pieces, piece, own, peer, weight, width, after):
    rows, part_width = own[0].shape
    parts = len(own)
    depth = parts * part_width
    whole = pl.BlockSpec((rows, part_width), lambda j, s: (0, 0))
    out = pl.BlockSpec((rows, width), lambda j, s: (0, 0))
    return pl.pallas_call(
        functools.partial(project_kernel, parts),
        grid_spec=pltpu.PrefetchScalarGridSpec(
            num_scalar_prefetch=1,
            grid=(2,),
            in_specs=[whole] * (2 * parts)
            + [pl.BlockSpec((depth // 2, width), lambda j, s: (j, s[pair] * pieces + piece))]
            + [pl.BlockSpec(memory_space=pl.ANY)] * len(after),
            out_specs=[out, out],
            scratch_shapes=[pltpu.VMEM((2 * rows, depth), BF16), pltpu.VMEM((2 * rows, width), F32)],
        ),
        out_shape=[jax.ShapeDtypeStruct((rows, width), BF16)] * 2,
        compiler_params=pltpu.CompilerParams(vmem_limit_bytes=20 * MIB),
        cost_estimate=pl.CostEstimate(
            flops=4 * rows * depth * width, bytes_accessed=2 * depth * width, transcendentals=0
        ),
        name="project",
    )(info, *own, *peer, weight, *after)


def query_kernel(pieces, pair, half, first, info_ref, *refs):
    one, other, far = refs[:pieces], refs[pieces : 2 * pieces], refs[2 * pieces : 3 * pieces]
    w_ref = refs[3 * pieces]
    acc_refs = () if first else refs[3 * pieces + 1 : 3 * pieces + 3]
    own_ref, peer_ref, info_out, x_ref = refs[-4:]
    rows = own_ref.shape[0]
    width = one[0].shape[1]

    @pl.when(pl.program_id(0) == 0)
    def _():
        for index in range(2 * half):
            info_out[index] = info_ref[index]
        for piece in range(pieces):
            columns = slice(piece * width, (piece + 1) * width)

            @pl.when(info_ref[half + pair] == 1)
            def _():
                x_ref[:rows, columns] = one[piece][...]

            @pl.when(info_ref[half + pair] == 0)
            def _():
                x_ref[:rows, columns] = other[piece][...]

            x_ref[rows:, columns] = far[piece][...]

    result = dot(x_ref[...], w_ref[...])
    if first:
        own_ref[...] = result[:rows]
        peer_ref[...] = result[rows:].astype(peer_ref.dtype)
    else:
        own_ref[...] = acc_refs[0][...] + result[:rows]
        peer_ref[...] = (acc_refs[1][...] + result[rows:]).astype(peer_ref.dtype)


def query_block(info, pair, half, one, other, far, weight, acc, last, after):
    pieces = len(one)
    rows, piece_width = one[0].shape
    depth = pieces * piece_width
    width = weight.shape[1]
    tile = min(1024, width)
    whole = pl.BlockSpec((rows, piece_width), lambda j, s: (0, 0))
    out = pl.BlockSpec((rows, tile), lambda j, s: (0, j))
    first = acc is None
    acc = () if first else acc
    return pl.pallas_call(
        functools.partial(query_kernel, pieces, pair, half, first),
        grid_spec=pltpu.PrefetchScalarGridSpec(
            num_scalar_prefetch=1,
            grid=(width // tile,),
            in_specs=[whole] * (3 * pieces)
            + [pl.BlockSpec((depth, tile), lambda j, s: (s[pair], j))]
            + [out] * len(acc)
            + [pl.BlockSpec(memory_space=pl.ANY)] * len(after),
            out_specs=[out, out, pl.BlockSpec(memory_space=pltpu.SMEM)],
            scratch_shapes=[pltpu.VMEM((2 * rows, depth), BF16)],
        ),
        out_shape=[
            jax.ShapeDtypeStruct((rows, width), F32),
            jax.ShapeDtypeStruct((rows, width), BF16 if last else F32),
            jax.ShapeDtypeStruct(info.shape, jnp.int32),
        ],
        compiler_params=pltpu.CompilerParams(vmem_limit_bytes=30 * MIB),
        cost_estimate=pl.CostEstimate(
            flops=4 * rows * depth * width, bytes_accessed=2 * depth * width + 16 * rows * width, transcendentals=0
        ),
        name="next_query",
    )(info, *one, *other, *far, weight, *acc, *after)


def ring_of(n):
    return [2 * p for p in range(n // 2)] + [2 * p + 1 for p in reversed(range(n // 2))]


def on_ring(n, att_queries, att_keys, att_values, out_weight, residual, norm_gain, next_weight):
    half = n // 2
    ring = ring_of(n)
    place = {chip: p for p, chip in enumerate(ring)}
    up = [(ring[p], ring[(p + 1) % n]) for p in range(n)]
    down = [(b, a) for a, b in up]
    swap = [(0, 1), (1, 0)]
    chip = lax.axis_index("tensor")
    core = lax.axis_index("tokens")
    rows, width = att_queries.shape
    pieces = 2 if width >= 256 else 1
    piece_width = residual.shape[1] // pieces

    table = np.zeros((n, 2, n), np.int32)
    for c in range(n):
        for k in range(half):
            near, far = ring[(place[c] + k) % n], ring[(place[c] + k + half) % n]
            for h in range(2):
                mine = near // half == h
                assert mine != (far // half == h)
                table[c, h, k] = (near if mine else far) - h * half
                table[c, h, half + k] = mine
    info = lax.dynamic_index_in_dim(jnp.asarray(table.reshape(2 * n, n)), chip * 2 + core, 0, keepdims=False)
    def is_near(index, k):
        return index[half + k] == 1

    heads_here = width // HD
    kv_head = chip * heads_here // (H // KVH)
    own_keys = lax.dynamic_index_in_dim(att_keys, kv_head, 1, keepdims=False)
    own_values = lax.dynamic_index_in_dim(att_values, kv_head, 1, keepdims=False)
    peer_keys = lax.ppermute(own_keys, "tokens", swap)
    peer_values = lax.ppermute(own_values, "tokens", swap)
    attended, attended_peer = [], []
    for part in range(2):
        queries = (att_queries, part, 2)
        attended.append(attention(core[None], queries, own_keys, own_values, peer_keys, peer_values, attended))
        attended_peer.append(lax.ppermute(attended[-1], "tokens", swap))

    def columns_of(array, piece):
        return array[:, piece * piece_width : (piece + 1) * piece_width]

    hops = [(half, half - 1) if piece % 2 == 0 else (half - 1, half) for piece in range(pieces)]
    chains = [(piece, way) for way in range(2) for piece in range(pieces)]
    chains = sorted(chains, key=lambda c: (c[0] + c[1]) % 2)
    events = [
        (piece, way, step) for step in range(1, half + 1) for piece, way in chains if step <= hops[piece][way]
    ]

    def place_of(piece, way, step):
        q = hops[piece][way] - step + 1
        return q if way == 0 else -q

    order = list(dict.fromkeys([(place_of(*event) % half, event[0]) for event in events] + [(0, p) for p in range(pieces)]))
    made = {}

    def make(after):
        if len(made) < len(order):
            k, piece = order[len(made)]
            mine, outgoing = project(
                info, k, pieces, piece, attended, attended_peer, out_weight, piece_width, after
            )
            made[k, piece] = (mine, lax.ppermute(outgoing, "tokens", swap))

    def block(q, piece):
        mine, swapped = made[q % half, piece]
        near = is_near(info, q % half) if q == q % half else jnp.logical_not(is_near(info, q % half))
        return jnp.where(near, mine, swapped).astype(F32)

    arrived = {}
    make(())
    make(())
    for piece, way, step in events:
        value = block(place_of(piece, way, step), piece)
        if step > 1:
            value = value + arrived[piece, way].astype(F32)
        value = value.astype(BF16)
        arrived[piece, way] = lax.ppermute(value, "tensor", up if way == 0 else down)
        make((value,))

    resid, scaled = [], []
    squares = jnp.zeros((rows,), F32)
    for piece in range(pieces):
        mixed = columns_of(residual, piece).astype(F32) + block(0, piece)
        for way in range(2):
            if hops[piece][way]:
                mixed = mixed + arrived[piece, way].astype(F32)
        resid.append(mixed.astype(BF16))
        gain = norm_gain[piece * piece_width : (piece + 1) * piece_width].astype(F32)
        scaled.append((mixed * gain).astype(BF16))
        squares = squares + jnp.sum(mixed * mixed, axis=1)
    resid_out = jnp.concatenate(resid, axis=1)

    held = {(piece, 0): scaled[piece] for piece in range(pieces)}
    for step in range(1, half + 1):
        for piece in range(pieces):
            for way, pairs in ((0, up), (1, down)):
                if step > hops[piece][way]:
                    continue
                sign = -1 if way == 0 else 1
                source = (piece, sign * (step - 1))
                target = sign * step
                value = lax.ppermute(held[source], "tensor", pairs)
                held[piece, target] = value
                if abs(target) == half:
                    held[piece, half] = held[piece, -half] = value
    distance = half
    totals = []
    while distance >= 1:
        shifted = [(ring[p], ring[(p + distance) % n]) for p in range(n)]
        squares = squares + lax.ppermute(squares, "tensor", shifted)
        totals.append(squares)
        distance //= 2

    acc = None
    when = sorted(range(half), key=lambda k: max(k, half - k))
    indices = [info, info]
    for count, k in enumerate(when):
        one = [held[piece, k] for piece in range(pieces)]
        other = [held[piece, k - half] for piece in range(pieces)]
        near = is_near(indices[-2] if count > 1 else indices[-1], k)
        far = [lax.ppermute(jnp.where(near, other[piece], one[piece]), "tokens", swap) for piece in range(pieces)]
        *acc, index = query_block(
            info, k, half, one, other, far, next_weight, acc, k == when[-1], totals[max(count - 1, 0) : count]
        )
        indices.append(index)
    query_sum = acc[0] + lax.ppermute(acc[1], "tokens", swap).astype(F32)
    factor = 1.0 / jnp.sqrt(squares / D + EPS_NORM)
    return (resid_out, (query_sum * factor[:, None]).astype(BF16))


def on_mesh(n, att_queries, att_keys, att_values, out_weight, residual, norm_gain, next_weight):
    rows, width = att_queries.shape
    swap = [(0, 1), (1, 0)]
    chip = lax.axis_index("tensor")
    core = lax.axis_index("tokens")
    kv_head = chip * (width // HD) // (H // KVH)
    own_keys = lax.dynamic_index_in_dim(att_keys, kv_head, 1, keepdims=False)
    own_values = lax.dynamic_index_in_dim(att_values, kv_head, 1, keepdims=False)
    peer_keys = lax.ppermute(own_keys, "tokens", swap)
    peer_values = lax.ppermute(own_values, "tokens", swap)
    attended = attention(core[None], (att_queries, 0, 1), own_keys, own_values, peer_keys, peer_values)
    both = lax.all_gather(attended, "tokens", axis=0, tiled=True)
    partial = dot(both, out_weight).astype(BF16)
    partial = lax.all_to_all(partial, "tokens", split_axis=0, concat_axis=1, tiled=True)
    attn_out = lax.psum_scatter(partial.astype(F32), "tensor", scatter_dimension=1, tiled=True)
    mixed = residual.astype(F32) + attn_out
    total_squares = lax.psum(jnp.sum(mixed * mixed, axis=1), "tensor")
    factor = 1.0 / jnp.sqrt(total_squares / D + EPS_NORM)
    normed = (mixed * factor[:, None] * norm_gain.astype(F32)).astype(BF16)
    gathered = lax.all_gather(normed, "tensor", axis=1, tiled=True)
    halves = lax.all_to_all(gathered, "tokens", split_axis=1, concat_axis=0, tiled=True)
    query_sum = lax.psum_scatter(dot(halves, next_weight), "tokens", scatter_dimension=0, tiled=True)
    return (mixed.astype(BF16), query_sum.astype(BF16))


def solution(mesh):
    n = mesh.shape["tensor"]
    in_specs = (
        P(("groups", "tokens"), "tensor"),
        P(("groups", "tokens"), None, None),
        P(("groups", "tokens"), None, None),
        P("tensor", "tokens"),
        P(("groups", "tokens"), "tensor"),
        P("tensor"),
        P("tokens", "tensor"),
    )
    out_specs = (P(("groups", "tokens"), "tensor"), P(("groups", "tokens"), "tensor"))
    body = functools.partial(on_ring if n <= RING_LIMIT else on_mesh, n)
    return jax.shard_map(body, mesh=mesh, in_specs=in_specs, out_specs=out_specs, check_vma=False)
```

```python
import functools
import math

import jax
import jax.numpy as jnp
import numpy as np
from jax import lax
from jax.experimental import pallas as pl
from jax.experimental.pallas import tpu as pltpu
from jax.sharding import PartitionSpec as P

D = 16384
H = 128
KVH = 8
HD = 128
EPS_NORM = 1e-05
BF16 = jnp.bfloat16
F32 = jnp.float32
RING_LIMIT = 16
MIB = 1024 * 1024


def dot(a, b):
    return jnp.dot(a, b, preferred_element_type=F32)


def attention_kernel(heads, core_ref, q_ref, k_ref, v_ref, pk_ref, pv_ref, *refs):
    o_ref = refs[-1]
    rows = q_ref.shape[0]
    inv_root = 1.0 / math.sqrt(HD)
    query_pos = lax.broadcasted_iota(jnp.int32, (rows, rows), 0)
    key_pos = lax.broadcasted_iota(jnp.int32, (rows, rows), 1)
    visible = key_pos <= query_pos
    peer_visible = core_ref[0] == 1
    contract = (((1,), (1,)), ((), ()))
    for head in range(heads):
        columns = slice(head * HD, (head + 1) * HD)
        query = q_ref[:, columns]
        own = lax.dot_general(query, k_ref[...], contract, preferred_element_type=F32) * inv_root
        far = lax.dot_general(query, pk_ref[...], contract, preferred_element_type=F32) * inv_root
        own = jnp.where(visible, own, -1e30)
        far = jnp.where(peer_visible, far, -1e30)
        top = jnp.maximum(jnp.max(own, axis=1, keepdims=True), jnp.max(far, axis=1, keepdims=True))
        own = jnp.exp(own - top)
        far = jnp.exp(far - top)
        total = jnp.sum(own, axis=1, keepdims=True) + jnp.sum(far, axis=1, keepdims=True)
        mixed = dot(own.astype(BF16), v_ref[...]) + dot(far.astype(BF16), pv_ref[...])
        o_ref[:, columns] = (mixed / total).astype(BF16)


def attention(core, queries, keys, values, peer_keys, peer_values, after=()):
    queries, index, count = queries
    rows, width = queries.shape
    width = width // count
    heads = min(4, width // HD)
    first = index * width // (heads * HD)
    whole = pl.BlockSpec((rows, HD), lambda h, s: (0, 0))
    wanted = pl.BlockSpec((rows, heads * HD), lambda h, s: (0, first + h))
    part = pl.BlockSpec((rows, heads * HD), lambda h, s: (0, h))
    return pl.pallas_call(
        functools.partial(attention_kernel, heads),
        grid_spec=pltpu.PrefetchScalarGridSpec(
            num_scalar_prefetch=1,
            grid=(width // (heads * HD),),
            in_specs=[wanted, whole, whole, whole, whole] + [pl.BlockSpec(memory_space=pl.ANY)] * len(after),
            out_specs=part,
        ),
        out_shape=jax.ShapeDtypeStruct((rows, width), BF16),
        compiler_params=pltpu.CompilerParams(vmem_limit_bytes=24 * MIB),
        cost_estimate=pl.CostEstimate(
            flops=8 * rows * rows * width, bytes_accessed=4 * rows * width, transcendentals=2 * rows * rows * width // HD
        ),
        name="attention",
    )(core, queries, keys, values, peer_keys, peer_values, *after)


def project_kernel(info_ref, x_ref, w_ref, *refs):
    own_ref, peer_ref = refs[-2:]
    rows = own_ref.shape[0]
    result = dot(x_ref[...], w_ref[...]).astype(BF16)
    own_ref[...] = result[:rows]
    peer_ref[...] = result[rows:]


def project(info, pair, pieces, piece, both, weight, width, after):
    rows, depth = both.shape
    rows = rows // 2
    tile = min(512, width)
    tiles = width // tile
    out = pl.BlockSpec((rows, tile), lambda j, s: (0, j))
    return pl.pallas_call(
        project_kernel,
        grid_spec=pltpu.PrefetchScalarGridSpec(
            num_scalar_prefetch=1,
            grid=(tiles,),
            in_specs=[
                pl.BlockSpec(memory_space=pltpu.VMEM),
                pl.BlockSpec((depth, tile), lambda j, s: (0, (s[pair] * pieces + piece) * tiles + j)),
            ]
            + [pl.BlockSpec(memory_space=pl.ANY)] * len(after),
            out_specs=[out, out],
        ),
        out_shape=[jax.ShapeDtypeStruct((rows, width), BF16)] * 2,
        compiler_params=pltpu.CompilerParams(vmem_limit_bytes=34 * MIB),
        cost_estimate=pl.CostEstimate(
            flops=4 * rows * depth * width, bytes_accessed=2 * depth * width, transcendentals=0
        ),
        name="project",
    )(info, both, weight, *after)


def query_kernel(pieces, pair, half, first, count, info_ref, *refs):
    one, other, far = refs[:pieces], refs[pieces : 2 * pieces], refs[2 * pieces : 3 * pieces]
    w_ref = refs[3 * pieces]
    acc_refs = () if first else refs[3 * pieces + 1 : 3 * pieces + 3]
    squares = refs[len(refs) - 5 - count : len(refs) - 5]
    own_ref, peer_ref, info_out, squares_out, x_ref = refs[-5:]
    rows = own_ref.shape[0]
    width = one[0].shape[1]

    @pl.when(pl.program_id(0) == 0)
    def _():
        for index in range(2 * half):
            info_out[index] = info_ref[index]
        total = squares[0][...]
        for more in squares[1:]:
            total = total + more[...]
        squares_out[...] = total
        for piece in range(pieces):
            columns = slice(piece * width, (piece + 1) * width)

            @pl.when(info_ref[half + pair] == 1)
            def _():
                x_ref[:rows, columns] = one[piece][...]

            @pl.when(info_ref[half + pair] == 0)
            def _():
                x_ref[:rows, columns] = other[piece][...]

            x_ref[rows:, columns] = far[piece][...]

    result = dot(x_ref[...], w_ref[...])
    if first:
        own_ref[...] = result[:rows]
        peer_ref[...] = result[rows:].astype(peer_ref.dtype)
    else:
        own_ref[...] = acc_refs[0][...] + result[:rows]
        peer_ref[...] = (acc_refs[1][...] + result[rows:]).astype(peer_ref.dtype)


def query_block(info, pair, half, one, other, far, weight, acc, last, squares):
    pieces = len(one)
    rows, piece_width = one[0].shape
    depth = pieces * piece_width
    width = weight.shape[1]
    tile = min(512, width)
    whole = pl.BlockSpec(memory_space=pltpu.VMEM)
    out = pl.BlockSpec((rows, tile), lambda j, s: (0, j))
    first = acc is None
    acc = () if first else acc
    return pl.pallas_call(
        functools.partial(query_kernel, pieces, pair, half, first, len(squares)),
        grid_spec=pltpu.PrefetchScalarGridSpec(
            num_scalar_prefetch=1,
            grid=(width // tile,),
            in_specs=[whole] * (3 * pieces)
            + [pl.BlockSpec((depth, tile), lambda j, s: (s[pair], j))]
            + [out] * len(acc)
            + [whole] * len(squares),
            out_specs=[out, out, pl.BlockSpec(memory_space=pltpu.SMEM), whole],
            scratch_shapes=[pltpu.VMEM((2 * rows, depth), BF16)],
        ),
        out_shape=[
            jax.ShapeDtypeStruct((rows, width), F32),
            jax.ShapeDtypeStruct((rows, width), BF16 if last else F32),
            jax.ShapeDtypeStruct(info.shape, jnp.int32),
            jax.ShapeDtypeStruct(squares[0].shape, F32),
        ],
        compiler_params=pltpu.CompilerParams(vmem_limit_bytes=34 * MIB),
        cost_estimate=pl.CostEstimate(
            flops=4 * rows * depth * width, bytes_accessed=2 * depth * width + 16 * rows * width, transcendentals=0
        ),
        name="next_query",
    )(info, *one, *other, *far, weight, *acc, *squares)


def ring_of(n):
    return [2 * p for p in range(n // 2)] + [2 * p + 1 for p in reversed(range(n // 2))]


def on_ring(n, att_queries, att_keys, att_values, out_weight, residual, norm_gain, next_weight):
    half = n // 2
    ring = ring_of(n)
    place = {chip: p for p, chip in enumerate(ring)}
    up = [(ring[p], ring[(p + 1) % n]) for p in range(n)]
    down = [(b, a) for a, b in up]
    swap = [(0, 1), (1, 0)]
    chip = lax.axis_index("tensor")
    core = lax.axis_index("tokens")
    rows, width = att_queries.shape
    pieces = 2 if width >= 256 else 1
    piece_width = residual.shape[1] // pieces

    table = np.zeros((n, 2, n), np.int32)
    for c in range(n):
        for k in range(half):
            near, far = ring[(place[c] + k) % n], ring[(place[c] + k + half) % n]
            for h in range(2):
                mine = near // half == h
                assert mine != (far // half == h)
                table[c, h, k] = (near if mine else far) - h * half
                table[c, h, half + k] = mine
    info = lax.dynamic_index_in_dim(jnp.asarray(table.reshape(2 * n, n)), chip * 2 + core, 0, keepdims=False)
    def is_near(index, k):
        return index[half + k] == 1

    heads_here = width // HD
    kv_head = chip * heads_here // (H // KVH)
    own_keys = lax.dynamic_index_in_dim(att_keys, kv_head, 1, keepdims=False)
    own_values = lax.dynamic_index_in_dim(att_values, kv_head, 1, keepdims=False)
    peer_keys = lax.ppermute(own_keys, "tokens", swap)
    peer_values = lax.ppermute(own_values, "tokens", swap)
    attended, attended_peer = [], []
    for part in range(2):
        queries = (att_queries, part, 2)
        attended.append(attention(core[None], queries, own_keys, own_values, peer_keys, peer_values, attended))
        attended_peer.append(lax.ppermute(attended[-1], "tokens", swap))

    both = jnp.concatenate(
        [jnp.concatenate(attended, axis=1), jnp.concatenate(attended_peer, axis=1)], axis=0
    )

    def columns_of(array, piece):
        return array[:, piece * piece_width : (piece + 1) * piece_width]

    hops = [(half, half - 1) if piece % 2 == 0 else (half - 1, half) for piece in range(pieces)]
    chains = [(piece, way) for way in range(2) for piece in range(pieces)]
    chains = sorted(chains, key=lambda c: (c[0] + c[1]) % 2)
    events = [
        (piece, way, step) for step in range(1, half + 1) for piece, way in chains if step <= hops[piece][way]
    ]

    def place_of(piece, way, step):
        q = hops[piece][way] - step + 1
        return q if way == 0 else -q

    order = list(dict.fromkeys([(place_of(*event) % half, event[0]) for event in events] + [(0, p) for p in range(pieces)]))
    made = {}

    def make(after):
        if len(made) < len(order):
            k, piece = order[len(made)]
            mine, outgoing = project(info, k, pieces, piece, both, out_weight, piece_width, after)
            made[k, piece] = (mine, lax.ppermute(outgoing, "tokens", swap))

    def block(q, piece):
        mine, swapped = made[q % half, piece]
        near = is_near(info, q % half) if q == q % half else jnp.logical_not(is_near(info, q % half))
        return jnp.where(near, mine, swapped).astype(F32)

    arrived, landed = {}, []
    make(())
    make(())
    for piece, way, step in events:
        value = block(place_of(piece, way, step), piece)
        if step > 1:
            value = value + arrived[piece, way].astype(F32)
        value = value.astype(BF16)
        arrived[piece, way] = lax.ppermute(value, "tensor", up if way == 0 else down)
        landed.append(arrived[piece, way])
        make((value, *landed[-3:-2]))

    resid, scaled = [], []
    squares = jnp.zeros((rows,), F32)
    for piece in range(pieces):
        mixed = columns_of(residual, piece).astype(F32) + block(0, piece)
        for way in range(2):
            if hops[piece][way]:
                mixed = mixed + arrived[piece, way].astype(F32)
        resid.append(mixed.astype(BF16))
        gain = norm_gain[piece * piece_width : (piece + 1) * piece_width].astype(F32)
        scaled.append((mixed * gain).astype(BF16))
        squares = squares + jnp.sum(mixed * mixed, axis=1)
    resid_out = jnp.concatenate(resid, axis=1)

    held = {(piece, 0): scaled[piece] for piece in range(pieces)}
    for step in range(1, half + 1):
        for piece in range(pieces):
            for way, pairs in ((0, up), (1, down)):
                if step > hops[piece][way]:
                    continue
                sign = -1 if way == 0 else 1
                source = (piece, sign * (step - 1))
                target = sign * step
                value = lax.ppermute(held[source], "tensor", pairs)
                held[piece, target] = value
                if abs(target) == half:
                    held[piece, half] = held[piece, -half] = value
    squares = squares[None]
    reach = half
    acc = None
    when = sorted(range(half), key=lambda k: max(k, half - k))
    indices = [info, info]
    for count, k in enumerate(when):
        one = [held[piece, k] for piece in range(pieces)]
        other = [held[piece, k - half] for piece in range(pieces)]
        near = is_near(indices[-2] if count > 1 else indices[-1], k)
        far = [lax.ppermute(jnp.where(near, other[piece], one[piece]), "tokens", swap) for piece in range(pieces)]
        sums = [squares]
        if reach >= 1 and count != half - 2:
            sums.append(lax.ppermute(squares, "tensor", [(ring[p], ring[(p + reach) % n]) for p in range(n)]))
            reach //= 2
        *acc, index, squares = query_block(
            info, k, half, one, other, far, next_weight, acc, k == when[-1], sums
        )
        indices.append(index)
    while reach >= 1:
        squares = squares + lax.ppermute(squares, "tensor", [(ring[p], ring[(p + reach) % n]) for p in range(n)])
        reach //= 2
    squares = squares[0]
    query_sum = acc[0] + lax.ppermute(acc[1], "tokens", swap).astype(F32)
    factor = 1.0 / jnp.sqrt(squares / D + EPS_NORM)
    return (resid_out, (query_sum * factor[:, None]).astype(BF16))


def on_mesh(n, att_queries, att_keys, att_values, out_weight, residual, norm_gain, next_weight):
    rows, width = att_queries.shape
    swap = [(0, 1), (1, 0)]
    chip = lax.axis_index("tensor")
    core = lax.axis_index("tokens")
    kv_head = chip * (width // HD) // (H // KVH)
    own_keys = lax.dynamic_index_in_dim(att_keys, kv_head, 1, keepdims=False)
    own_values = lax.dynamic_index_in_dim(att_values, kv_head, 1, keepdims=False)
    peer_keys = lax.ppermute(own_keys, "tokens", swap)
    peer_values = lax.ppermute(own_values, "tokens", swap)
    attended = attention(core[None], (att_queries, 0, 1), own_keys, own_values, peer_keys, peer_values)
    both = lax.all_gather(attended, "tokens", axis=0, tiled=True)
    partial = dot(both, out_weight).astype(BF16)
    partial = lax.all_to_all(partial, "tokens", split_axis=0, concat_axis=1, tiled=True)
    attn_out = lax.psum_scatter(partial.astype(F32), "tensor", scatter_dimension=1, tiled=True)
    mixed = residual.astype(F32) + attn_out
    total_squares = lax.psum(jnp.sum(mixed * mixed, axis=1), "tensor")
    factor = 1.0 / jnp.sqrt(total_squares / D + EPS_NORM)
    normed = (mixed * factor[:, None] * norm_gain.astype(F32)).astype(BF16)
    gathered = lax.all_gather(normed, "tensor", axis=1, tiled=True)
    halves = lax.all_to_all(gathered, "tokens", split_axis=1, concat_axis=0, tiled=True)
    query_sum = lax.psum_scatter(dot(halves, next_weight), "tokens", scatter_dimension=0, tiled=True)
    return (mixed.astype(BF16), query_sum.astype(BF16))


def solution(mesh):
    n = mesh.shape["tensor"]
    in_specs = (
        P(("groups", "tokens"), "tensor"),
        P(("groups", "tokens"), None, None),
        P(("groups", "tokens"), None, None),
        P("tensor", "tokens"),
        P(("groups", "tokens"), "tensor"),
        P("tensor"),
        P("tokens", "tensor"),
    )
    out_specs = (P(("groups", "tokens"), "tensor"), P(("groups", "tokens"), "tensor"))
    body = functools.partial(on_ring if n <= RING_LIMIT else on_mesh, n)
    return jax.shard_map(body, mesh=mesh, in_specs=in_specs, out_specs=out_specs, check_vma=False)
```

```python
import functools
import math

import jax
import jax.numpy as jnp
import numpy as np
from jax import lax
from jax.experimental import pallas as pl
from jax.experimental.pallas import tpu as pltpu
from jax.sharding import PartitionSpec as P

D = 16384
H = 128
KVH = 8
HD = 128
EPS_NORM = 1e-05
BF16 = jnp.bfloat16
F32 = jnp.float32
RING_LIMIT = 16
MIB = 1024 * 1024


def dot(a, b):
    return jnp.dot(a, b, preferred_element_type=F32)


def attention_kernel(heads, core_ref, q_ref, own_ref, far_ref, *refs):
    o_ref = refs[-1]
    k_ref, v_ref, pk_ref, pv_ref = own_ref.at[0], own_ref.at[1], far_ref.at[0], far_ref.at[1]
    rows = q_ref.shape[0]
    inv_root = 1.0 / math.sqrt(HD)
    query_pos = lax.broadcasted_iota(jnp.int32, (rows, rows), 0)
    key_pos = lax.broadcasted_iota(jnp.int32, (rows, rows), 1)
    visible = key_pos <= query_pos
    peer_visible = core_ref[0] == 1
    contract = (((1,), (1,)), ((), ()))
    for head in range(heads):
        columns = slice(head * HD, (head + 1) * HD)
        query = q_ref[:, columns]
        own = lax.dot_general(query, k_ref[...], contract, preferred_element_type=F32) * inv_root
        far = lax.dot_general(query, pk_ref[...], contract, preferred_element_type=F32) * inv_root
        own = jnp.where(visible, own, -1e30)
        far = jnp.where(peer_visible, far, -1e30)
        top = jnp.maximum(jnp.max(own, axis=1, keepdims=True), jnp.max(far, axis=1, keepdims=True))
        own = jnp.exp(own - top)
        far = jnp.exp(far - top)
        total = jnp.sum(own, axis=1, keepdims=True) + jnp.sum(far, axis=1, keepdims=True)
        mixed = dot(own.astype(BF16), v_ref[...]) + dot(far.astype(BF16), pv_ref[...])
        o_ref[:, columns] = (mixed / total).astype(BF16)


def attention(core, queries, own, far, after=()):
    queries, index, count = queries
    rows, width = queries.shape
    width = width // count
    heads = min(4, width // HD)
    first = index * width // (heads * HD)
    whole = pl.BlockSpec(memory_space=pltpu.VMEM)
    wanted = pl.BlockSpec((rows, heads * HD), lambda h, s: (0, first + h))
    part = pl.BlockSpec((rows, heads * HD), lambda h, s: (0, h))
    return pl.pallas_call(
        functools.partial(attention_kernel, heads),
        grid_spec=pltpu.PrefetchScalarGridSpec(
            num_scalar_prefetch=1,
            grid=(width // (heads * HD),),
            in_specs=[wanted, whole, whole] + [pl.BlockSpec(memory_space=pl.ANY)] * len(after),
            out_specs=part,
        ),
        out_shape=jax.ShapeDtypeStruct((rows, width), BF16),
        compiler_params=pltpu.CompilerParams(vmem_limit_bytes=24 * MIB),
        cost_estimate=pl.CostEstimate(
            flops=8 * rows * rows * width, bytes_accessed=4 * rows * width, transcendentals=2 * rows * rows * width // HD
        ),
        name="attention",
    )(core, queries, own, far, *after)


def project_kernel(info_ref, x_ref, w_ref, *refs):
    own_ref, peer_ref = refs[-2:]
    rows = own_ref.shape[0]
    result = dot(x_ref[...], w_ref[...]).astype(BF16)
    own_ref[...] = result[:rows]
    peer_ref[...] = result[rows:]


def project(info, pair, pieces, piece, both, weight, width, after):
    rows, depth = both.shape
    rows = rows // 2
    tile = min(256, width)
    tiles = width // tile
    out = pl.BlockSpec((rows, tile), lambda j, s: (0, j))
    return pl.pallas_call(
        project_kernel,
        grid_spec=pltpu.PrefetchScalarGridSpec(
            num_scalar_prefetch=1,
            grid=(tiles,),
            in_specs=[
                pl.BlockSpec(memory_space=pltpu.VMEM),
                pl.BlockSpec((depth, tile), lambda j, s: (0, (s[pair] * pieces + piece) * tiles + j)),
            ]
            + [pl.BlockSpec(memory_space=pl.ANY)] * len(after),
            out_specs=[out, out],
        ),
        out_shape=[jax.ShapeDtypeStruct((rows, width), BF16)] * 2,
        compiler_params=pltpu.CompilerParams(vmem_limit_bytes=34 * MIB),
        cost_estimate=pl.CostEstimate(
            flops=4 * rows * depth * width, bytes_accessed=2 * depth * width, transcendentals=0
        ),
        name="project",
    )(info, both, weight, *after)


def query_kernel(sizes, code, first, info_ref, *refs):
    chosen, far = refs[: sizes[0]], refs[sizes[0] : sum(sizes)]
    w_ref = refs[sum(sizes)]
    own_ref, peer_ref, x_ref = refs[-3:]
    rows = own_ref.shape[0]

    @pl.when(pl.program_id(0) == 0)
    def _():
        for blocks, place in ((chosen, slice(0, rows)), (far, slice(rows, 2 * rows))):
            for choice, block in enumerate(blocks):

                @pl.when(info_ref[code] == choice if len(blocks) > 1 else True)
                def _():
                    x_ref[place] = block[...]

    for part, (place, out) in enumerate(((slice(0, rows), own_ref), (slice(rows, 2 * rows), peer_ref))):
        result = dot(x_ref[place], w_ref[...])
        if not first:
            result = result + refs[sum(sizes) + 1 + part][...]
        out[...] = result.astype(out.dtype)


def query_block(info, pair, code, chosen, far, weight, acc, last):
    rows, depth = far[0].shape
    width = weight.shape[1]
    tile = min(512, width)
    whole = pl.BlockSpec(memory_space=pltpu.VMEM)
    out = pl.BlockSpec((rows, tile), lambda j, s: (0, j))
    return pl.pallas_call(
        functools.partial(query_kernel, (len(chosen), len(far)), code, not acc),
        grid_spec=pltpu.PrefetchScalarGridSpec(
            num_scalar_prefetch=1,
            grid=(width // tile,),
            in_specs=[whole] * (len(chosen) + len(far))
            + [pl.BlockSpec((depth, tile), lambda j, s: (s[pair], j))]
            + [out] * len(acc),
            out_specs=[out, out],
            scratch_shapes=[pltpu.VMEM((2 * rows, depth), BF16)],
        ),
        out_shape=[
            jax.ShapeDtypeStruct((rows, width), F32),
            jax.ShapeDtypeStruct((rows, width), BF16 if last else F32),
        ],
        compiler_params=pltpu.CompilerParams(vmem_limit_bytes=34 * MIB),
        cost_estimate=pl.CostEstimate(
            flops=4 * rows * depth * width, bytes_accessed=2 * depth * width + 16 * rows * width, transcendentals=0
        ),
        name="next_query",
    )(info, *chosen, *far, weight, *acc)


def add_kernel(total_ref, more_ref, *refs):
    refs[-1][...] = total_ref[...] + more_ref[...]


def add_in_step(total, more, blocks):
    whole = pl.BlockSpec(memory_space=pltpu.VMEM)
    free = pl.BlockSpec(memory_space=pl.ANY)
    *blocks, total = pl.pallas_call(
        add_kernel,
        in_specs=[whole, whole] + [free] * len(blocks),
        out_specs=[free] * len(blocks) + [whole],
        out_shape=[jax.ShapeDtypeStruct(block.shape, block.dtype) for block in (*blocks, total)],
        input_output_aliases={2 + index: index for index in range(len(blocks))},
        name="add_squares",
    )(total, more, *blocks)
    return total, blocks


def pick_kernel(codes, sizes, info_ref, *refs):
    outs = refs[len(refs) - len(codes) :]
    start = 0
    for code, size, out in zip(codes, sizes, outs):
        for choice in range(size):

            @pl.when(info_ref[code] == choice)
            def _():
                out[...] = refs[start + choice][...]

        start += size


def pick(info, codes, groups, after):
    whole = pl.BlockSpec(memory_space=pltpu.VMEM)
    first = groups[0][0]
    return pl.pallas_call(
        functools.partial(pick_kernel, codes, [len(group) for group in groups]),
        grid_spec=pltpu.PrefetchScalarGridSpec(
            num_scalar_prefetch=1,
            grid=(1,),
            in_specs=[whole] * sum(len(group) for group in groups) + [pl.BlockSpec(memory_space=pl.ANY)] * len(after),
            out_specs=[whole] * len(groups),
        ),
        out_shape=[jax.ShapeDtypeStruct(first.shape, first.dtype)] * len(groups),
        name="pick",
    )(info, *[block for group in groups for block in group], *after)


def ring_of(n):
    return [2 * p for p in range(n // 2)] + [2 * p + 1 for p in reversed(range(n // 2))]


def tables(n):
    half = n // 2
    ring = ring_of(n)
    place = {chip: p for p, chip in enumerate(ring)}
    table = np.zeros((n, 2, 2 * half + n), np.int32)
    for chip in range(n):
        for core in range(2):

            def is_mine(q):
                return ring[(place[chip] + q) % n] // half == core

            for k in range(half):
                near = is_mine(k)
                assert near != is_mine(k - half)
                table[chip, core, k] = ring[(place[chip] + (k if near else k - half)) % n] - core * half
                q = (k if near else k - half) * (1 if core == 0 else -1)
                if k > 0:
                    table[chip, core, half + k] = block_choices(k, half).index(q)
                else:
                    table[chip, core, half] = 0 if near else 1 + core
            for q in range(1 - half, half + 1):
                real = q if core == 0 else -q
                pair = (real % half, 0 if is_mine(real) else 1)
                table[chip, core, 2 * half + q + half - 1] = sum_choices(q, half).index(pair)
    return table.reshape(2 * n, -1)


def block_choices(k, half):
    return list(dict.fromkeys([k, k - half, -k, half - k]))


def sum_choices(q, half):
    return [(k, kind) for k in dict.fromkeys([q % half, -q % half]) for kind in (0, 1)]


def choose(code, arrays):
    result = arrays[-1]
    for index in reversed(range(len(arrays) - 1)):
        result = jnp.where(code == index, arrays[index], result)
    return result


def on_ring(n, att_queries, att_keys, att_values, out_weight, residual, norm_gain, next_weight):
    half = n // 2
    ring = ring_of(n)
    up = [(ring[p], ring[(p + 1) % n]) for p in range(n)]
    swap = [(0, 1), (1, 0)]
    long_way = [(2 * a, 2 * b) for a, b in up] + [(2 * b + 1, 2 * a + 1) for a, b in up]
    short_way = [(2 * b, 2 * a) for a, b in up] + [(2 * a + 1, 2 * b + 1) for a, b in up]
    devices = ("tensor", "tokens")
    chip = lax.axis_index("tensor")
    core = lax.axis_index("tokens")
    rows, width = att_queries.shape
    info = lax.dynamic_index_in_dim(jnp.asarray(tables(n)), chip * 2 + core, 0, keepdims=False)

    heads_here = width // HD
    kv_head = chip * heads_here // (H // KVH)
    own = jnp.stack([lax.dynamic_index_in_dim(array, kv_head, 1, keepdims=False) for array in (att_keys, att_values)])
    far = lax.ppermute(own, "tokens", swap)
    attended, attended_peer = [], []
    for part in range(2):
        queries = (att_queries, part, 2)
        attended.append(attention(core[None], queries, own, far, attended))
        attended_peer.append(lax.ppermute(attended[-1], "tokens", swap))
    both = jnp.concatenate(
        [jnp.concatenate(attended, axis=1), jnp.concatenate(attended_peer, axis=1)], axis=0
    )

    made = {}

    def make(k, after=()):
        made[k, 0], outgoing = project(info, k, 1, 0, both, out_weight, residual.shape[1], after)
        made[k, 1] = lax.ppermute(outgoing, "tokens", swap)

    def partial_sum(q):
        return choose(info[2 * half + q + half - 1], [made[key] for key in sum_choices(q, half)]).astype(F32)

    arrived = {}

    def send(way, step):
        q = half - step + 1 if way == "long" else step - half
        value = partial_sum(q)
        if step > 1:
            value = value + arrived[way].astype(F32)
        value = value.astype(BF16)
        arrived[way] = lax.ppermute(value, devices, long_way if way == "long" else short_way)
        return value

    def need(q, after):
        for k in dict.fromkeys([q % half, -q % half]):
            if (k, 0) not in made:
                make(k, after)

    make(0)
    make(1)
    recent = [send("long", 1)]
    for step in range(1, half):
        need(step - half, recent)
        need(half - step, recent)
        recent = [send("short", step), send("long", step + 1)]

    mixed = residual.astype(F32) + partial_sum(0) + arrived["long"].astype(F32) + arrived["short"].astype(F32)
    resid_out = mixed.astype(BF16)
    scaled = (mixed * norm_gain.astype(F32)).astype(BF16)
    squares = jnp.sum(mixed * mixed, axis=1)[None]

    held = {0: scaled}
    long_block, short_block = scaled, scaled
    reach = half
    for step in range(1, half):
        long_block = lax.ppermute(long_block, devices, long_way)
        short_block = lax.ppermute(short_block, devices, short_way)
        if reach >= 1:
            more = lax.ppermute(squares, "tensor", [(ring[p], ring[(p + reach) % n]) for p in range(n)])
            squares, (long_block, short_block) = add_in_step(squares, more, [long_block, short_block])
            reach //= 2
        held[-step], held[step] = long_block, short_block
    while reach >= 1:
        squares = squares + lax.ppermute(squares, "tensor", [(ring[p], ring[(p + reach) % n]) for p in range(n)])
        reach //= 2
    meets = {b: ring[(p + half) % n] // half for p, b in enumerate(ring)}
    last_hop = [
        lax.ppermute(held[1 - half], devices, [(2 * a, 2 * b + meets[b]) for a, b in up]),
        lax.ppermute(held[1 - half], devices, [(2 * b + 1, 2 * a + meets[a]) for a, b in up]),
    ]
    scaled_peer = lax.ppermute(scaled, "tokens", swap)

    acc, after = (), ()
    groups = {}
    for k in range(1, half):
        groups.setdefault(max(k, half - k), []).append(k)
    for reached in sorted(groups):
        pairs = groups[reached]
        wanted = {k: [held[q] for q in block_choices(k, half)] for k in pairs}
        others = [[wanted[k][index ^ 1] for index in range(len(wanted[k]))] for k in pairs]
        outgoing = pick(info, [half + k for k in pairs], others, after)
        far = [lax.ppermute(block, "tokens", swap) for block in outgoing]
        for k, block in zip(pairs, far):
            acc = query_block(info, k, half + k, wanted[k], [block], next_weight, acc, False)
            after = acc[:1]
    acc = query_block(
        info, 0, half, [scaled, *last_hop], [scaled_peer, *reversed(last_hop)], next_weight, acc, True
    )
    query_sum = acc[0] + lax.ppermute(acc[1], "tokens", swap).astype(F32)
    factor = 1.0 / jnp.sqrt(squares[0] / D + EPS_NORM)
    return (resid_out, (query_sum * factor[:, None]).astype(BF16))


def on_mesh(n, att_queries, att_keys, att_values, out_weight, residual, norm_gain, next_weight):
    rows, width = att_queries.shape
    swap = [(0, 1), (1, 0)]
    chip = lax.axis_index("tensor")
    core = lax.axis_index("tokens")
    kv_head = chip * (width // HD) // (H // KVH)
    own = jnp.stack([lax.dynamic_index_in_dim(array, kv_head, 1, keepdims=False) for array in (att_keys, att_values)])
    far = lax.ppermute(own, "tokens", swap)
    attended = attention(core[None], (att_queries, 0, 1), own, far)
    both = lax.all_gather(attended, "tokens", axis=0, tiled=True)
    partial = dot(both, out_weight).astype(BF16)
    partial = lax.all_to_all(partial, "tokens", split_axis=0, concat_axis=1, tiled=True)
    attn_out = lax.psum_scatter(partial.astype(F32), "tensor", scatter_dimension=1, tiled=True)
    mixed = residual.astype(F32) + attn_out
    total_squares = lax.psum(jnp.sum(mixed * mixed, axis=1), "tensor")
    factor = 1.0 / jnp.sqrt(total_squares / D + EPS_NORM)
    normed = (mixed * factor[:, None] * norm_gain.astype(F32)).astype(BF16)
    gathered = lax.all_gather(normed, "tensor", axis=1, tiled=True)
    halves = lax.all_to_all(gathered, "tokens", split_axis=1, concat_axis=0, tiled=True)
    query_sum = lax.psum_scatter(dot(halves, next_weight), "tokens", scatter_dimension=0, tiled=True)
    return (mixed.astype(BF16), query_sum.astype(BF16))


def solution(mesh):
    n = mesh.shape["tensor"]
    in_specs = (
        P(("groups", "tokens"), "tensor"),
        P(("groups", "tokens"), None, None),
        P(("groups", "tokens"), None, None),
        P("tensor", "tokens"),
        P(("groups", "tokens"), "tensor"),
        P("tensor"),
        P("tokens", "tensor"),
    )
    out_specs = (P(("groups", "tokens"), "tensor"), P(("groups", "tokens"), "tensor"))
    body = functools.partial(on_ring if n <= RING_LIMIT else on_mesh, n)
    return jax.shard_map(body, mesh=mesh, in_specs=in_specs, out_specs=out_specs, check_vma=False)
```

```python
import functools
import math

import jax
import jax.numpy as jnp
import numpy as np
from jax import lax
from jax.experimental import pallas as pl
from jax.experimental.pallas import tpu as pltpu
from jax.sharding import PartitionSpec as P

D = 16384
H = 128
KVH = 8
HD = 128
EPS_NORM = 1e-05
BF16 = jnp.bfloat16
F32 = jnp.float32
RING_LIMIT = 16
MIB = 1024 * 1024


def dot(a, b):
    return jnp.dot(a, b, preferred_element_type=F32)


def attention_kernel(heads, core_ref, q_ref, own_ref, far_ref, *refs):
    o_ref = refs[-1]
    k_ref, v_ref, pk_ref, pv_ref = own_ref.at[0], own_ref.at[1], far_ref.at[0], far_ref.at[1]
    rows = q_ref.shape[0]
    inv_root = 1.0 / math.sqrt(HD)
    query_pos = lax.broadcasted_iota(jnp.int32, (rows, rows), 0)
    key_pos = lax.broadcasted_iota(jnp.int32, (rows, rows), 1)
    visible = key_pos <= query_pos
    peer_visible = core_ref[0] == 1
    contract = (((1,), (1,)), ((), ()))
    for head in range(heads):
        columns = slice(head * HD, (head + 1) * HD)
        query = q_ref[:, columns]
        own = lax.dot_general(query, k_ref[...], contract, preferred_element_type=F32) * inv_root
        far = lax.dot_general(query, pk_ref[...], contract, preferred_element_type=F32) * inv_root
        own = jnp.where(visible, own, -1e30)
        far = jnp.where(peer_visible, far, -1e30)
        top = jnp.maximum(jnp.max(own, axis=1, keepdims=True), jnp.max(far, axis=1, keepdims=True))
        own = jnp.exp(own - top)
        far = jnp.exp(far - top)
        total = jnp.sum(own, axis=1, keepdims=True) + jnp.sum(far, axis=1, keepdims=True)
        mixed = dot(own.astype(BF16), v_ref[...]) + dot(far.astype(BF16), pv_ref[...])
        o_ref[:, columns] = (mixed / total).astype(BF16)


def attention(core, queries, own, far, after=()):
    queries, index, count = queries
    rows, width = queries.shape
    width = width // count
    heads = min(4, width // HD)
    first = index * width // (heads * HD)
    whole = pl.BlockSpec(memory_space=pltpu.VMEM)
    wanted = pl.BlockSpec((rows, heads * HD), lambda h, s: (0, first + h))
    part = pl.BlockSpec((rows, heads * HD), lambda h, s: (0, h))
    return pl.pallas_call(
        functools.partial(attention_kernel, heads),
        grid_spec=pltpu.PrefetchScalarGridSpec(
            num_scalar_prefetch=1,
            grid=(width // (heads * HD),),
            in_specs=[wanted, whole, whole] + [pl.BlockSpec(memory_space=pl.ANY)] * len(after),
            out_specs=part,
        ),
        out_shape=jax.ShapeDtypeStruct((rows, width), BF16),
        compiler_params=pltpu.CompilerParams(vmem_limit_bytes=24 * MIB),
        cost_estimate=pl.CostEstimate(
            flops=8 * rows * rows * width, bytes_accessed=4 * rows * width, transcendentals=2 * rows * rows * width // HD
        ),
        name="attention",
    )(core, queries, own, far, *after)


def project_kernel(info_ref, x_ref, w_ref, *refs):
    own_ref, peer_ref = refs[-2:]
    rows = own_ref.shape[0]
    result = dot(x_ref[...], w_ref[...]).astype(BF16)
    own_ref[...] = result[:rows]
    peer_ref[...] = result[rows:]


def project(info, pair, pieces, piece, both, weight, width, after):
    rows, depth = both.shape
    rows = rows // 2
    tile = min(512, width)
    tiles = width // tile
    out = pl.BlockSpec((rows, tile), lambda j, s: (0, j))
    return pl.pallas_call(
        project_kernel,
        grid_spec=pltpu.PrefetchScalarGridSpec(
            num_scalar_prefetch=1,
            grid=(tiles,),
            in_specs=[
                pl.BlockSpec(memory_space=pltpu.VMEM),
                pl.BlockSpec((depth, tile), lambda j, s: (0, (s[pair] * pieces + piece) * tiles + j)),
            ]
            + [pl.BlockSpec(memory_space=pltpu.VMEM)] * len(after),
            out_specs=[out, out],
        ),
        out_shape=[jax.ShapeDtypeStruct((rows, width), BF16)] * 2,
        compiler_params=pltpu.CompilerParams(vmem_limit_bytes=34 * MIB),
        cost_estimate=pl.CostEstimate(
            flops=4 * rows * depth * width, bytes_accessed=2 * depth * width, transcendentals=0
        ),
        name="project",
    )(info, both, weight, *after)


def query_kernel(sizes, code, first, info_ref, *refs):
    chosen, far = refs[: sizes[0]], refs[sizes[0] : sum(sizes)]
    w_ref = refs[sum(sizes)]
    own_ref, peer_ref, x_ref = refs[-3:]
    rows = own_ref.shape[0]

    @pl.when(pl.program_id(0) == 0)
    def _():
        for blocks, place in ((chosen, slice(0, rows)), (far, slice(rows, 2 * rows))):
            for choice, block in enumerate(blocks):

                @pl.when(info_ref[code] == choice if len(blocks) > 1 else True)
                def _():
                    x_ref[place] = block[...]

    for part, (place, out) in enumerate(((slice(0, rows), own_ref), (slice(rows, 2 * rows), peer_ref))):
        result = dot(x_ref[place], w_ref[...])
        if not first:
            result = result + refs[sum(sizes) + 1 + part][...]
        out[...] = result.astype(out.dtype)


def query_block(info, pair, code, chosen, far, weight, acc, last):
    rows, depth = far[0].shape
    width = weight.shape[1]
    tile = min(512, width)
    whole = pl.BlockSpec(memory_space=pltpu.VMEM)
    out = pl.BlockSpec((rows, tile), lambda j, s: (0, j))
    return pl.pallas_call(
        functools.partial(query_kernel, (len(chosen), len(far)), code, not acc),
        grid_spec=pltpu.PrefetchScalarGridSpec(
            num_scalar_prefetch=1,
            grid=(width // tile,),
            in_specs=[whole] * (len(chosen) + len(far))
            + [pl.BlockSpec((depth, tile), lambda j, s: (s[pair], j))]
            + [out] * len(acc),
            out_specs=[out, out],
            scratch_shapes=[pltpu.VMEM((2 * rows, depth), BF16)],
        ),
        out_shape=[
            jax.ShapeDtypeStruct((rows, width), F32),
            jax.ShapeDtypeStruct((rows, width), BF16 if last else F32),
        ],
        compiler_params=pltpu.CompilerParams(vmem_limit_bytes=24 * MIB),
        cost_estimate=pl.CostEstimate(
            flops=4 * rows * depth * width, bytes_accessed=2 * depth * width + 16 * rows * width, transcendentals=0
        ),
        name="next_query",
    )(info, *chosen, *far, weight, *acc)


def add_kernel(total_ref, more_ref, *refs):
    refs[-1][...] = total_ref[...] + more_ref[...]


def add_in_step(total, more, blocks, after):
    whole = pl.BlockSpec(memory_space=pltpu.VMEM)
    *blocks, total = pl.pallas_call(
        add_kernel,
        in_specs=[whole] * (2 + len(blocks) + len(after)),
        out_specs=[whole] * (len(blocks) + 1),
        out_shape=[jax.ShapeDtypeStruct(block.shape, block.dtype) for block in (*blocks, total)],
        input_output_aliases={2 + index: index for index in range(len(blocks))},
        compiler_params=pltpu.CompilerParams(vmem_limit_bytes=4 * MIB),
        name="add_squares",
    )(total, more, *blocks, *after)
    return total, blocks


def pick_kernel(codes, sizes, info_ref, *refs):
    outs = refs[len(refs) - len(codes) :]
    start = 0
    for code, size, out in zip(codes, sizes, outs):
        for choice in range(size):

            @pl.when(info_ref[code] == choice)
            def _():
                out[...] = refs[start + choice][...]

        start += size


def pick(info, codes, groups, after):
    whole = pl.BlockSpec(memory_space=pltpu.VMEM)
    first = groups[0][0]
    return pl.pallas_call(
        functools.partial(pick_kernel, codes, [len(group) for group in groups]),
        grid_spec=pltpu.PrefetchScalarGridSpec(
            num_scalar_prefetch=1,
            grid=(1,),
            in_specs=[whole] * (sum(len(group) for group in groups) + len(after)),
            out_specs=[whole] * len(groups),
        ),
        out_shape=[jax.ShapeDtypeStruct(first.shape, first.dtype)] * len(groups),
        compiler_params=pltpu.CompilerParams(vmem_limit_bytes=4 * MIB),
        name="pick",
    )(info, *[block for group in groups for block in group], *after)


def ring_of(n):
    return [2 * p for p in range(n // 2)] + [2 * p + 1 for p in reversed(range(n // 2))]


def tables(n):
    half = n // 2
    ring = ring_of(n)
    place = {chip: p for p, chip in enumerate(ring)}
    table = np.zeros((n, 2, 2 * half + n), np.int32)
    for chip in range(n):
        for core in range(2):

            def is_mine(q):
                return ring[(place[chip] + q) % n] // half == core

            for k in range(half):
                near = is_mine(k)
                assert near != is_mine(k - half)
                table[chip, core, k] = ring[(place[chip] + (k if near else k - half)) % n] - core * half
                q = (k if near else k - half) * (1 if core == 0 else -1)
                if k > 0:
                    table[chip, core, half + k] = block_choices(k, half).index(q)
                else:
                    table[chip, core, half] = 0 if near else 1 + core
            for q in range(1 - half, half + 1):
                real = q if core == 0 else -q
                pair = (real % half, 0 if is_mine(real) else 1)
                table[chip, core, 2 * half + q + half - 1] = sum_choices(q, half).index(pair)
    return table.reshape(2 * n, -1)


def block_choices(k, half):
    return list(dict.fromkeys([k, k - half, -k, half - k]))


def sum_choices(q, half):
    return [(k, kind) for k in dict.fromkeys([q % half, -q % half]) for kind in (0, 1)]


def choose(code, arrays):
    result = arrays[-1]
    for index in reversed(range(len(arrays) - 1)):
        result = jnp.where(code == index, arrays[index], result)
    return result


def on_ring(n, att_queries, att_keys, att_values, out_weight, residual, norm_gain, next_weight):
    half = n // 2
    ring = ring_of(n)
    up = [(ring[p], ring[(p + 1) % n]) for p in range(n)]
    swap = [(0, 1), (1, 0)]
    long_way = [(2 * a, 2 * b) for a, b in up] + [(2 * b + 1, 2 * a + 1) for a, b in up]
    short_way = [(2 * b, 2 * a) for a, b in up] + [(2 * a + 1, 2 * b + 1) for a, b in up]
    devices = ("tensor", "tokens")
    chip = lax.axis_index("tensor")
    core = lax.axis_index("tokens")
    rows, width = att_queries.shape
    info = lax.dynamic_index_in_dim(jnp.asarray(tables(n)), chip * 2 + core, 0, keepdims=False)

    heads_here = width // HD
    kv_head = chip * heads_here // (H // KVH)
    own = jnp.stack([lax.dynamic_index_in_dim(array, kv_head, 1, keepdims=False) for array in (att_keys, att_values)])
    far = lax.ppermute(own, "tokens", swap)
    attended, attended_peer = [], []
    for part in range(2):
        queries = (att_queries, part, 2)
        attended.append(attention(core[None], queries, own, far, attended))
        attended_peer.append(lax.ppermute(attended[-1], "tokens", swap))
    both = jnp.concatenate(
        [jnp.concatenate(attended, axis=1), jnp.concatenate(attended_peer, axis=1)], axis=0
    )

    made = {}

    def make(k, after=()):
        made[k, 0], outgoing = project(info, k, 1, 0, both, out_weight, residual.shape[1], after)
        made[k, 1] = lax.ppermute(outgoing, "tokens", swap)

    def partial_sum(q):
        return choose(info[2 * half + q + half - 1], [made[key] for key in sum_choices(q, half)]).astype(F32)

    arrived = {}

    def send(way, step, previous):
        q = half - step + 1 if way == "long" else step - half
        value = partial_sum(q)
        if step > 1:
            value = value + lax.optimization_barrier((arrived[way], previous))[0].astype(F32)
        value = value.astype(BF16)
        arrived[way] = lax.ppermute(value, devices, long_way if way == "long" else short_way)
        return value

    make(0)
    for k in range(1, half):
        if k != half - k:
            make(k)
    value = send("long", 1, None)
    if half % 2 == 0:
        make(half // 2, [value])
    for step in range(1, half):
        value = send("short", step, value)
        value = send("long", step + 1, value)

    mixed = residual.astype(F32) + partial_sum(0) + arrived["long"].astype(F32) + arrived["short"].astype(F32)
    resid_out = mixed.astype(BF16)
    scaled = (mixed * norm_gain.astype(F32)).astype(BF16)
    squares = jnp.sum(mixed * mixed, axis=1)[None]

    held = {0: scaled}
    long_block, short_block = scaled, scaled
    scaled_peer = lax.ppermute(scaled, "tokens", swap)
    groups = {}
    for k in range(1, half):
        groups.setdefault(max(k, half - k), []).append(k)
    reach = 1
    acc, after = (), ()
    for step in range(1, half):
        long_block = lax.ppermute(long_block, devices, long_way)
        short_block = lax.ppermute(short_block, devices, short_way)
        if reach < n:
            more = lax.ppermute(squares, "tensor", [(c, c ^ reach) for c in range(n)])
            squares, (long_block,) = add_in_step(squares, more, [long_block], after)
            reach *= 2
        held[-step], held[step] = long_block, short_block
        pairs = groups.get(step, [])
        if pairs:
            wanted = {k: [held[q] for q in block_choices(k, half)] for k in pairs}
            others = [[wanted[k][index ^ 1] for index in range(len(wanted[k]))] for k in pairs]
            outgoing = pick(info, [half + k for k in pairs], others, after)
            far = [lax.ppermute(block, "tokens", swap) for block in outgoing]
            for k, block in zip(pairs, far):
                acc = query_block(info, k, half + k, wanted[k], [block], next_weight, acc, False)
            after = acc[:1]
    while reach < n:
        squares = squares + lax.ppermute(squares, "tensor", [(c, c ^ reach) for c in range(n)])
        reach *= 2
    meets = {b: ring[(p + half) % n] // half for p, b in enumerate(ring)}
    last_hop = [
        lax.ppermute(held[1 - half], devices, [(2 * a, 2 * b + meets[b]) for a, b in up]),
        lax.ppermute(held[1 - half], devices, [(2 * b + 1, 2 * a + meets[a]) for a, b in up]),
    ]
    acc = query_block(
        info, 0, half, [scaled, *last_hop], [scaled_peer, *reversed(last_hop)], next_weight, acc, True
    )
    query_sum = acc[0] + lax.ppermute(acc[1], "tokens", swap).astype(F32)
    factor = 1.0 / jnp.sqrt(squares[0] / D + EPS_NORM)
    return (resid_out, (query_sum * factor[:, None]).astype(BF16))


def on_mesh(n, att_queries, att_keys, att_values, out_weight, residual, norm_gain, next_weight):
    rows, width = att_queries.shape
    swap = [(0, 1), (1, 0)]
    chip = lax.axis_index("tensor")
    core = lax.axis_index("tokens")
    kv_head = chip * (width // HD) // (H // KVH)
    own = jnp.stack([lax.dynamic_index_in_dim(array, kv_head, 1, keepdims=False) for array in (att_keys, att_values)])
    far = lax.ppermute(own, "tokens", swap)
    attended = attention(core[None], (att_queries, 0, 1), own, far)
    both = lax.all_gather(attended, "tokens", axis=0, tiled=True)
    partial = dot(both, out_weight).astype(BF16)
    partial = lax.all_to_all(partial, "tokens", split_axis=0, concat_axis=1, tiled=True)
    attn_out = lax.psum_scatter(partial.astype(F32), "tensor", scatter_dimension=1, tiled=True)
    mixed = residual.astype(F32) + attn_out
    total_squares = lax.psum(jnp.sum(mixed * mixed, axis=1), "tensor")
    factor = 1.0 / jnp.sqrt(total_squares / D + EPS_NORM)
    normed = (mixed * factor[:, None] * norm_gain.astype(F32)).astype(BF16)
    gathered = lax.all_gather(normed, "tensor", axis=1, tiled=True)
    halves = lax.all_to_all(gathered, "tokens", split_axis=1, concat_axis=0, tiled=True)
    query_sum = lax.psum_scatter(dot(halves, next_weight), "tokens", scatter_dimension=0, tiled=True)
    return (mixed.astype(BF16), query_sum.astype(BF16))


def solution(mesh):
    n = mesh.shape["tensor"]
    in_specs = (
        P(("groups", "tokens"), "tensor"),
        P(("groups", "tokens"), None, None),
        P(("groups", "tokens"), None, None),
        P("tensor", "tokens"),
        P(("groups", "tokens"), "tensor"),
        P("tensor"),
        P("tokens", "tensor"),
    )
    out_specs = (P(("groups", "tokens"), "tensor"), P(("groups", "tokens"), "tensor"))
    body = functools.partial(on_ring if n <= RING_LIMIT else on_mesh, n)
    return jax.shard_map(body, mesh=mesh, in_specs=in_specs, out_specs=out_specs, check_vma=False)
```

```python
import functools
import math

import jax
import jax.numpy as jnp
import numpy as np
from jax import lax
from jax.experimental import pallas as pl
from jax.experimental.pallas import tpu as pltpu
from jax.sharding import PartitionSpec as P

D = 16384
H = 128
KVH = 8
HD = 128
EPS_NORM = 1e-05
BF16 = jnp.bfloat16
F32 = jnp.float32
RING_LIMIT = 16
MIB = 1024 * 1024


def dot(a, b):
    return jnp.dot(a, b, preferred_element_type=F32)


def attention_kernel(heads, core_ref, q_ref, own_ref, far_ref, *refs):
    o_ref = refs[-1]
    k_ref, v_ref, pk_ref, pv_ref = own_ref.at[0], own_ref.at[1], far_ref.at[0], far_ref.at[1]
    rows = q_ref.shape[0]
    inv_root = 1.0 / math.sqrt(HD)
    query_pos = lax.broadcasted_iota(jnp.int32, (rows, rows), 0)
    key_pos = lax.broadcasted_iota(jnp.int32, (rows, rows), 1)
    visible = key_pos <= query_pos
    peer_visible = core_ref[0] == 1
    contract = (((1,), (1,)), ((), ()))
    for head in range(heads):
        columns = slice(head * HD, (head + 1) * HD)
        query = q_ref[:, columns]
        own = lax.dot_general(query, k_ref[...], contract, preferred_element_type=F32) * inv_root
        far = lax.dot_general(query, pk_ref[...], contract, preferred_element_type=F32) * inv_root
        own = jnp.where(visible, own, -1e30)
        far = jnp.where(peer_visible, far, -1e30)
        top = jnp.maximum(jnp.max(own, axis=1, keepdims=True), jnp.max(far, axis=1, keepdims=True))
        own = jnp.exp(own - top)
        far = jnp.exp(far - top)
        total = jnp.sum(own, axis=1, keepdims=True) + jnp.sum(far, axis=1, keepdims=True)
        mixed = dot(own.astype(BF16), v_ref[...]) + dot(far.astype(BF16), pv_ref[...])
        o_ref[:, columns] = (mixed / total).astype(BF16)


def attention(core, queries, own, far, after=()):
    queries, index, count = queries
    rows, width = queries.shape
    width = width // count
    heads = min(4, width // HD)
    first = index * width // (heads * HD)
    whole = pl.BlockSpec(memory_space=pltpu.VMEM)
    wanted = pl.BlockSpec((rows, heads * HD), lambda h, s: (0, first + h))
    part = pl.BlockSpec((rows, heads * HD), lambda h, s: (0, h))
    return pl.pallas_call(
        functools.partial(attention_kernel, heads),
        grid_spec=pltpu.PrefetchScalarGridSpec(
            num_scalar_prefetch=1,
            grid=(width // (heads * HD),),
            in_specs=[wanted, whole, whole] + [pl.BlockSpec(memory_space=pl.ANY)] * len(after),
            out_specs=part,
        ),
        out_shape=jax.ShapeDtypeStruct((rows, width), BF16),
        compiler_params=pltpu.CompilerParams(vmem_limit_bytes=24 * MIB),
        cost_estimate=pl.CostEstimate(
            flops=8 * rows * rows * width, bytes_accessed=4 * rows * width, transcendentals=2 * rows * rows * width // HD
        ),
        name="attention",
    )(core, queries, own, far, *after)


def project_kernel(info_ref, x_ref, w_ref, *refs):
    own_ref, peer_ref = refs[-2:]
    rows = own_ref.shape[0]
    result = dot(x_ref[...], w_ref[...]).astype(BF16)
    own_ref[...] = result[:rows]
    peer_ref[...] = result[rows:]


def project(info, pair, pieces, piece, both, weight, width, after):
    rows, depth = both.shape
    rows = rows // 2
    tile = min(512, width)
    tiles = width // tile
    out = pl.BlockSpec((rows, tile), lambda j, s: (0, j))
    return pl.pallas_call(
        project_kernel,
        grid_spec=pltpu.PrefetchScalarGridSpec(
            num_scalar_prefetch=1,
            grid=(tiles,),
            in_specs=[
                pl.BlockSpec(memory_space=pltpu.VMEM),
                pl.BlockSpec((depth, tile), lambda j, s: (0, (s[pair] * pieces + piece) * tiles + j)),
            ]
            + [pl.BlockSpec(memory_space=pltpu.VMEM)] * len(after),
            out_specs=[out, out],
        ),
        out_shape=[jax.ShapeDtypeStruct((rows, width), BF16)] * 2,
        compiler_params=pltpu.CompilerParams(vmem_limit_bytes=34 * MIB),
        cost_estimate=pl.CostEstimate(
            flops=4 * rows * depth * width, bytes_accessed=2 * depth * width, transcendentals=0
        ),
        name="project",
    )(info, both, weight, *after)


def query_kernel(sizes, code, first, info_ref, *refs):
    chosen, far = refs[: sizes[0]], refs[sizes[0] : sum(sizes)]
    w_ref = refs[sum(sizes)]
    own_ref, peer_ref, x_ref = refs[-3:]
    rows = own_ref.shape[0]

    @pl.when(pl.program_id(0) == 0)
    def _():
        for blocks, place in ((chosen, slice(0, rows)), (far, slice(rows, 2 * rows))):
            for choice, block in enumerate(blocks):

                @pl.when(info_ref[code] == choice if len(blocks) > 1 else True)
                def _():
                    x_ref[place] = block[...]

    for part, (place, out) in enumerate(((slice(0, rows), own_ref), (slice(rows, 2 * rows), peer_ref))):
        result = dot(x_ref[place], w_ref[...])
        if not first:
            result = result + refs[sum(sizes) + 1 + part][...]
        out[...] = result.astype(out.dtype)


def query_block(info, pair, code, chosen, far, weight, acc, last):
    rows, depth = far[0].shape
    width = weight.shape[1]
    tile = min(512, width)
    whole = pl.BlockSpec(memory_space=pltpu.VMEM)
    out = pl.BlockSpec((rows, tile), lambda j, s: (0, j))
    return pl.pallas_call(
        functools.partial(query_kernel, (len(chosen), len(far)), code, not acc),
        grid_spec=pltpu.PrefetchScalarGridSpec(
            num_scalar_prefetch=1,
            grid=(width // tile,),
            in_specs=[whole] * (len(chosen) + len(far))
            + [pl.BlockSpec((depth, tile), lambda j, s: (s[pair], j))]
            + [out] * len(acc),
            out_specs=[out, out],
            scratch_shapes=[pltpu.VMEM((2 * rows, depth), BF16)],
        ),
        out_shape=[
            jax.ShapeDtypeStruct((rows, width), F32),
            jax.ShapeDtypeStruct((rows, width), BF16 if last else F32),
        ],
        compiler_params=pltpu.CompilerParams(vmem_limit_bytes=24 * MIB),
        cost_estimate=pl.CostEstimate(
            flops=4 * rows * depth * width, bytes_accessed=2 * depth * width + 16 * rows * width, transcendentals=0
        ),
        name="next_query",
    )(info, *chosen, *far, weight, *acc)


def add_kernel(total_ref, more_ref, *refs):
    refs[-1][...] = total_ref[...] + more_ref[...]


def add_in_step(total, more, blocks, after):
    whole = pl.BlockSpec(memory_space=pltpu.VMEM)
    *blocks, total = pl.pallas_call(
        add_kernel,
        in_specs=[whole] * (2 + len(blocks) + len(after)),
        out_specs=[whole] * (len(blocks) + 1),
        out_shape=[jax.ShapeDtypeStruct(block.shape, block.dtype) for block in (*blocks, total)],
        input_output_aliases={2 + index: index for index in range(len(blocks))},
        compiler_params=pltpu.CompilerParams(vmem_limit_bytes=4 * MIB),
        name="add_squares",
    )(total, more, *blocks, *after)
    return total, blocks


def hold_kernel(*refs):
    pass


def hold(array, after):
    whole = pl.BlockSpec(memory_space=pltpu.VMEM)
    return pl.pallas_call(
        hold_kernel,
        in_specs=[whole] * (1 + len(after)),
        out_specs=whole,
        out_shape=jax.ShapeDtypeStruct(array.shape, array.dtype),
        input_output_aliases={0: 0},
        compiler_params=pltpu.CompilerParams(vmem_limit_bytes=4 * MIB),
        name="hold",
    )(array, *after)


def pick_kernel(codes, sizes, info_ref, *refs):
    outs = refs[len(refs) - len(codes) :]
    start = 0
    for code, size, out in zip(codes, sizes, outs):
        for choice in range(size):

            @pl.when(info_ref[code] == choice)
            def _():
                out[...] = refs[start + choice][...]

        start += size


def pick(info, codes, groups, after):
    whole = pl.BlockSpec(memory_space=pltpu.VMEM)
    first = groups[0][0]
    return pl.pallas_call(
        functools.partial(pick_kernel, codes, [len(group) for group in groups]),
        grid_spec=pltpu.PrefetchScalarGridSpec(
            num_scalar_prefetch=1,
            grid=(1,),
            in_specs=[whole] * (sum(len(group) for group in groups) + len(after)),
            out_specs=[whole] * len(groups),
        ),
        out_shape=[jax.ShapeDtypeStruct(first.shape, first.dtype)] * len(groups),
        compiler_params=pltpu.CompilerParams(vmem_limit_bytes=4 * MIB),
        name="pick",
    )(info, *[block for group in groups for block in group], *after)


def ring_of(n):
    return [2 * p for p in range(n // 2)] + [2 * p + 1 for p in reversed(range(n // 2))]


def tables(n):
    half = n // 2
    ring = ring_of(n)
    place = {chip: p for p, chip in enumerate(ring)}
    table = np.zeros((n, 2, 2 * half + n), np.int32)
    for chip in range(n):
        for core in range(2):

            def is_mine(q):
                return ring[(place[chip] + q) % n] // half == core

            for k in range(half):
                near = is_mine(k)
                assert near != is_mine(k - half)
                table[chip, core, k] = ring[(place[chip] + (k if near else k - half)) % n] - core * half
                q = (k if near else k - half) * (1 if core == 0 else -1)
                if k > 0:
                    table[chip, core, half + k] = block_choices(k, half).index(q)
                else:
                    table[chip, core, half] = 0 if near else 1 + core
            for q in range(1 - half, half + 1):
                real = q if core == 0 else -q
                pair = (real % half, 0 if is_mine(real) else 1)
                table[chip, core, 2 * half + q + half - 1] = sum_choices(q, half).index(pair)
    return table.reshape(2 * n, -1)


def block_choices(k, half):
    return list(dict.fromkeys([k, k - half, -k, half - k]))


def sum_choices(q, half):
    return [(k, kind) for k in dict.fromkeys([q % half, -q % half]) for kind in (0, 1)]


def choose(code, arrays):
    result = arrays[-1]
    for index in reversed(range(len(arrays) - 1)):
        result = jnp.where(code == index, arrays[index], result)
    return result


def on_ring(n, att_queries, att_keys, att_values, out_weight, residual, norm_gain, next_weight):
    half = n // 2
    ring = ring_of(n)
    up = [(ring[p], ring[(p + 1) % n]) for p in range(n)]
    swap = [(0, 1), (1, 0)]
    long_way = [(2 * a, 2 * b) for a, b in up] + [(2 * b + 1, 2 * a + 1) for a, b in up]
    short_way = [(2 * b, 2 * a) for a, b in up] + [(2 * a + 1, 2 * b + 1) for a, b in up]
    devices = ("tensor", "tokens")
    chip = lax.axis_index("tensor")
    core = lax.axis_index("tokens")
    rows, width = att_queries.shape
    info = lax.dynamic_index_in_dim(jnp.asarray(tables(n)), chip * 2 + core, 0, keepdims=False)

    heads_here = width // HD
    kv_head = chip * heads_here // (H // KVH)
    own = jnp.stack([lax.dynamic_index_in_dim(array, kv_head, 1, keepdims=False) for array in (att_keys, att_values)])
    far = lax.ppermute(own, "tokens", swap)
    attended, attended_peer = [], []
    for part in range(2):
        queries = (att_queries, part, 2)
        attended.append(attention(core[None], queries, own, far, attended))
        attended_peer.append(lax.ppermute(attended[-1], "tokens", swap))
    both = jnp.concatenate(
        [jnp.concatenate(attended, axis=1), jnp.concatenate(attended_peer, axis=1)], axis=0
    )

    made = {}

    def make(k, after=(), arrivals=()):
        made[k, 0], outgoing = project(info, k, 1, 0, both, out_weight, residual.shape[1], after)
        if arrivals:
            outgoing = hold(outgoing, arrivals)
        made[k, 1] = lax.ppermute(outgoing, "tokens", swap)

    def partial_sum(q):
        return choose(info[2 * half + q + half - 1], [made[key] for key in sum_choices(q, half)]).astype(F32)

    arrived = {}

    def send(way, step, previous):
        q = half - step + 1 if way == "long" else step - half
        value = partial_sum(q)
        if step > 1:
            value = value + lax.optimization_barrier((arrived[way], previous))[0].astype(F32)
        value = value.astype(BF16)
        arrived[way] = lax.ppermute(value, devices, long_way if way == "long" else short_way)
        return value

    make(0)
    make(1)
    long_value = send("long", 1, None)
    for k in range(half - 1, half // 2, -1):
        make(k, [long_value], [arrived["long"]])
    value = send("short", 1, long_value)
    for k in range(2, half // 2 + 1):
        make(k, [value], [arrived["short"]])
    value = send("long", 2, value)
    for step in range(2, half):
        value = send("short", step, value)
        value = send("long", step + 1, value)

    mixed = residual.astype(F32) + partial_sum(0) + arrived["long"].astype(F32) + arrived["short"].astype(F32)
    resid_out = mixed.astype(BF16)
    scaled = (mixed * norm_gain.astype(F32)).astype(BF16)
    squares = jnp.sum(mixed * mixed, axis=1)[None]

    held = {0: scaled}
    scaled_peer = lax.ppermute(scaled, "tokens", swap)
    long_block, short_block = scaled, hold(scaled, [scaled_peer])
    groups = {}
    for k in range(1, half):
        groups.setdefault(max(k, half - k), []).append(k)
    reach = 1
    acc, after = (), ()
    for step in range(1, half):
        long_block = lax.ppermute(long_block, devices, long_way)
        short_block = lax.ppermute(short_block, devices, short_way)
        if reach < n:
            more = lax.ppermute(squares, "tensor", [(c, c ^ reach) for c in range(n)])
            squares, (long_block,) = add_in_step(squares, more, [long_block], after)
            reach *= 2
        held[-step], held[step] = long_block, short_block
        pairs = groups.get(step, [])
        if pairs:
            wanted = {k: [held[q] for q in block_choices(k, half)] for k in pairs}
            others = [[wanted[k][index ^ 1] for index in range(len(wanted[k]))] for k in pairs]
            outgoing = pick(info, [half + k for k in pairs], others, after)
            far = [lax.ppermute(block, "tokens", swap) for block in outgoing]
            for k, block in zip(pairs, far):
                acc = query_block(info, k, half + k, wanted[k], [block], next_weight, acc, False)
            after = acc[:1]
    while reach < n:
        squares = squares + lax.ppermute(squares, "tensor", [(c, c ^ reach) for c in range(n)])
        reach *= 2
    meets = {b: ring[(p + half) % n] // half for p, b in enumerate(ring)}
    last_hop = [
        lax.ppermute(held[1 - half], devices, [(2 * a, 2 * b + meets[b]) for a, b in up]),
        lax.ppermute(held[1 - half], devices, [(2 * b + 1, 2 * a + meets[a]) for a, b in up]),
    ]
    acc = query_block(
        info, 0, half, [scaled, *last_hop], [scaled_peer, *reversed(last_hop)], next_weight, acc, True
    )
    query_sum = acc[0] + lax.ppermute(acc[1], "tokens", swap).astype(F32)
    factor = 1.0 / jnp.sqrt(squares[0] / D + EPS_NORM)
    return (resid_out, (query_sum * factor[:, None]).astype(BF16))


def on_mesh(n, att_queries, att_keys, att_values, out_weight, residual, norm_gain, next_weight):
    rows, width = att_queries.shape
    swap = [(0, 1), (1, 0)]
    chip = lax.axis_index("tensor")
    core = lax.axis_index("tokens")
    kv_head = chip * (width // HD) // (H // KVH)
    own = jnp.stack([lax.dynamic_index_in_dim(array, kv_head, 1, keepdims=False) for array in (att_keys, att_values)])
    far = lax.ppermute(own, "tokens", swap)
    attended = attention(core[None], (att_queries, 0, 1), own, far)
    both = lax.all_gather(attended, "tokens", axis=0, tiled=True)
    partial = dot(both, out_weight).astype(BF16)
    partial = lax.all_to_all(partial, "tokens", split_axis=0, concat_axis=1, tiled=True)
    attn_out = lax.psum_scatter(partial.astype(F32), "tensor", scatter_dimension=1, tiled=True)
    mixed = residual.astype(F32) + attn_out
    total_squares = lax.psum(jnp.sum(mixed * mixed, axis=1), "tensor")
    factor = 1.0 / jnp.sqrt(total_squares / D + EPS_NORM)
    normed = (mixed * factor[:, None] * norm_gain.astype(F32)).astype(BF16)
    gathered = lax.all_gather(normed, "tensor", axis=1, tiled=True)
    halves = lax.all_to_all(gathered, "tokens", split_axis=1, concat_axis=0, tiled=True)
    query_sum = lax.psum_scatter(dot(halves, next_weight), "tokens", scatter_dimension=0, tiled=True)
    return (mixed.astype(BF16), query_sum.astype(BF16))


def solution(mesh):
    n = mesh.shape["tensor"]
    in_specs = (
        P(("groups", "tokens"), "tensor"),
        P(("groups", "tokens"), None, None),
        P(("groups", "tokens"), None, None),
        P("tensor", "tokens"),
        P(("groups", "tokens"), "tensor"),
        P("tensor"),
        P("tokens", "tensor"),
    )
    out_specs = (P(("groups", "tokens"), "tensor"), P(("groups", "tokens"), "tensor"))
    body = functools.partial(on_ring if n <= RING_LIMIT else on_mesh, n)
    return jax.shard_map(body, mesh=mesh, in_specs=in_specs, out_specs=out_specs, check_vma=False)
```

```python
import functools
import math

import jax
import jax.numpy as jnp
import numpy as np
from jax import lax
from jax.experimental import pallas as pl
from jax.experimental.pallas import tpu as pltpu
from jax.sharding import PartitionSpec as P

D = 16384
H = 128
KVH = 8
HD = 128
EPS_NORM = 1e-05
BF16 = jnp.bfloat16
F32 = jnp.float32
RING_LIMIT = 16
EXTRA = 8
MIB = 1024 * 1024


def dot(a, b):
    return jnp.dot(a, b, preferred_element_type=F32)


def attention_kernel(heads, core_ref, q_ref, own_ref, far_ref, *refs):
    o_ref = refs[-1]
    k_ref, v_ref, pk_ref, pv_ref = own_ref.at[0], own_ref.at[1], far_ref.at[0], far_ref.at[1]
    rows = q_ref.shape[0]
    inv_root = 1.0 / math.sqrt(HD)
    query_pos = lax.broadcasted_iota(jnp.int32, (rows, rows), 0)
    key_pos = lax.broadcasted_iota(jnp.int32, (rows, rows), 1)
    visible = key_pos <= query_pos
    peer_visible = core_ref[0] == 1
    contract = (((1,), (1,)), ((), ()))
    for head in range(heads):
        columns = slice(head * HD, (head + 1) * HD)
        query = q_ref[:, columns]
        own = lax.dot_general(query, k_ref[...], contract, preferred_element_type=F32) * inv_root
        far = lax.dot_general(query, pk_ref[...], contract, preferred_element_type=F32) * inv_root
        own = jnp.where(visible, own, -1e30)
        far = jnp.where(peer_visible, far, -1e30)
        top = jnp.maximum(jnp.max(own, axis=1, keepdims=True), jnp.max(far, axis=1, keepdims=True))
        own = jnp.exp(own - top)
        far = jnp.exp(far - top)
        total = jnp.sum(own, axis=1, keepdims=True) + jnp.sum(far, axis=1, keepdims=True)
        mixed = dot(own.astype(BF16), v_ref[...]) + dot(far.astype(BF16), pv_ref[...])
        o_ref[:, columns] = (mixed / total).astype(BF16)


def attention(core, queries, own, far, after=()):
    queries, index, count = queries
    rows, width = queries.shape
    width = width // count
    heads = min(4, width // HD)
    first = index * width // (heads * HD)
    whole = pl.BlockSpec(memory_space=pltpu.VMEM)
    wanted = pl.BlockSpec((rows, heads * HD), lambda h, s: (0, first + h))
    part = pl.BlockSpec((rows, heads * HD), lambda h, s: (0, h))
    return pl.pallas_call(
        functools.partial(attention_kernel, heads),
        grid_spec=pltpu.PrefetchScalarGridSpec(
            num_scalar_prefetch=1,
            grid=(width // (heads * HD),),
            in_specs=[wanted, whole, whole] + [pl.BlockSpec(memory_space=pl.ANY)] * len(after),
            out_specs=part,
        ),
        out_shape=jax.ShapeDtypeStruct((rows, width), BF16),
        compiler_params=pltpu.CompilerParams(vmem_limit_bytes=24 * MIB),
        cost_estimate=pl.CostEstimate(
            flops=8 * rows * rows * width, bytes_accessed=4 * rows * width, transcendentals=2 * rows * rows * width // HD
        ),
        name="attention",
    )(core, queries, own, far, *after)


def project_kernel(info_ref, x_ref, w_ref, *refs):
    own_ref, peer_ref = refs[-2:]
    rows = own_ref.shape[0]
    result = dot(x_ref[...], w_ref[...]).astype(BF16)
    own_ref[...] = result[:rows]
    peer_ref[...] = result[rows:]


def project(info, pair, pieces, piece, both, weight, width, after):
    rows, depth = both.shape
    rows = rows // 2
    tile = min(512, width)
    tiles = width // tile
    out = pl.BlockSpec((rows, tile), lambda j, s: (0, j))
    return pl.pallas_call(
        project_kernel,
        grid_spec=pltpu.PrefetchScalarGridSpec(
            num_scalar_prefetch=1,
            grid=(tiles,),
            in_specs=[
                pl.BlockSpec(memory_space=pltpu.VMEM),
                pl.BlockSpec((depth, tile), lambda j, s: (0, (s[pair] * pieces + piece) * tiles + j)),
            ]
            + [pl.BlockSpec(memory_space=pltpu.VMEM)] * len(after),
            out_specs=[out, out],
        ),
        out_shape=[jax.ShapeDtypeStruct((rows, width), BF16)] * 2,
        compiler_params=pltpu.CompilerParams(vmem_limit_bytes=34 * MIB),
        cost_estimate=pl.CostEstimate(
            flops=4 * rows * depth * width, bytes_accessed=2 * depth * width, transcendentals=0
        ),
        name="project",
    )(info, both, weight, *after)


def query_kernel(sizes, code, first, info_ref, *refs):
    chosen, far = refs[: sizes[0]], refs[sizes[0] : sum(sizes)]
    w_ref = refs[sum(sizes)]
    own_ref, peer_ref, x_ref = refs[-3:]
    rows = own_ref.shape[0]

    @pl.when(pl.program_id(0) == 0)
    def _():
        for blocks, place in ((chosen, slice(0, rows)), (far, slice(rows, 2 * rows))):
            for choice, block in enumerate(blocks):

                @pl.when(info_ref[code] == choice if len(blocks) > 1 else True)
                def _():
                    x_ref[place] = block[:rows]

    for part, (place, out) in enumerate(((slice(0, rows), own_ref), (slice(rows, 2 * rows), peer_ref))):
        result = dot(x_ref[place], w_ref[...])
        if not first:
            result = result + refs[sum(sizes) + 1 + part][...]
        out[...] = result.astype(out.dtype)


def query_block(info, pair, code, chosen, far, weight, acc, rows, last):
    depth = far[0].shape[1]
    width = weight.shape[1]
    tile = min(512, width)
    whole = pl.BlockSpec(memory_space=pltpu.VMEM)
    out = pl.BlockSpec((rows, tile), lambda j, s: (0, j))
    return pl.pallas_call(
        functools.partial(query_kernel, (len(chosen), len(far)), code, not acc),
        grid_spec=pltpu.PrefetchScalarGridSpec(
            num_scalar_prefetch=1,
            grid=(width // tile,),
            in_specs=[whole] * (len(chosen) + len(far))
            + [pl.BlockSpec((depth, tile), lambda j, s: (s[pair], j))]
            + [out] * len(acc),
            out_specs=[out, out],
            scratch_shapes=[pltpu.VMEM((2 * rows, depth), BF16)],
        ),
        out_shape=[
            jax.ShapeDtypeStruct((rows, width), F32),
            jax.ShapeDtypeStruct((rows, width), BF16 if last else F32),
        ],
        compiler_params=pltpu.CompilerParams(vmem_limit_bytes=24 * MIB),
        cost_estimate=pl.CostEstimate(
            flops=4 * rows * depth * width, bytes_accessed=2 * depth * width + 16 * rows * width, transcendentals=0
        ),
        name="next_query",
    )(info, *chosen, *far, weight, *acc)


def hold_kernel(*refs):
    pass


def hold(array, after):
    whole = pl.BlockSpec(memory_space=pltpu.VMEM)
    return pl.pallas_call(
        hold_kernel,
        in_specs=[whole] * (1 + len(after)),
        out_specs=whole,
        out_shape=jax.ShapeDtypeStruct(array.shape, array.dtype),
        input_output_aliases={0: 0},
        compiler_params=pltpu.CompilerParams(vmem_limit_bytes=4 * MIB),
        name="hold",
    )(array, *after)


def pick_kernel(codes, sizes, info_ref, *refs):
    outs = refs[len(refs) - len(codes) :]
    start = 0
    for code, size, out in zip(codes, sizes, outs):
        for choice in range(size):

            @pl.when(info_ref[code] == choice)
            def _():
                out[...] = refs[start + choice][: out.shape[0]]

        start += size


def pick(info, codes, groups, rows, after):
    whole = pl.BlockSpec(memory_space=pltpu.VMEM)
    shape = jax.ShapeDtypeStruct((rows, groups[0][0].shape[1]), groups[0][0].dtype)
    return pl.pallas_call(
        functools.partial(pick_kernel, codes, [len(group) for group in groups]),
        grid_spec=pltpu.PrefetchScalarGridSpec(
            num_scalar_prefetch=1,
            grid=(1,),
            in_specs=[whole] * (sum(len(group) for group in groups) + len(after)),
            out_specs=[whole] * len(groups),
        ),
        out_shape=[shape] * len(groups),
        compiler_params=pltpu.CompilerParams(vmem_limit_bytes=4 * MIB),
        name="pick",
    )(info, *[block for group in groups for block in group], *after)


def ring_of(n):
    return [2 * p for p in range(n // 2)] + [2 * p + 1 for p in reversed(range(n // 2))]


def tables(n):
    half = n // 2
    ring = ring_of(n)
    place = {chip: p for p, chip in enumerate(ring)}
    table = np.zeros((n, 2, 2 * half + n), np.int32)
    for chip in range(n):
        for core in range(2):

            def is_mine(q):
                return ring[(place[chip] + q) % n] // half == core

            for k in range(half):
                near = is_mine(k)
                assert near != is_mine(k - half)
                table[chip, core, k] = ring[(place[chip] + (k if near else k - half)) % n] - core * half
                q = (k if near else k - half) * (1 if core == 0 else -1)
                if k > 0:
                    table[chip, core, half + k] = block_choices(k, half).index(q)
                else:
                    table[chip, core, half] = 0 if near else 1 + core
            for q in range(1 - half, half + 1):
                real = q if core == 0 else -q
                pair = (real % half, 0 if is_mine(real) else 1)
                table[chip, core, 2 * half + q + half - 1] = sum_choices(q, half).index(pair)
    return table.reshape(2 * n, -1)


def block_choices(k, half):
    return list(dict.fromkeys([k, k - half, -k, half - k]))


def sum_choices(q, half):
    return [(k, kind) for k in dict.fromkeys([q % half, -q % half]) for kind in (0, 1)]


def choose(code, arrays):
    result = arrays[-1]
    for index in reversed(range(len(arrays) - 1)):
        result = jnp.where(code == index, arrays[index], result)
    return result


def on_ring(n, att_queries, att_keys, att_values, out_weight, residual, norm_gain, next_weight):
    half = n // 2
    ring = ring_of(n)
    up = [(ring[p], ring[(p + 1) % n]) for p in range(n)]
    swap = [(0, 1), (1, 0)]
    long_way = [(2 * a, 2 * b) for a, b in up] + [(2 * b + 1, 2 * a + 1) for a, b in up]
    short_way = [(2 * b, 2 * a) for a, b in up] + [(2 * a + 1, 2 * b + 1) for a, b in up]
    devices = ("tensor", "tokens")
    chip = lax.axis_index("tensor")
    core = lax.axis_index("tokens")
    rows, width = att_queries.shape
    info = lax.dynamic_index_in_dim(jnp.asarray(tables(n)), chip * 2 + core, 0, keepdims=False)

    heads_here = width // HD
    kv_head = chip * heads_here // (H // KVH)
    own = jnp.stack([lax.dynamic_index_in_dim(array, kv_head, 1, keepdims=False) for array in (att_keys, att_values)])
    far = lax.ppermute(own, "tokens", swap)
    attended, attended_peer = [], []
    for part in range(2):
        queries = (att_queries, part, 2)
        attended.append(attention(core[None], queries, own, far, attended))
        attended_peer.append(lax.ppermute(attended[-1], "tokens", swap))
    both = jnp.concatenate(
        [jnp.concatenate(attended, axis=1), jnp.concatenate(attended_peer, axis=1)], axis=0
    )

    made = {}

    def make(k, after=(), arrivals=()):
        made[k, 0], outgoing = project(info, k, 1, 0, both, out_weight, residual.shape[1], after)
        if arrivals:
            outgoing = hold(outgoing, arrivals)
        made[k, 1] = lax.ppermute(outgoing, "tokens", swap)

    def partial_sum(q):
        return choose(info[2 * half + q + half - 1], [made[key] for key in sum_choices(q, half)]).astype(F32)

    arrived = {}

    def send(way, step, previous):
        q = half - step + 1 if way == "long" else step - half
        value = partial_sum(q)
        if step > 1:
            value = value + lax.optimization_barrier((arrived[way], previous))[0].astype(F32)
        value = value.astype(BF16)
        arrived[way] = lax.ppermute(value, devices, long_way if way == "long" else short_way)
        return value

    make(0)
    make(1)
    long_value = send("long", 1, None)
    for k in range(half - 1, half // 2, -1):
        make(k, [long_value], [arrived["long"]])
    short_value = send("short", 1, long_value)
    value = send("long", 2, short_value)
    for k in range(2, half // 2 + 1):
        make(k, [short_value, value], [arrived["short"], arrived["long"]])
    for step in range(2, half):
        value = send("short", step, value)
        value = send("long", step + 1, value)

    mixed = residual.astype(F32) + partial_sum(0) + arrived["long"].astype(F32) + arrived["short"].astype(F32)
    resid_out = mixed.astype(BF16)
    scaled = (mixed * norm_gain.astype(F32)).astype(BF16)
    squares = jnp.sum(mixed * mixed, axis=1)
    high = lax.reduce_precision(squares, 8, 7)
    middle = lax.reduce_precision(squares - high, 8, 7)
    digits = jnp.stack([high, middle, squares - high - middle]).astype(BF16)
    digits = jnp.pad(digits, ((0, EXTRA - 3), (0, scaled.shape[1] - rows)))
    message = jnp.concatenate([scaled, digits], axis=0)

    def squares_in(block):
        return block[rows : rows + 3, :rows].astype(F32)

    held = {0: message}
    message_peer = lax.ppermute(message, "tokens", swap)
    long_block, short_block = message, hold(message, [message_peer])
    groups = {}
    for k in range(1, half):
        groups.setdefault(max(k, half - k), []).append(k)
    acc, after = (), ()
    for step in range(1, half):
        long_block = lax.ppermute(long_block, devices, long_way)
        short_block = lax.ppermute(short_block, devices, short_way)
        if after:
            long_block = hold(long_block, after)
        held[-step], held[step] = long_block, short_block
        pairs = groups.get(step, [])
        if pairs:
            wanted = {k: [held[q] for q in block_choices(k, half)] for k in pairs}
            others = [[wanted[k][index ^ 1] for index in range(len(wanted[k]))] for k in pairs]
            outgoing = pick(info, [half + k for k in pairs], others, rows, after)
            far = [lax.ppermute(block, "tokens", swap) for block in outgoing]
            for k, block in zip(pairs, far):
                acc = query_block(info, k, half + k, wanted[k], [block], next_weight, acc, rows, False)
            after = acc[:1]
    meets = {b: ring[(p + half) % n] // half for p, b in enumerate(ring)}
    last_hop = [
        lax.ppermute(held[1 - half], devices, [(2 * a, 2 * b + meets[b]) for a, b in up]),
        lax.ppermute(held[1 - half], devices, [(2 * b + 1, 2 * a + meets[a]) for a, b in up]),
    ]
    acc = query_block(
        info, 0, half, [message, *last_hop], [message_peer, *reversed(last_hop)], next_weight, acc, rows, True
    )
    query_sum = acc[0] + lax.ppermute(acc[1], "tokens", swap).astype(F32)
    last = [squares_in(block) for block in last_hop]
    digits = lax.ppermute(jnp.where(core == 0, last[1], last[0]), "tokens", swap)
    digits = digits + jnp.where(core == 0, last[0], last[1])
    for step in range(1, half):
        digits = digits + squares_in(held[step]) + squares_in(held[-step])
    squares = squares + jnp.sum(digits, axis=0)
    factor = 1.0 / jnp.sqrt(squares / D + EPS_NORM)
    return (resid_out, (query_sum * factor[:, None]).astype(BF16))


def on_mesh(n, att_queries, att_keys, att_values, out_weight, residual, norm_gain, next_weight):
    rows, width = att_queries.shape
    swap = [(0, 1), (1, 0)]
    chip = lax.axis_index("tensor")
    core = lax.axis_index("tokens")
    kv_head = chip * (width // HD) // (H // KVH)
    own = jnp.stack([lax.dynamic_index_in_dim(array, kv_head, 1, keepdims=False) for array in (att_keys, att_values)])
    far = lax.ppermute(own, "tokens", swap)
    attended = attention(core[None], (att_queries, 0, 1), own, far)
    both = lax.all_gather(attended, "tokens", axis=0, tiled=True)
    partial = dot(both, out_weight).astype(BF16)
    partial = lax.all_to_all(partial, "tokens", split_axis=0, concat_axis=1, tiled=True)
    attn_out = lax.psum_scatter(partial.astype(F32), "tensor", scatter_dimension=1, tiled=True)
    mixed = residual.astype(F32) + attn_out
    total_squares = lax.psum(jnp.sum(mixed * mixed, axis=1), "tensor")
    factor = 1.0 / jnp.sqrt(total_squares / D + EPS_NORM)
    normed = (mixed * factor[:, None] * norm_gain.astype(F32)).astype(BF16)
    gathered = lax.all_gather(normed, "tensor", axis=1, tiled=True)
    halves = lax.all_to_all(gathered, "tokens", split_axis=1, concat_axis=0, tiled=True)
    query_sum = lax.psum_scatter(dot(halves, next_weight), "tokens", scatter_dimension=0, tiled=True)
    return (mixed.astype(BF16), query_sum.astype(BF16))


def solution(mesh):
    n = mesh.shape["tensor"]
    in_specs = (
        P(("groups", "tokens"), "tensor"),
        P(("groups", "tokens"), None, None),
        P(("groups", "tokens"), None, None),
        P("tensor", "tokens"),
        P(("groups", "tokens"), "tensor"),
        P("tensor"),
        P("tokens", "tensor"),
    )
    out_specs = (P(("groups", "tokens"), "tensor"), P(("groups", "tokens"), "tensor"))
    body = functools.partial(on_ring if n <= RING_LIMIT else on_mesh, n)
    return jax.shard_map(body, mesh=mesh, in_specs=in_specs, out_specs=out_specs, check_vma=False)
```

```python
import functools
import math

import jax
import jax.numpy as jnp
import numpy as np
from jax import lax
from jax.experimental import pallas as pl
from jax.experimental.pallas import tpu as pltpu
from jax.sharding import PartitionSpec as P

D = 16384
H = 128
KVH = 8
HD = 128
EPS_NORM = 1e-05
BF16 = jnp.bfloat16
F32 = jnp.float32
RING_LIMIT = 16
MIB = 1024 * 1024


def dot(a, b):
    return jnp.dot(a, b, preferred_element_type=F32)


def attention_kernel(heads, core_ref, q_ref, own_ref, far_ref, *refs):
    o_ref = refs[-1]
    k_ref, v_ref, pk_ref, pv_ref = own_ref.at[0], own_ref.at[1], far_ref.at[0], far_ref.at[1]
    rows = q_ref.shape[0]
    inv_root = 1.0 / math.sqrt(HD)
    query_pos = lax.broadcasted_iota(jnp.int32, (rows, rows), 0)
    key_pos = lax.broadcasted_iota(jnp.int32, (rows, rows), 1)
    visible = key_pos <= query_pos
    peer_visible = core_ref[0] == 1
    contract = (((1,), (1,)), ((), ()))
    for head in range(heads):
        columns = slice(head * HD, (head + 1) * HD)
        query = q_ref[:, columns]
        own = lax.dot_general(query, k_ref[...], contract, preferred_element_type=F32) * inv_root
        far = lax.dot_general(query, pk_ref[...], contract, preferred_element_type=F32) * inv_root
        own = jnp.where(visible, own, -1e30)
        far = jnp.where(peer_visible, far, -1e30)
        top = jnp.maximum(jnp.max(own, axis=1, keepdims=True), jnp.max(far, axis=1, keepdims=True))
        own = jnp.exp(own - top)
        far = jnp.exp(far - top)
        total = jnp.sum(own, axis=1, keepdims=True) + jnp.sum(far, axis=1, keepdims=True)
        mixed = dot(own.astype(BF16), v_ref[...]) + dot(far.astype(BF16), pv_ref[...])
        o_ref[:, columns] = (mixed / total).astype(BF16)


def attention(core, queries, own, far, after=()):
    queries, index, count = queries
    rows, width = queries.shape
    width = width // count
    heads = min(4, width // HD)
    first = index * width // (heads * HD)
    whole = pl.BlockSpec(memory_space=pltpu.VMEM)
    wanted = pl.BlockSpec((rows, heads * HD), lambda h, s: (0, first + h))
    part = pl.BlockSpec((rows, heads * HD), lambda h, s: (0, h))
    return pl.pallas_call(
        functools.partial(attention_kernel, heads),
        grid_spec=pltpu.PrefetchScalarGridSpec(
            num_scalar_prefetch=1,
            grid=(width // (heads * HD),),
            in_specs=[wanted, whole, whole] + [pl.BlockSpec(memory_space=pl.ANY)] * len(after),
            out_specs=part,
        ),
        out_shape=jax.ShapeDtypeStruct((rows, width), BF16),
        compiler_params=pltpu.CompilerParams(vmem_limit_bytes=24 * MIB),
        cost_estimate=pl.CostEstimate(
            flops=8 * rows * rows * width, bytes_accessed=4 * rows * width, transcendentals=2 * rows * rows * width // HD
        ),
        name="attention",
    )(core, queries, own, far, *after)


def project_kernel(info_ref, x_ref, w_ref, *refs):
    own_ref, peer_ref = refs[-2:]
    rows = own_ref.shape[0]
    result = dot(x_ref[...], w_ref[...]).astype(BF16)
    own_ref[...] = result[:rows]
    peer_ref[...] = result[rows:]


def project(info, pair, pieces, piece, both, weight, width, after):
    rows, depth = both.shape
    rows = rows // 2
    tile = min(512, width)
    tiles = width // tile
    out = pl.BlockSpec((rows, tile), lambda j, s: (0, j))
    return pl.pallas_call(
        project_kernel,
        grid_spec=pltpu.PrefetchScalarGridSpec(
            num_scalar_prefetch=1,
            grid=(tiles,),
            in_specs=[
                pl.BlockSpec(memory_space=pltpu.VMEM),
                pl.BlockSpec((depth, tile), lambda j, s: (0, (s[pair] * pieces + piece) * tiles + j)),
            ]
            + [pl.BlockSpec(memory_space=pltpu.VMEM)] * len(after),
            out_specs=[out, out],
        ),
        out_shape=[jax.ShapeDtypeStruct((rows, width), BF16)] * 2,
        compiler_params=pltpu.CompilerParams(vmem_limit_bytes=34 * MIB),
        cost_estimate=pl.CostEstimate(
            flops=4 * rows * depth * width, bytes_accessed=2 * depth * width, transcendentals=0
        ),
        name="project",
    )(info, both, weight, *after)


def query_kernel(codes, sizes, first, info_ref, *refs):
    own_ref, peer_ref, x_ref = refs[-3:]
    rows = own_ref.shape[0]
    start = 0
    fills = []
    for index, (code, groups) in enumerate(zip(codes, sizes)):
        for half_index, (choices, parts) in enumerate(groups):
            fills.append((index, half_index, code, refs[start : start + choices * parts], parts))
            start += choices * parts
    weights = refs[start : start + len(codes)]
    depth = weights[0].shape[0]

    @pl.when(pl.program_id(0) == 0)
    def _():
        for index, half_index, code, blocks, parts in fills:
            place = slice(half_index * rows, (half_index + 1) * rows)
            width = depth // parts
            for choice in range(len(blocks) // parts):

                @pl.when(info_ref[code] == choice if len(blocks) > parts else True)
                def _():
                    for part in range(parts):
                        columns = slice(index * depth + part * width, index * depth + (part + 1) * width)
                        x_ref[place, columns] = blocks[choice * parts + part][...]

    for half_index, out in enumerate((own_ref, peer_ref)):
        place = slice(half_index * rows, (half_index + 1) * rows)
        result = None if first else refs[start + len(codes) + half_index][...]
        for index, w_ref in enumerate(weights):
            product = dot(x_ref[place, index * depth : (index + 1) * depth], w_ref[...])
            result = product if result is None else result + product
        out[...] = result.astype(out.dtype)


def query_block(info, half, blocks, weight, acc, last):
    rows = blocks[0][1][0][0].shape[0]
    depth = sum(piece.shape[1] for piece in blocks[0][1][0])
    width = weight.shape[1]
    tile = min(512, width)
    whole = pl.BlockSpec(memory_space=pltpu.VMEM)
    out = pl.BlockSpec((rows, tile), lambda j, s: (0, j))
    sizes = [[(len(choices), len(choices[0])) for choices in (own, far)] for _, own, far in blocks]
    arrays = [piece for _, own, far in blocks for choices in (own, far) for choice in choices for piece in choice]
    weight_specs = [
        pl.BlockSpec((depth, tile), functools.partial(lambda pair, j, s: (s[pair], j), pair)) for pair, _, _ in blocks
    ]
    return pl.pallas_call(
        functools.partial(query_kernel, [half + pair for pair, _, _ in blocks], sizes, not acc),
        grid_spec=pltpu.PrefetchScalarGridSpec(
            num_scalar_prefetch=1,
            grid=(width // tile,),
            in_specs=[whole] * len(arrays) + weight_specs + [out] * len(acc),
            out_specs=[out, out],
            scratch_shapes=[pltpu.VMEM((2 * rows, depth * len(blocks)), BF16)],
        ),
        out_shape=[
            jax.ShapeDtypeStruct((rows, width), F32),
            jax.ShapeDtypeStruct((rows, width), BF16 if last else F32),
        ],
        compiler_params=pltpu.CompilerParams(vmem_limit_bytes=26 * MIB),
        cost_estimate=pl.CostEstimate(
            flops=4 * rows * depth * width * len(blocks),
            bytes_accessed=2 * depth * width * len(blocks) + 16 * rows * width,
            transcendentals=0,
        ),
        name="next_query",
    )(info, *arrays, *[weight] * len(blocks), *acc)


def add_kernel(total_ref, more_ref, *refs):
    refs[-1][...] = total_ref[...] + more_ref[...]


def add_in_step(total, more, blocks, after):
    whole = pl.BlockSpec(memory_space=pltpu.VMEM)
    *blocks, total = pl.pallas_call(
        add_kernel,
        in_specs=[whole] * (2 + len(blocks) + len(after)),
        out_specs=[whole] * (len(blocks) + 1),
        out_shape=[jax.ShapeDtypeStruct(block.shape, block.dtype) for block in (*blocks, total)],
        input_output_aliases={2 + index: index for index in range(len(blocks))},
        compiler_params=pltpu.CompilerParams(vmem_limit_bytes=4 * MIB),
        name="add_squares",
    )(total, more, *blocks, *after)
    return total, blocks


def hold_kernel(*refs):
    pass


def hold(array, after):
    whole = pl.BlockSpec(memory_space=pltpu.VMEM)
    return pl.pallas_call(
        hold_kernel,
        in_specs=[whole] * (1 + len(after)),
        out_specs=whole,
        out_shape=jax.ShapeDtypeStruct(array.shape, array.dtype),
        input_output_aliases={0: 0},
        compiler_params=pltpu.CompilerParams(vmem_limit_bytes=4 * MIB),
        name="hold",
    )(array, *after)


def pick_kernel(codes, sizes, info_ref, *refs):
    outs = refs[len(refs) - len(codes) :]
    start = 0
    for code, (choices, parts), out in zip(codes, sizes, outs):
        width = out.shape[1] // parts
        for choice in range(choices):

            @pl.when(info_ref[code] == choice)
            def _():
                for part in range(parts):
                    out[:, part * width : (part + 1) * width] = refs[start + choice * parts + part][...]

        start += choices * parts


def pick(info, codes, groups, after):
    whole = pl.BlockSpec(memory_space=pltpu.VMEM)
    arrays = [piece for group in groups for choice in group for piece in choice]
    rows, piece_width = arrays[0].shape
    shape = jax.ShapeDtypeStruct((rows, piece_width * len(groups[0][0])), arrays[0].dtype)
    return pl.pallas_call(
        functools.partial(pick_kernel, codes, [(len(group), len(group[0])) for group in groups]),
        grid_spec=pltpu.PrefetchScalarGridSpec(
            num_scalar_prefetch=1,
            grid=(1,),
            in_specs=[whole] * (len(arrays) + len(after)),
            out_specs=[whole] * len(groups),
        ),
        out_shape=[shape] * len(groups),
        compiler_params=pltpu.CompilerParams(vmem_limit_bytes=4 * MIB),
        name="pick",
    )(info, *arrays, *after)


def ring_of(n):
    return [2 * p for p in range(n // 2)] + [2 * p + 1 for p in reversed(range(n // 2))]


def tables(n):
    half = n // 2
    ring = ring_of(n)
    place = {chip: p for p, chip in enumerate(ring)}
    table = np.zeros((n, 2, 2 * half + n), np.int32)
    for chip in range(n):
        for core in range(2):

            def is_mine(q):
                return ring[(place[chip] + q) % n] // half == core

            for k in range(half):
                near = is_mine(k)
                assert near != is_mine(k - half)
                table[chip, core, k] = ring[(place[chip] + (k if near else k - half)) % n] - core * half
                q = (k if near else k - half) * (1 if core == 0 else -1)
                if k > 0:
                    table[chip, core, half + k] = block_choices(k, half).index(q)
                else:
                    table[chip, core, half] = 0 if near else 1 + core
            for q in range(1 - half, half + 1):
                real = q if core == 0 else -q
                pair = (real % half, 0 if is_mine(real) else 1)
                table[chip, core, 2 * half + q + half - 1] = sum_choices(q, half).index(pair)
    return table.reshape(2 * n, -1)


def block_choices(k, half):
    return list(dict.fromkeys([k, k - half, -k, half - k]))


def sum_choices(q, half):
    return [(k, kind) for k in dict.fromkeys([q % half, -q % half]) for kind in (0, 1)]


def choose(code, arrays):
    result = arrays[-1]
    for index in reversed(range(len(arrays) - 1)):
        result = jnp.where(code == index, arrays[index], result)
    return result


def on_ring(n, att_queries, att_keys, att_values, out_weight, residual, norm_gain, next_weight):
    half = n // 2
    ring = ring_of(n)
    up = [(ring[p], ring[(p + 1) % n]) for p in range(n)]
    swap = [(0, 1), (1, 0)]
    long_way = [(2 * a, 2 * b) for a, b in up] + [(2 * b + 1, 2 * a + 1) for a, b in up]
    short_way = [(2 * b, 2 * a) for a, b in up] + [(2 * a + 1, 2 * b + 1) for a, b in up]
    devices = ("tensor", "tokens")
    chip = lax.axis_index("tensor")
    core = lax.axis_index("tokens")
    rows, width = att_queries.shape
    info = lax.dynamic_index_in_dim(jnp.asarray(tables(n)), chip * 2 + core, 0, keepdims=False)

    heads_here = width // HD
    kv_head = chip * heads_here // (H // KVH)
    own = jnp.stack([lax.dynamic_index_in_dim(array, kv_head, 1, keepdims=False) for array in (att_keys, att_values)])
    far = lax.ppermute(own, "tokens", swap)
    attended, attended_peer = [], []
    for part in range(2):
        queries = (att_queries, part, 2)
        attended.append(attention(core[None], queries, own, far, attended))
        attended_peer.append(lax.ppermute(attended[-1], "tokens", swap))
    both = jnp.concatenate(
        [jnp.concatenate(attended, axis=1), jnp.concatenate(attended_peer, axis=1)], axis=0
    )

    made = {}

    def make(k, after=(), arrivals=()):
        made[k, 0], outgoing = project(info, k, 1, 0, both, out_weight, residual.shape[1], after)
        if arrivals:
            outgoing = hold(outgoing, arrivals)
        made[k, 1] = lax.ppermute(outgoing, "tokens", swap)

    def partial_sum(q):
        return choose(info[2 * half + q + half - 1], [made[key] for key in sum_choices(q, half)]).astype(F32)

    arrived = {}

    def send(way, step, previous):
        q = half - step + 1 if way == "long" else step - half
        value = partial_sum(q)
        if step > 1:
            value = value + lax.optimization_barrier((arrived[way], previous))[0].astype(F32)
        value = value.astype(BF16)
        arrived[way] = lax.ppermute(value, devices, long_way if way == "long" else short_way)
        return value

    make(0)
    make(1)
    long_value = send("long", 1, None)
    for k in range(half - 1, half // 2, -1):
        make(k, [long_value], [arrived["long"]])
    value = send("short", 1, long_value)
    for k in range(2, half // 2 + 1):
        make(k, [value], [arrived["short"]])
    value = send("long", 2, value)
    for step in range(2, half):
        value = send("short", step, value)
        value = send("long", step + 1, value)

    arrived["short"] = hold(arrived["short"], [])
    mixed = residual.astype(F32) + partial_sum(0) + arrived["long"].astype(F32) + arrived["short"].astype(F32)
    resid_out = mixed.astype(BF16)
    scaled = (mixed * norm_gain.astype(F32)).astype(BF16)
    squares = jnp.sum(mixed * mixed, axis=1)[None]

    scaled_peer = lax.ppermute(scaled, "tokens", swap)
    held = {0: scaled}
    groups = {}
    for k in range(1, half):
        groups.setdefault(max(k, half - k), []).append(k)
    reach = 1
    acc, after = (), ()
    for step in range(1, half):
        held[-step] = lax.ppermute(held[1 - step], devices, long_way)
        held[step] = lax.ppermute(held[step - 1], devices, short_way)
        if reach < n:
            more = lax.ppermute(squares, "tensor", [(c, c ^ reach) for c in range(n)])
            squares, (held[-step],) = add_in_step(squares, more, [held[-step]], after)
            reach *= 2
        pairs = groups.get(step, [])
        if pairs:
            wanted = {k: [[held[q]] for q in block_choices(k, half)] for k in pairs}
            others = [[wanted[k][index ^ 1] for index in range(len(wanted[k]))] for k in pairs]
            outgoing = pick(info, [half + k for k in pairs], others, after)
            far = [lax.ppermute(block, "tokens", swap) for block in outgoing]
            blocks = [(k, wanted[k], [[block]]) for k, block in zip(pairs, far)]
            acc = query_block(info, half, blocks, next_weight, acc, False)
            after = acc[:1]
    while reach < n:
        squares = squares + lax.ppermute(squares, "tensor", [(c, c ^ reach) for c in range(n)])
        reach *= 2
    meets = {b: ring[(p + half) % n] // half for p, b in enumerate(ring)}
    last_hop = [
        lax.ppermute(held[1 - half], devices, [(2 * a, 2 * b + meets[b]) for a, b in up]),
        lax.ppermute(held[1 - half], devices, [(2 * b + 1, 2 * a + meets[a]) for a, b in up]),
    ]
    own = [[scaled], *[[block] for block in last_hop]]
    far = [[scaled_peer], *[[block] for block in reversed(last_hop)]]
    acc = query_block(info, half, [(0, own, far)], next_weight, acc, True)
    query_sum = acc[0] + lax.ppermute(acc[1], "tokens", swap).astype(F32)
    factor = 1.0 / jnp.sqrt(squares[0] / D + EPS_NORM)
    return (resid_out, (query_sum * factor[:, None]).astype(BF16))


def on_mesh(n, att_queries, att_keys, att_values, out_weight, residual, norm_gain, next_weight):
    rows, width = att_queries.shape
    swap = [(0, 1), (1, 0)]
    chip = lax.axis_index("tensor")
    core = lax.axis_index("tokens")
    kv_head = chip * (width // HD) // (H // KVH)
    own = jnp.stack([lax.dynamic_index_in_dim(array, kv_head, 1, keepdims=False) for array in (att_keys, att_values)])
    far = lax.ppermute(own, "tokens", swap)
    attended = attention(core[None], (att_queries, 0, 1), own, far)
    both = lax.all_gather(attended, "tokens", axis=0, tiled=True)
    partial = dot(both, out_weight).astype(BF16)
    partial = lax.all_to_all(partial, "tokens", split_axis=0, concat_axis=1, tiled=True)
    attn_out = lax.psum_scatter(partial.astype(F32), "tensor", scatter_dimension=1, tiled=True)
    mixed = residual.astype(F32) + attn_out
    total_squares = lax.psum(jnp.sum(mixed * mixed, axis=1), "tensor")
    factor = 1.0 / jnp.sqrt(total_squares / D + EPS_NORM)
    normed = (mixed * factor[:, None] * norm_gain.astype(F32)).astype(BF16)
    gathered = lax.all_gather(normed, "tensor", axis=1, tiled=True)
    halves = lax.all_to_all(gathered, "tokens", split_axis=1, concat_axis=0, tiled=True)
    query_sum = lax.psum_scatter(dot(halves, next_weight), "tokens", scatter_dimension=0, tiled=True)
    return (mixed.astype(BF16), query_sum.astype(BF16))


def solution(mesh):
    n = mesh.shape["tensor"]
    in_specs = (
        P(("groups", "tokens"), "tensor"),
        P(("groups", "tokens"), None, None),
        P(("groups", "tokens"), None, None),
        P("tensor", "tokens"),
        P(("groups", "tokens"), "tensor"),
        P("tensor"),
        P("tokens", "tensor"),
    )
    out_specs = (P(("groups", "tokens"), "tensor"), P(("groups", "tokens"), "tensor"))
    body = functools.partial(on_ring if n <= RING_LIMIT else on_mesh, n)
    return jax.shard_map(body, mesh=mesh, in_specs=in_specs, out_specs=out_specs, check_vma=False)
```

```python
import functools
import math

import jax
import jax.numpy as jnp
import numpy as np
from jax import lax
from jax.experimental import pallas as pl
from jax.experimental.pallas import tpu as pltpu
from jax.sharding import PartitionSpec as P

D = 16384
H = 128
KVH = 8
HD = 128
EPS_NORM = 1e-05
BF16 = jnp.bfloat16
F32 = jnp.float32
RING_LIMIT = 16
MIB = 1024 * 1024


def dot(a, b):
    return jnp.dot(a, b, preferred_element_type=F32)


def attention_kernel(heads, core_ref, q_ref, own_ref, far_ref, *refs):
    o_ref = refs[-1]
    k_ref, v_ref, pk_ref, pv_ref = own_ref.at[0], own_ref.at[1], far_ref.at[0], far_ref.at[1]
    rows = q_ref.shape[0]
    scale = math.log2(math.e) / math.sqrt(HD)
    query_pos = lax.broadcasted_iota(jnp.int32, (rows, rows), 0)
    key_pos = lax.broadcasted_iota(jnp.int32, (rows, rows), 1)
    visible = key_pos <= query_pos
    peer_visible = core_ref[0] == 1
    contract = (((1,), (1,)), ((), ()))
    for head in range(heads):
        columns = slice(head * HD, (head + 1) * HD)
        query = q_ref[:, columns]
        own = lax.dot_general(query, k_ref[...], contract, preferred_element_type=F32)
        far = lax.dot_general(query, pk_ref[...], contract, preferred_element_type=F32)
        own = jnp.where(visible, own, -1e30)
        far = jnp.where(peer_visible, far, -1e30)
        top = jnp.maximum(jnp.max(own, axis=1, keepdims=True), jnp.max(far, axis=1, keepdims=True))
        own = jnp.exp2((own - top) * scale)
        far = jnp.exp2((far - top) * scale)
        total = jnp.sum(own, axis=1, keepdims=True) + jnp.sum(far, axis=1, keepdims=True)
        mixed = dot(own.astype(BF16), v_ref[...]) + dot(far.astype(BF16), pv_ref[...])
        o_ref[:, columns] = (mixed / total).astype(BF16)


def attention(core, queries, own, far, after=()):
    queries, index, count = queries
    rows, width = queries.shape
    width = width // count
    heads = min(4, width // HD)
    first = index * width // (heads * HD)
    whole = pl.BlockSpec(memory_space=pltpu.VMEM)
    wanted = pl.BlockSpec((rows, heads * HD), lambda h, s: (0, first + h))
    part = pl.BlockSpec((rows, heads * HD), lambda h, s: (0, h))
    return pl.pallas_call(
        functools.partial(attention_kernel, heads),
        grid_spec=pltpu.PrefetchScalarGridSpec(
            num_scalar_prefetch=1,
            grid=(width // (heads * HD),),
            in_specs=[wanted, whole, whole] + [pl.BlockSpec(memory_space=pl.ANY)] * len(after),
            out_specs=part,
        ),
        out_shape=jax.ShapeDtypeStruct((rows, width), BF16),
        compiler_params=pltpu.CompilerParams(vmem_limit_bytes=24 * MIB),
        cost_estimate=pl.CostEstimate(
            flops=8 * rows * rows * width, bytes_accessed=4 * rows * width, transcendentals=2 * rows * rows * width // HD
        ),
        name="attention",
    )(core, queries, own, far, *after)


def project_kernel(info_ref, x_ref, w_ref, *refs):
    own_ref, peer_ref = refs[-2:]
    rows = own_ref.shape[0]
    result = dot(x_ref[...], w_ref[...]).astype(BF16)
    own_ref[...] = result[:rows]
    peer_ref[...] = result[rows:]


def project(info, pair, pieces, piece, both, weight, width, after):
    rows, depth = both.shape
    rows = rows // 2
    tile = min(512, width)
    tiles = width // tile
    out = pl.BlockSpec((rows, tile), lambda j, s: (0, j))
    return pl.pallas_call(
        project_kernel,
        grid_spec=pltpu.PrefetchScalarGridSpec(
            num_scalar_prefetch=1,
            grid=(tiles,),
            in_specs=[
                pl.BlockSpec(memory_space=pltpu.VMEM),
                pl.BlockSpec((depth, tile), lambda j, s: (0, (s[pair] * pieces + piece) * tiles + j)),
            ]
            + [pl.BlockSpec(memory_space=pltpu.VMEM)] * len(after),
            out_specs=[out, out],
        ),
        out_shape=[jax.ShapeDtypeStruct((rows, width), BF16)] * 2,
        compiler_params=pltpu.CompilerParams(vmem_limit_bytes=34 * MIB),
        cost_estimate=pl.CostEstimate(
            flops=4 * rows * depth * width, bytes_accessed=2 * depth * width, transcendentals=0
        ),
        name="project",
    )(info, both, weight, *after)


def query_kernel(codes, sizes, first, info_ref, *refs):
    own_ref, peer_ref, x_ref = refs[-3:]
    rows = own_ref.shape[0]
    start = 0
    fills = []
    for index, (code, groups) in enumerate(zip(codes, sizes)):
        for half_index, (choices, parts) in enumerate(groups):
            fills.append((index, half_index, code, refs[start : start + choices * parts], parts))
            start += choices * parts
    weights = refs[start : start + len(codes)]
    depth = weights[0].shape[0]

    @pl.when(pl.program_id(0) == 0)
    def _():
        for index, half_index, code, blocks, parts in fills:
            place = slice(half_index * rows, (half_index + 1) * rows)
            width = depth // parts
            for choice in range(len(blocks) // parts):

                @pl.when(info_ref[code] == choice if len(blocks) > parts else True)
                def _():
                    for part in range(parts):
                        columns = slice(index * depth + part * width, index * depth + (part + 1) * width)
                        x_ref[place, columns] = blocks[choice * parts + part][...]

    for half_index, out in enumerate((own_ref, peer_ref)):
        place = slice(half_index * rows, (half_index + 1) * rows)
        result = None if first else refs[start + len(codes) + half_index][...]
        for index, w_ref in enumerate(weights):
            product = dot(x_ref[place, index * depth : (index + 1) * depth], w_ref[...])
            result = product if result is None else result + product
        out[...] = result.astype(out.dtype)


def query_block(info, half, blocks, weight, acc, last):
    rows = blocks[0][1][0][0].shape[0]
    depth = sum(piece.shape[1] for piece in blocks[0][1][0])
    width = weight.shape[1]
    tile = min(512, width)
    whole = pl.BlockSpec(memory_space=pltpu.VMEM)
    out = pl.BlockSpec((rows, tile), lambda j, s: (0, j))
    sizes = [[(len(choices), len(choices[0])) for choices in (own, far)] for _, own, far in blocks]
    arrays = [piece for _, own, far in blocks for choices in (own, far) for choice in choices for piece in choice]
    weight_specs = [
        pl.BlockSpec((depth, tile), functools.partial(lambda pair, j, s: (s[pair], j), pair)) for pair, _, _ in blocks
    ]
    return pl.pallas_call(
        functools.partial(query_kernel, [half + pair for pair, _, _ in blocks], sizes, not acc),
        grid_spec=pltpu.PrefetchScalarGridSpec(
            num_scalar_prefetch=1,
            grid=(width // tile,),
            in_specs=[whole] * len(arrays) + weight_specs + [out] * len(acc),
            out_specs=[out, out],
            scratch_shapes=[pltpu.VMEM((2 * rows, depth * len(blocks)), BF16)],
        ),
        out_shape=[
            jax.ShapeDtypeStruct((rows, width), F32),
            jax.ShapeDtypeStruct((rows, width), BF16 if last else F32),
        ],
        compiler_params=pltpu.CompilerParams(vmem_limit_bytes=26 * MIB),
        cost_estimate=pl.CostEstimate(
            flops=4 * rows * depth * width * len(blocks),
            bytes_accessed=2 * depth * width * len(blocks) + 16 * rows * width,
            transcendentals=0,
        ),
        name="next_query",
    )(info, *arrays, *[weight] * len(blocks), *acc)


def add_kernel(total_ref, more_ref, *refs):
    refs[-1][...] = total_ref[...] + more_ref[...]


def add_in_step(total, more, blocks, after):
    whole = pl.BlockSpec(memory_space=pltpu.VMEM)
    *blocks, total = pl.pallas_call(
        add_kernel,
        in_specs=[whole] * (2 + len(blocks) + len(after)),
        out_specs=[whole] * (len(blocks) + 1),
        out_shape=[jax.ShapeDtypeStruct(block.shape, block.dtype) for block in (*blocks, total)],
        input_output_aliases={2 + index: index for index in range(len(blocks))},
        compiler_params=pltpu.CompilerParams(vmem_limit_bytes=4 * MIB),
        name="add_squares",
    )(total, more, *blocks, *after)
    return total, blocks


def hold_kernel(*refs):
    pass


def hold(array, after):
    whole = pl.BlockSpec(memory_space=pltpu.VMEM)
    return pl.pallas_call(
        hold_kernel,
        in_specs=[whole] * (1 + len(after)),
        out_specs=whole,
        out_shape=jax.ShapeDtypeStruct(array.shape, array.dtype),
        input_output_aliases={0: 0},
        compiler_params=pltpu.CompilerParams(vmem_limit_bytes=4 * MIB),
        name="hold",
    )(array, *after)


def pick_kernel(codes, sizes, info_ref, *refs):
    outs = refs[len(refs) - len(codes) :]
    start = 0
    for code, (choices, parts), out in zip(codes, sizes, outs):
        width = out.shape[1] // parts
        for choice in range(choices):

            @pl.when(info_ref[code] == choice)
            def _():
                for part in range(parts):
                    out[:, part * width : (part + 1) * width] = refs[start + choice * parts + part][...]

        start += choices * parts


def pick(info, codes, groups, after):
    whole = pl.BlockSpec(memory_space=pltpu.VMEM)
    arrays = [piece for group in groups for choice in group for piece in choice]
    rows, piece_width = arrays[0].shape
    shape = jax.ShapeDtypeStruct((rows, piece_width * len(groups[0][0])), arrays[0].dtype)
    return pl.pallas_call(
        functools.partial(pick_kernel, codes, [(len(group), len(group[0])) for group in groups]),
        grid_spec=pltpu.PrefetchScalarGridSpec(
            num_scalar_prefetch=1,
            grid=(1,),
            in_specs=[whole] * (len(arrays) + len(after)),
            out_specs=[whole] * len(groups),
        ),
        out_shape=[shape] * len(groups),
        compiler_params=pltpu.CompilerParams(vmem_limit_bytes=4 * MIB),
        name="pick",
    )(info, *arrays, *after)


def ring_of(n):
    return [2 * p for p in range(n // 2)] + [2 * p + 1 for p in reversed(range(n // 2))]


def tables(n):
    half = n // 2
    ring = ring_of(n)
    place = {chip: p for p, chip in enumerate(ring)}
    table = np.zeros((n, 2, 2 * half + n), np.int32)
    for chip in range(n):
        for core in range(2):

            def is_mine(q):
                return ring[(place[chip] + q) % n] // half == core

            for k in range(half):
                near = is_mine(k)
                assert near != is_mine(k - half)
                table[chip, core, k] = ring[(place[chip] + (k if near else k - half)) % n] - core * half
                q = (k if near else k - half) * (1 if core == 0 else -1)
                if k > 0:
                    table[chip, core, half + k] = block_choices(k, half).index(q)
                else:
                    table[chip, core, half] = 0 if near else 1 + core
            for q in range(1 - half, half + 1):
                real = q if core == 0 else -q
                pair = (real % half, 0 if is_mine(real) else 1)
                table[chip, core, 2 * half + q + half - 1] = sum_choices(q, half).index(pair)
    return table.reshape(2 * n, -1)


def block_choices(k, half):
    return list(dict.fromkeys([k, k - half, -k, half - k]))


def sum_choices(q, half):
    return [(k, kind) for k in dict.fromkeys([q % half, -q % half]) for kind in (0, 1)]


def choose(code, arrays):
    result = arrays[-1]
    for index in reversed(range(len(arrays) - 1)):
        result = jnp.where(code == index, arrays[index], result)
    return result


def on_ring(n, att_queries, att_keys, att_values, out_weight, residual, norm_gain, next_weight):
    half = n // 2
    ring = ring_of(n)
    up = [(ring[p], ring[(p + 1) % n]) for p in range(n)]
    swap = [(0, 1), (1, 0)]
    long_way = [(2 * a, 2 * b) for a, b in up] + [(2 * b + 1, 2 * a + 1) for a, b in up]
    short_way = [(2 * b, 2 * a) for a, b in up] + [(2 * a + 1, 2 * b + 1) for a, b in up]
    devices = ("tensor", "tokens")
    chip = lax.axis_index("tensor")
    core = lax.axis_index("tokens")
    rows, width = att_queries.shape
    info = lax.dynamic_index_in_dim(jnp.asarray(tables(n)), chip * 2 + core, 0, keepdims=False)

    heads_here = width // HD
    kv_head = chip * heads_here // (H // KVH)
    own = jnp.stack([lax.dynamic_index_in_dim(array, kv_head, 1, keepdims=False) for array in (att_keys, att_values)])
    far = lax.ppermute(own, "tokens", swap)
    attended, attended_peer = [], []
    for part in range(2):
        queries = (att_queries, part, 2)
        attended.append(attention(core[None], queries, own, far, attended))
        attended_peer.append(lax.ppermute(attended[-1], "tokens", swap))
    both = jnp.concatenate(
        [jnp.concatenate(attended, axis=1), jnp.concatenate(attended_peer, axis=1)], axis=0
    )

    made = {}

    def make(k, after=(), arrivals=()):
        made[k, 0], outgoing = project(info, k, 1, 0, both, out_weight, residual.shape[1], after)
        if arrivals:
            outgoing = hold(outgoing, arrivals)
        made[k, 1] = lax.ppermute(outgoing, "tokens", swap)

    def partial_sum(q):
        return choose(info[2 * half + q + half - 1], [made[key] for key in sum_choices(q, half)]).astype(F32)

    arrived = {}

    def send(way, step, previous):
        q = half - step + 1 if way == "long" else step - half
        value = partial_sum(q)
        if step > 1:
            before = arrived[way]
            if (way, step) == ("short", 2):
                before = hold(before, [arrived["long"]])
            value = value + lax.optimization_barrier((before, previous))[0].astype(F32)
        value = value.astype(BF16)
        arrived[way] = lax.ppermute(value, devices, long_way if way == "long" else short_way)
        return value

    make(0)
    make(1)
    long_value = send("long", 1, None)
    for k in range(half - 1, half // 2, -1):
        make(k, [long_value], [arrived["long"]])
    short_value = send("short", 1, long_value)
    value = send("long", 2, short_value)
    for k in range(2, half // 2 + 1):
        make(k, [short_value, value])
    for step in range(2, half):
        value = send("short", step, value)
        value = send("long", step + 1, value)

    arrived["short"] = hold(arrived["short"], [])
    own_sum = partial_sum(0)

    def mix(long_sum, short_sum):
        return residual.astype(F32) + own_sum + long_sum.astype(F32) + short_sum.astype(F32)

    scaled = (mix(arrived["long"], arrived["short"]) * norm_gain.astype(F32)).astype(BF16)
    mixed = mix(*lax.optimization_barrier((arrived["long"], arrived["short"], scaled))[:2])
    resid_out = mixed.astype(BF16)
    squares = jnp.sum(mixed * mixed, axis=1)[None]

    scaled_peer = lax.ppermute(scaled, "tokens", swap)
    held = {0: scaled}
    groups = {}
    for k in range(1, half):
        groups.setdefault(max(k, half - k), []).append(k)
    reach = 1
    acc, after = (), ()
    for step in range(1, half):
        held[-step] = lax.ppermute(held[1 - step], devices, long_way)
        held[step] = lax.ppermute(held[step - 1], devices, short_way)
        if reach < n:
            more = lax.ppermute(squares, "tensor", [(c, c ^ reach) for c in range(n)])
            squares, (held[-step],) = add_in_step(squares, more, [held[-step]], after)
            reach *= 2
        pairs = groups.get(step, [])
        if pairs:
            wanted = {k: [[held[q]] for q in block_choices(k, half)] for k in pairs}
            others = [[wanted[k][index ^ 1] for index in range(len(wanted[k]))] for k in pairs]
            outgoing = pick(info, [half + k for k in pairs], others, after)
            far = [lax.ppermute(block, "tokens", swap) for block in outgoing]
            blocks = [(k, wanted[k], [[block]]) for k, block in zip(pairs, far)]
            acc = query_block(info, half, blocks, next_weight, acc, False)
            after = acc[:1]
    while reach < n:
        squares = squares + lax.ppermute(squares, "tensor", [(c, c ^ reach) for c in range(n)])
        reach *= 2
    meets = {b: ring[(p + half) % n] // half for p, b in enumerate(ring)}
    last_hop = [
        lax.ppermute(held[1 - half], devices, [(2 * a, 2 * b + meets[b]) for a, b in up]),
        lax.ppermute(held[1 - half], devices, [(2 * b + 1, 2 * a + meets[a]) for a, b in up]),
    ]
    own = [[scaled], *[[block] for block in last_hop]]
    far = [[scaled_peer], *[[block] for block in reversed(last_hop)]]
    acc = query_block(info, half, [(0, own, far)], next_weight, acc, True)
    query_sum = acc[0] + lax.ppermute(acc[1], "tokens", swap).astype(F32)
    factor = 1.0 / jnp.sqrt(squares[0] / D + EPS_NORM)
    return (resid_out, (query_sum * factor[:, None]).astype(BF16))


def on_mesh(n, att_queries, att_keys, att_values, out_weight, residual, norm_gain, next_weight):
    rows, width = att_queries.shape
    swap = [(0, 1), (1, 0)]
    chip = lax.axis_index("tensor")
    core = lax.axis_index("tokens")
    kv_head = chip * (width // HD) // (H // KVH)
    own = jnp.stack([lax.dynamic_index_in_dim(array, kv_head, 1, keepdims=False) for array in (att_keys, att_values)])
    far = lax.ppermute(own, "tokens", swap)
    attended = attention(core[None], (att_queries, 0, 1), own, far)
    both = lax.all_gather(attended, "tokens", axis=0, tiled=True)
    partial = dot(both, out_weight).astype(BF16)
    partial = lax.all_to_all(partial, "tokens", split_axis=0, concat_axis=1, tiled=True)
    attn_out = lax.psum_scatter(partial.astype(F32), "tensor", scatter_dimension=1, tiled=True)
    mixed = residual.astype(F32) + attn_out
    total_squares = lax.psum(jnp.sum(mixed * mixed, axis=1), "tensor")
    factor = 1.0 / jnp.sqrt(total_squares / D + EPS_NORM)
    normed = (mixed * factor[:, None] * norm_gain.astype(F32)).astype(BF16)
    gathered = lax.all_gather(normed, "tensor", axis=1, tiled=True)
    halves = lax.all_to_all(gathered, "tokens", split_axis=1, concat_axis=0, tiled=True)
    query_sum = lax.psum_scatter(dot(halves, next_weight), "tokens", scatter_dimension=0, tiled=True)
    return (mixed.astype(BF16), query_sum.astype(BF16))


def solution(mesh):
    n = mesh.shape["tensor"]
    in_specs = (
        P(("groups", "tokens"), "tensor"),
        P(("groups", "tokens"), None, None),
        P(("groups", "tokens"), None, None),
        P("tensor", "tokens"),
        P(("groups", "tokens"), "tensor"),
        P("tensor"),
        P("tokens", "tensor"),
    )
    out_specs = (P(("groups", "tokens"), "tensor"), P(("groups", "tokens"), "tensor"))
    body = functools.partial(on_ring if n <= RING_LIMIT else on_mesh, n)
    return jax.shard_map(body, mesh=mesh, in_specs=in_specs, out_specs=out_specs, check_vma=False)
```

```python
import functools
import math

import jax
import jax.numpy as jnp
import numpy as np
from jax import lax
from jax.experimental import pallas as pl
from jax.experimental.pallas import tpu as pltpu
from jax.sharding import PartitionSpec as P

D = 16384
H = 128
KVH = 8
HD = 128
EPS_NORM = 1e-05
BF16 = jnp.bfloat16
F32 = jnp.float32
RING_LIMIT = 16
MIB = 1024 * 1024


def dot(a, b):
    return jnp.dot(a, b, preferred_element_type=F32)


def attention_kernel(heads, core_ref, q_ref, own_ref, far_ref, *refs):
    o_ref = refs[-1]
    k_ref, v_ref, pk_ref, pv_ref = own_ref.at[0], own_ref.at[1], far_ref.at[0], far_ref.at[1]
    rows = q_ref.shape[0]
    scale = math.log2(math.e) / math.sqrt(HD)
    query_pos = lax.broadcasted_iota(jnp.int32, (rows, rows), 0)
    key_pos = lax.broadcasted_iota(jnp.int32, (rows, rows), 1)
    visible = key_pos <= query_pos
    peer_visible = core_ref[0] == 1
    contract = (((1,), (1,)), ((), ()))
    for head in range(heads):
        columns = slice(head * HD, (head + 1) * HD)
        query = q_ref[:, columns]
        own = lax.dot_general(query, k_ref[...], contract, preferred_element_type=F32)
        far = lax.dot_general(query, pk_ref[...], contract, preferred_element_type=F32)
        own = jnp.where(visible, own, -1e30)
        far = jnp.where(peer_visible, far, -1e30)
        top = jnp.maximum(jnp.max(own, axis=1, keepdims=True), jnp.max(far, axis=1, keepdims=True))
        own = jnp.exp2((own - top) * scale)
        far = jnp.exp2((far - top) * scale)
        total = jnp.sum(own, axis=1, keepdims=True) + jnp.sum(far, axis=1, keepdims=True)
        mixed = dot(own.astype(BF16), v_ref[...]) + dot(far.astype(BF16), pv_ref[...])
        o_ref[:, columns] = (mixed / total).astype(BF16)


def attention(core, queries, own, far, after=()):
    queries, index, count = queries
    rows, width = queries.shape
    width = width // count
    heads = min(4, width // HD)
    first = index * width // (heads * HD)
    whole = pl.BlockSpec(memory_space=pltpu.VMEM)
    wanted = pl.BlockSpec((rows, heads * HD), lambda h, s: (0, first + h))
    part = pl.BlockSpec((rows, heads * HD), lambda h, s: (0, h))
    return pl.pallas_call(
        functools.partial(attention_kernel, heads),
        grid_spec=pltpu.PrefetchScalarGridSpec(
            num_scalar_prefetch=1,
            grid=(width // (heads * HD),),
            in_specs=[wanted, whole, whole] + [pl.BlockSpec(memory_space=pl.ANY)] * len(after),
            out_specs=part,
        ),
        out_shape=jax.ShapeDtypeStruct((rows, width), BF16),
        compiler_params=pltpu.CompilerParams(vmem_limit_bytes=24 * MIB),
        cost_estimate=pl.CostEstimate(
            flops=8 * rows * rows * width, bytes_accessed=4 * rows * width, transcendentals=2 * rows * rows * width // HD
        ),
        name="attention",
    )(core, queries, own, far, *after)


def project_kernel(info_ref, x_ref, w_ref, *refs):
    own_ref, peer_ref = refs[-2:]
    rows = own_ref.shape[0]
    result = dot(x_ref[...], w_ref[...]).astype(BF16)
    own_ref[...] = result[:rows]
    peer_ref[...] = result[rows:]


def project(info, pair, pieces, piece, both, weight, width, after):
    rows, depth = both.shape
    rows = rows // 2
    tile = min(512, width)
    tiles = width // tile
    out = pl.BlockSpec((rows, tile), lambda j, s: (0, j))
    return pl.pallas_call(
        project_kernel,
        grid_spec=pltpu.PrefetchScalarGridSpec(
            num_scalar_prefetch=1,
            grid=(tiles,),
            in_specs=[
                pl.BlockSpec(memory_space=pltpu.VMEM),
                pl.BlockSpec((depth, tile), lambda j, s: (0, (s[pair] * pieces + piece) * tiles + j)),
            ]
            + [pl.BlockSpec(memory_space=pltpu.VMEM)] * len(after),
            out_specs=[out, out],
        ),
        out_shape=[jax.ShapeDtypeStruct((rows, width), BF16)] * 2,
        compiler_params=pltpu.CompilerParams(vmem_limit_bytes=34 * MIB),
        cost_estimate=pl.CostEstimate(
            flops=4 * rows * depth * width, bytes_accessed=2 * depth * width, transcendentals=0
        ),
        name="project",
    )(info, both, weight, *after)


def query_kernel(codes, sizes, first, info_ref, *refs):
    own_ref, peer_ref, x_ref = refs[-3:]
    rows = own_ref.shape[0]
    start = 0
    fills = []
    for index, (code, groups) in enumerate(zip(codes, sizes)):
        for half_index, (choices, parts) in enumerate(groups):
            fills.append((index, half_index, code, refs[start : start + choices * parts], parts))
            start += choices * parts
    weights = refs[start : start + len(codes)]
    depth = weights[0].shape[0]

    @pl.when(pl.program_id(0) == 0)
    def _():
        for index, half_index, code, blocks, parts in fills:
            place = slice(half_index * rows, (half_index + 1) * rows)
            width = depth // parts
            for choice in range(len(blocks) // parts):

                @pl.when(info_ref[code] == choice if len(blocks) > parts else True)
                def _():
                    for part in range(parts):
                        columns = slice(index * depth + part * width, index * depth + (part + 1) * width)
                        x_ref[place, columns] = blocks[choice * parts + part][...]

    for half_index, out in enumerate((own_ref, peer_ref)):
        place = slice(half_index * rows, (half_index + 1) * rows)
        result = None if first else refs[start + len(codes) + half_index][...]
        for index, w_ref in enumerate(weights):
            product = dot(x_ref[place, index * depth : (index + 1) * depth], w_ref[...])
            result = product if result is None else result + product
        out[...] = result.astype(out.dtype)


def query_block(info, half, blocks, weight, acc, last):
    rows = blocks[0][1][0][0].shape[0]
    depth = sum(piece.shape[1] for piece in blocks[0][1][0])
    width = weight.shape[1]
    tile = min(512, width)
    whole = pl.BlockSpec(memory_space=pltpu.VMEM)
    out = pl.BlockSpec((rows, tile), lambda j, s: (0, j))
    sizes = [[(len(choices), len(choices[0])) for choices in (own, far)] for _, own, far in blocks]
    arrays = [piece for _, own, far in blocks for choices in (own, far) for choice in choices for piece in choice]
    weight_specs = [
        pl.BlockSpec((depth, tile), functools.partial(lambda pair, j, s: (s[pair], j), pair)) for pair, _, _ in blocks
    ]
    return pl.pallas_call(
        functools.partial(query_kernel, [half + pair for pair, _, _ in blocks], sizes, not acc),
        grid_spec=pltpu.PrefetchScalarGridSpec(
            num_scalar_prefetch=1,
            grid=(width // tile,),
            in_specs=[whole] * len(arrays) + weight_specs + [out] * len(acc),
            out_specs=[out, out],
            scratch_shapes=[pltpu.VMEM((2 * rows, depth * len(blocks)), BF16)],
        ),
        out_shape=[
            jax.ShapeDtypeStruct((rows, width), F32),
            jax.ShapeDtypeStruct((rows, width), BF16 if last else F32),
        ],
        compiler_params=pltpu.CompilerParams(vmem_limit_bytes=26 * MIB),
        cost_estimate=pl.CostEstimate(
            flops=4 * rows * depth * width * len(blocks),
            bytes_accessed=2 * depth * width * len(blocks) + 16 * rows * width,
            transcendentals=0,
        ),
        name="next_query",
    )(info, *arrays, *[weight] * len(blocks), *acc)


def add_kernel(total_ref, more_ref, *refs):
    refs[-1][...] = total_ref[...] + more_ref[...]


def add_in_step(total, more, blocks, after):
    whole = pl.BlockSpec(memory_space=pltpu.VMEM)
    *blocks, total = pl.pallas_call(
        add_kernel,
        in_specs=[whole] * (2 + len(blocks) + len(after)),
        out_specs=[whole] * (len(blocks) + 1),
        out_shape=[jax.ShapeDtypeStruct(block.shape, block.dtype) for block in (*blocks, total)],
        input_output_aliases={2 + index: index for index in range(len(blocks))},
        compiler_params=pltpu.CompilerParams(vmem_limit_bytes=4 * MIB),
        name="add_squares",
    )(total, more, *blocks, *after)
    return total, blocks


def hold_kernel(*refs):
    pass


def hold(array, after):
    whole = pl.BlockSpec(memory_space=pltpu.VMEM)
    return pl.pallas_call(
        hold_kernel,
        in_specs=[whole] * (1 + len(after)),
        out_specs=whole,
        out_shape=jax.ShapeDtypeStruct(array.shape, array.dtype),
        input_output_aliases={0: 0},
        compiler_params=pltpu.CompilerParams(vmem_limit_bytes=4 * MIB),
        name="hold",
    )(array, *after)


def pick_kernel(codes, sizes, info_ref, *refs):
    outs = refs[len(refs) - len(codes) :]
    start = 0
    for code, (choices, parts), out in zip(codes, sizes, outs):
        width = out.shape[1] // parts
        for choice in range(choices):

            @pl.when(info_ref[code] == choice)
            def _():
                for part in range(parts):
                    out[:, part * width : (part + 1) * width] = refs[start + choice * parts + part][...]

        start += choices * parts


def pick(info, codes, groups, after):
    whole = pl.BlockSpec(memory_space=pltpu.VMEM)
    arrays = [piece for group in groups for choice in group for piece in choice]
    rows, piece_width = arrays[0].shape
    shape = jax.ShapeDtypeStruct((rows, piece_width * len(groups[0][0])), arrays[0].dtype)
    return pl.pallas_call(
        functools.partial(pick_kernel, codes, [(len(group), len(group[0])) for group in groups]),
        grid_spec=pltpu.PrefetchScalarGridSpec(
            num_scalar_prefetch=1,
            grid=(1,),
            in_specs=[whole] * (len(arrays) + len(after)),
            out_specs=[whole] * len(groups),
        ),
        out_shape=[shape] * len(groups),
        compiler_params=pltpu.CompilerParams(vmem_limit_bytes=4 * MIB),
        name="pick",
    )(info, *arrays, *after)


def ring_of(n):
    return [2 * p for p in range(n // 2)] + [2 * p + 1 for p in reversed(range(n // 2))]


def tables(n):
    half = n // 2
    ring = ring_of(n)
    place = {chip: p for p, chip in enumerate(ring)}
    table = np.zeros((n, 2, 2 * half), np.int32)
    flags = np.zeros((n, 2, 4 * n), bool)
    for chip in range(n):
        for core in range(2):

            def is_mine(q):
                return ring[(place[chip] + q) % n] // half == core

            for k in range(half):
                near = is_mine(k)
                assert near != is_mine(k - half)
                table[chip, core, k] = ring[(place[chip] + (k if near else k - half)) % n] - core * half
                q = (k if near else k - half) * (1 if core == 0 else -1)
                if k > 0:
                    table[chip, core, half + k] = block_choices(k, half).index(q)
                else:
                    table[chip, core, half] = 0 if near else 1 + core
            for q in range(1 - half, half + 1):
                real = q if core == 0 else -q
                pair = (real % half, 0 if is_mine(real) else 1)
                flags[chip, core, 4 * (q + half - 1) + sum_choices(q, half).index(pair)] = True
    return table.reshape(2 * n, -1), flags.reshape(2 * n, -1)


def block_choices(k, half):
    return list(dict.fromkeys([k, k - half, -k, half - k]))


def sum_choices(q, half):
    return [(k, kind) for k in dict.fromkeys([q % half, -q % half]) for kind in (0, 1)]


def choose(flags, arrays):
    result = arrays[-1]
    for index in reversed(range(len(arrays) - 1)):
        result = jnp.where(flags[index], arrays[index], result)
    return result


def on_ring(n, att_queries, att_keys, att_values, out_weight, residual, norm_gain, next_weight):
    half = n // 2
    ring = ring_of(n)
    up = [(ring[p], ring[(p + 1) % n]) for p in range(n)]
    swap = [(0, 1), (1, 0)]
    long_way = [(2 * a, 2 * b) for a, b in up] + [(2 * b + 1, 2 * a + 1) for a, b in up]
    short_way = [(2 * b, 2 * a) for a, b in up] + [(2 * a + 1, 2 * b + 1) for a, b in up]
    devices = ("tensor", "tokens")
    chip = lax.axis_index("tensor")
    core = lax.axis_index("tokens")
    rows, width = att_queries.shape
    info, flags = (
        lax.dynamic_index_in_dim(jnp.asarray(table), chip * 2 + core, 0, keepdims=False) for table in tables(n)
    )

    heads_here = width // HD
    kv_head = chip * heads_here // (H // KVH)
    own = jnp.stack([lax.dynamic_index_in_dim(array, kv_head, 1, keepdims=False) for array in (att_keys, att_values)])
    far = lax.ppermute(own, "tokens", swap)
    attended, attended_peer = [], []
    for part in range(2):
        queries = (att_queries, part, 2)
        attended.append(attention(core[None], queries, own, far, attended))
        attended_peer.append(lax.ppermute(attended[-1], "tokens", swap))
    both = jnp.concatenate(
        [jnp.concatenate(attended, axis=1), jnp.concatenate(attended_peer, axis=1)], axis=0
    )

    made = {}

    def make(k, after=(), arrivals=()):
        made[k, 0], outgoing = project(info, k, 1, 0, both, out_weight, residual.shape[1], after)
        if arrivals:
            outgoing = hold(outgoing, arrivals)
        made[k, 1] = lax.ppermute(outgoing, "tokens", swap)

    def partial_sum(q):
        return choose(flags[4 * (q + half - 1) :], [made[key] for key in sum_choices(q, half)]).astype(F32)

    arrived = {}

    def send(way, step, previous):
        q = half - step + 1 if way == "long" else step - half
        value = partial_sum(q)
        if step > 1:
            before = arrived[way]
            if (way, step) == ("short", 2):
                before = hold(before, [arrived["long"]])
            value = value + lax.optimization_barrier((before, previous))[0].astype(F32)
        value = value.astype(BF16)
        arrived[way] = lax.ppermute(value, devices, long_way if way == "long" else short_way)
        return value

    make(0)
    make(1)
    long_value = send("long", 1, None)
    for k in range(half - 1, half // 2, -1):
        make(k, [long_value], [arrived["long"]])
    short_value = send("short", 1, long_value)
    value = send("long", 2, short_value)
    for k in range(2, half // 2 + 1):
        make(k, [short_value, value])
    for step in range(2, half):
        value = send("short", step, value)
        value = send("long", step + 1, value)

    arrived["short"] = hold(arrived["short"], [])
    mixed = residual.astype(F32) + partial_sum(0) + arrived["long"].astype(F32) + arrived["short"].astype(F32)
    resid_out = mixed.astype(BF16)
    scaled = (mixed * norm_gain.astype(F32)).astype(BF16)
    squares = jnp.sum(mixed * mixed, axis=1)[None]

    scaled_peer = lax.ppermute(scaled, "tokens", swap)
    held = {0: scaled}
    groups = {}
    for k in range(1, half):
        groups.setdefault(max(k, half - k), []).append(k)
    reach = 1
    acc, after = (), ()
    for step in range(1, half):
        held[-step] = lax.ppermute(held[1 - step], devices, long_way)
        held[step] = lax.ppermute(held[step - 1], devices, short_way)
        if reach < n:
            more = lax.ppermute(squares, "tensor", [(c, c ^ reach) for c in range(n)])
            squares, (held[-step],) = add_in_step(squares, more, [held[-step]], after)
            reach *= 2
        pairs = groups.get(step, [])
        if pairs:
            wanted = {k: [[held[q]] for q in block_choices(k, half)] for k in pairs}
            others = [[wanted[k][index ^ 1] for index in range(len(wanted[k]))] for k in pairs]
            outgoing = pick(info, [half + k for k in pairs], others, after)
            far = [lax.ppermute(block, "tokens", swap) for block in outgoing]
            blocks = [(k, wanted[k], [[block]]) for k, block in zip(pairs, far)]
            acc = query_block(info, half, blocks, next_weight, acc, False)
            after = acc[:1]
    while reach < n:
        squares = squares + lax.ppermute(squares, "tensor", [(c, c ^ reach) for c in range(n)])
        reach *= 2
    meets = {b: ring[(p + half) % n] // half for p, b in enumerate(ring)}
    last_hop = [
        lax.ppermute(held[1 - half], devices, [(2 * a, 2 * b + meets[b]) for a, b in up]),
        lax.ppermute(held[1 - half], devices, [(2 * b + 1, 2 * a + meets[a]) for a, b in up]),
    ]
    own = [[scaled], *[[block] for block in last_hop]]
    far = [[scaled_peer], *[[block] for block in reversed(last_hop)]]
    acc = query_block(info, half, [(0, own, far)], next_weight, acc, True)
    query_sum = acc[0] + lax.ppermute(acc[1], "tokens", swap).astype(F32)
    factor = 1.0 / jnp.sqrt(squares[0] / D + EPS_NORM)
    return (resid_out, (query_sum * factor[:, None]).astype(BF16))


def on_mesh(n, att_queries, att_keys, att_values, out_weight, residual, norm_gain, next_weight):
    rows, width = att_queries.shape
    swap = [(0, 1), (1, 0)]
    chip = lax.axis_index("tensor")
    core = lax.axis_index("tokens")
    kv_head = chip * (width // HD) // (H // KVH)
    own = jnp.stack([lax.dynamic_index_in_dim(array, kv_head, 1, keepdims=False) for array in (att_keys, att_values)])
    far = lax.ppermute(own, "tokens", swap)
    attended = attention(core[None], (att_queries, 0, 1), own, far)
    both = lax.all_gather(attended, "tokens", axis=0, tiled=True)
    partial = dot(both, out_weight).astype(BF16)
    partial = lax.all_to_all(partial, "tokens", split_axis=0, concat_axis=1, tiled=True)
    attn_out = lax.psum_scatter(partial.astype(F32), "tensor", scatter_dimension=1, tiled=True)
    mixed = residual.astype(F32) + attn_out
    total_squares = lax.psum(jnp.sum(mixed * mixed, axis=1), "tensor")
    factor = 1.0 / jnp.sqrt(total_squares / D + EPS_NORM)
    normed = (mixed * factor[:, None] * norm_gain.astype(F32)).astype(BF16)
    gathered = lax.all_gather(normed, "tensor", axis=1, tiled=True)
    halves = lax.all_to_all(gathered, "tokens", split_axis=1, concat_axis=0, tiled=True)
    query_sum = lax.psum_scatter(dot(halves, next_weight), "tokens", scatter_dimension=0, tiled=True)
    return (mixed.astype(BF16), query_sum.astype(BF16))


def solution(mesh):
    n = mesh.shape["tensor"]
    in_specs = (
        P(("groups", "tokens"), "tensor"),
        P(("groups", "tokens"), None, None),
        P(("groups", "tokens"), None, None),
        P("tensor", "tokens"),
        P(("groups", "tokens"), "tensor"),
        P("tensor"),
        P("tokens", "tensor"),
    )
    out_specs = (P(("groups", "tokens"), "tensor"), P(("groups", "tokens"), "tensor"))
    body = functools.partial(on_ring if n <= RING_LIMIT else on_mesh, n)
    return jax.shard_map(body, mesh=mesh, in_specs=in_specs, out_specs=out_specs, check_vma=False)
```

```python
import functools
import math

import jax
import jax.numpy as jnp
import numpy as np
from jax import lax
from jax.experimental import pallas as pl
from jax.experimental.pallas import tpu as pltpu
from jax.sharding import PartitionSpec as P

D = 16384
H = 128
KVH = 8
HD = 128
EPS_NORM = 1e-05
BF16 = jnp.bfloat16
F32 = jnp.float32
RING_LIMIT = 16
MIB = 1024 * 1024


def dot(a, b):
    return jnp.dot(a, b, preferred_element_type=F32)


def attention_kernel(heads, core_ref, q_ref, own_ref, far_ref, *refs):
    o_ref = refs[-1]
    k_ref, v_ref, pk_ref, pv_ref = own_ref.at[0], own_ref.at[1], far_ref.at[0], far_ref.at[1]
    rows = q_ref.shape[0]
    scale = math.log2(math.e) / math.sqrt(HD)
    query_pos = lax.broadcasted_iota(jnp.int32, (rows, rows), 0)
    key_pos = lax.broadcasted_iota(jnp.int32, (rows, rows), 1)
    visible = key_pos <= query_pos
    peer_visible = core_ref[0] == 1
    contract = (((1,), (1,)), ((), ()))
    for head in range(heads):
        columns = slice(head * HD, (head + 1) * HD)
        query = q_ref[:, columns]
        own = lax.dot_general(query, k_ref[...], contract, preferred_element_type=F32)
        far = lax.dot_general(query, pk_ref[...], contract, preferred_element_type=F32)
        own = jnp.where(visible, own, -1e30)
        far = jnp.where(peer_visible, far, -1e30)
        top = jnp.maximum(jnp.max(own, axis=1, keepdims=True), jnp.max(far, axis=1, keepdims=True))
        own = jnp.exp2((own - top) * scale)
        far = jnp.exp2((far - top) * scale)
        total = jnp.sum(own, axis=1, keepdims=True) + jnp.sum(far, axis=1, keepdims=True)
        mixed = dot(own.astype(BF16), v_ref[...]) + dot(far.astype(BF16), pv_ref[...])
        o_ref[:, columns] = (mixed / total).astype(BF16)


def attention(core, queries, own, far, after=()):
    queries, index, count = queries
    rows, width = queries.shape
    width = width // count
    heads = min(4, width // HD)
    first = index * width // (heads * HD)
    whole = pl.BlockSpec(memory_space=pltpu.VMEM)
    wanted = pl.BlockSpec((rows, heads * HD), lambda h, s: (0, first + h))
    part = pl.BlockSpec((rows, heads * HD), lambda h, s: (0, h))
    return pl.pallas_call(
        functools.partial(attention_kernel, heads),
        grid_spec=pltpu.PrefetchScalarGridSpec(
            num_scalar_prefetch=1,
            grid=(width // (heads * HD),),
            in_specs=[wanted, whole, whole] + [pl.BlockSpec(memory_space=pl.ANY)] * len(after),
            out_specs=part,
        ),
        out_shape=jax.ShapeDtypeStruct((rows, width), BF16),
        compiler_params=pltpu.CompilerParams(vmem_limit_bytes=24 * MIB),
        cost_estimate=pl.CostEstimate(
            flops=8 * rows * rows * width, bytes_accessed=4 * rows * width, transcendentals=2 * rows * rows * width // HD
        ),
        name="attention",
    )(core, queries, own, far, *after)


def project_kernel(info_ref, x_ref, w_ref, *refs):
    own_ref, peer_ref = refs[-2:]
    rows = own_ref.shape[0]
    result = dot(x_ref[...], w_ref[...]).astype(BF16)
    own_ref[...] = result[:rows]
    peer_ref[...] = result[rows:]


def project(info, pair, pieces, piece, both, weight, width, after):
    rows, depth = both.shape
    rows = rows // 2
    tile = min(512, width)
    tiles = width // tile
    out = pl.BlockSpec((rows, tile), lambda j, s: (0, j))
    return pl.pallas_call(
        project_kernel,
        grid_spec=pltpu.PrefetchScalarGridSpec(
            num_scalar_prefetch=1,
            grid=(tiles,),
            in_specs=[
                pl.BlockSpec(memory_space=pltpu.VMEM),
                pl.BlockSpec((depth, tile), lambda j, s: (0, (s[pair] * pieces + piece) * tiles + j)),
            ]
            + [pl.BlockSpec(memory_space=pltpu.VMEM)] * len(after),
            out_specs=[out, out],
        ),
        out_shape=[jax.ShapeDtypeStruct((rows, width), BF16)] * 2,
        compiler_params=pltpu.CompilerParams(vmem_limit_bytes=34 * MIB),
        cost_estimate=pl.CostEstimate(
            flops=4 * rows * depth * width, bytes_accessed=2 * depth * width, transcendentals=0
        ),
        name="project",
    )(info, both, weight, *after)


def query_kernel(codes, sizes, first, info_ref, *refs):
    own_ref, peer_ref, x_ref = refs[-3:]
    rows = own_ref.shape[0]
    start = 0
    fills = []
    for index, (code, groups) in enumerate(zip(codes, sizes)):
        for half_index, (choices, parts) in enumerate(groups):
            fills.append((index, half_index, code, refs[start : start + choices * parts], parts))
            start += choices * parts
    weights = refs[start : start + len(codes)]
    depth = weights[0].shape[0]

    @pl.when(pl.program_id(0) == 0)
    def _():
        for index, half_index, code, blocks, parts in fills:
            place = slice(half_index * rows, (half_index + 1) * rows)
            width = depth // parts
            for choice in range(len(blocks) // parts):

                @pl.when(info_ref[code] == choice if len(blocks) > parts else True)
                def _():
                    for part in range(parts):
                        columns = slice(index * depth + part * width, index * depth + (part + 1) * width)
                        x_ref[place, columns] = blocks[choice * parts + part][...]

    for half_index, out in enumerate((own_ref, peer_ref)):
        place = slice(half_index * rows, (half_index + 1) * rows)
        result = None if first else refs[start + len(codes) + half_index][...]
        for index, w_ref in enumerate(weights):
            product = dot(x_ref[place, index * depth : (index + 1) * depth], w_ref[...])
            result = product if result is None else result + product
        out[...] = result.astype(out.dtype)


def query_block(info, half, blocks, weight, acc, last):
    rows = blocks[0][1][0][0].shape[0]
    depth = sum(piece.shape[1] for piece in blocks[0][1][0])
    width = weight.shape[1]
    tile = min(512, width)
    whole = pl.BlockSpec(memory_space=pltpu.VMEM)
    out = pl.BlockSpec((rows, tile), lambda j, s: (0, j))
    sizes = [[(len(choices), len(choices[0])) for choices in (own, far)] for _, own, far in blocks]
    arrays = [piece for _, own, far in blocks for choices in (own, far) for choice in choices for piece in choice]
    weight_specs = [
        pl.BlockSpec((depth, tile), functools.partial(lambda pair, j, s: (s[pair], j), pair)) for pair, _, _ in blocks
    ]
    return pl.pallas_call(
        functools.partial(query_kernel, [half + pair for pair, _, _ in blocks], sizes, not acc),
        grid_spec=pltpu.PrefetchScalarGridSpec(
            num_scalar_prefetch=1,
            grid=(width // tile,),
            in_specs=[whole] * len(arrays) + weight_specs + [out] * len(acc),
            out_specs=[out, out],
            scratch_shapes=[pltpu.VMEM((2 * rows, depth * len(blocks)), BF16)],
        ),
        out_shape=[
            jax.ShapeDtypeStruct((rows, width), F32),
            jax.ShapeDtypeStruct((rows, width), BF16 if last else F32),
        ],
        compiler_params=pltpu.CompilerParams(vmem_limit_bytes=26 * MIB),
        cost_estimate=pl.CostEstimate(
            flops=4 * rows * depth * width * len(blocks),
            bytes_accessed=2 * depth * width * len(blocks) + 16 * rows * width,
            transcendentals=0,
        ),
        name="next_query",
    )(info, *arrays, *[weight] * len(blocks), *acc)


def add_kernel(total_ref, more_ref, *refs):
    refs[-1][...] = total_ref[...] + more_ref[...]


def add_in_step(total, more, blocks, after):
    whole = pl.BlockSpec(memory_space=pltpu.VMEM)
    *blocks, total = pl.pallas_call(
        add_kernel,
        in_specs=[whole] * (2 + len(blocks) + len(after)),
        out_specs=[whole] * (len(blocks) + 1),
        out_shape=[jax.ShapeDtypeStruct(block.shape, block.dtype) for block in (*blocks, total)],
        input_output_aliases={2 + index: index for index in range(len(blocks))},
        compiler_params=pltpu.CompilerParams(vmem_limit_bytes=4 * MIB),
        name="add_squares",
    )(total, more, *blocks, *after)
    return total, blocks


def hold_kernel(*refs):
    pass


def hold(array, after):
    whole = pl.BlockSpec(memory_space=pltpu.VMEM)
    return pl.pallas_call(
        hold_kernel,
        in_specs=[whole] * (1 + len(after)),
        out_specs=whole,
        out_shape=jax.ShapeDtypeStruct(array.shape, array.dtype),
        input_output_aliases={0: 0},
        compiler_params=pltpu.CompilerParams(vmem_limit_bytes=4 * MIB),
        name="hold",
    )(array, *after)


def pick_kernel(codes, sizes, info_ref, *refs):
    outs = refs[len(refs) - len(codes) :]
    start = 0
    for code, (choices, parts), out in zip(codes, sizes, outs):
        width = out.shape[1] // parts
        for choice in range(choices):

            @pl.when(info_ref[code] == choice)
            def _():
                for part in range(parts):
                    out[:, part * width : (part + 1) * width] = refs[start + choice * parts + part][...]

        start += choices * parts


def pick(info, codes, groups, after):
    whole = pl.BlockSpec(memory_space=pltpu.VMEM)
    arrays = [piece for group in groups for choice in group for piece in choice]
    rows, piece_width = arrays[0].shape
    shape = jax.ShapeDtypeStruct((rows, piece_width * len(groups[0][0])), arrays[0].dtype)
    return pl.pallas_call(
        functools.partial(pick_kernel, codes, [(len(group), len(group[0])) for group in groups]),
        grid_spec=pltpu.PrefetchScalarGridSpec(
            num_scalar_prefetch=1,
            grid=(1,),
            in_specs=[whole] * (len(arrays) + len(after)),
            out_specs=[whole] * len(groups),
        ),
        out_shape=[shape] * len(groups),
        compiler_params=pltpu.CompilerParams(vmem_limit_bytes=4 * MIB),
        name="pick",
    )(info, *arrays, *after)


def ring_of(n):
    return [2 * p for p in range(n // 2)] + [2 * p + 1 for p in reversed(range(n // 2))]


def tables(n):
    half = n // 2
    ring = ring_of(n)
    place = {chip: p for p, chip in enumerate(ring)}
    table = np.zeros((n, 2, 2 * half + n), np.int32)
    for chip in range(n):
        for core in range(2):

            def is_mine(q):
                return ring[(place[chip] + q) % n] // half == core

            for k in range(half):
                near = is_mine(k)
                assert near != is_mine(k - half)
                table[chip, core, k] = ring[(place[chip] + (k if near else k - half)) % n] - core * half
                q = (k if near else k - half) * (1 if core == 0 else -1)
                if k > 0:
                    table[chip, core, half + k] = block_choices(k, half).index(q)
                else:
                    table[chip, core, half] = 0 if near else 1 + core
            for q in range(1 - half, half + 1):
                real = q if core == 0 else -q
                pair = (real % half, 0 if is_mine(real) else 1)
                table[chip, core, 2 * half + q + half - 1] = sum_choices(q, half).index(pair)
    return table.reshape(2 * n, -1)


def block_choices(k, half):
    return list(dict.fromkeys([k, k - half, -k, half - k]))


def sum_choices(q, half):
    return [(k, kind) for k in dict.fromkeys([q % half, -q % half]) for kind in (0, 1)]


def choose(code, arrays):
    result = arrays[-1]
    for index in reversed(range(len(arrays) - 1)):
        result = jnp.where(code == index, arrays[index], result)
    return result


def on_ring(n, att_queries, att_keys, att_values, out_weight, residual, norm_gain, next_weight):
    half = n // 2
    ring = ring_of(n)
    up = [(ring[p], ring[(p + 1) % n]) for p in range(n)]
    swap = [(0, 1), (1, 0)]
    long_way = [(2 * a, 2 * b) for a, b in up] + [(2 * b + 1, 2 * a + 1) for a, b in up]
    short_way = [(2 * b, 2 * a) for a, b in up] + [(2 * a + 1, 2 * b + 1) for a, b in up]
    devices = ("tensor", "tokens")
    chip = lax.axis_index("tensor")
    core = lax.axis_index("tokens")
    rows, width = att_queries.shape
    info = lax.dynamic_index_in_dim(jnp.asarray(tables(n)), chip * 2 + core, 0, keepdims=False)

    heads_here = width // HD
    kv_head = chip * heads_here // (H // KVH)
    own = jnp.stack([lax.dynamic_index_in_dim(array, kv_head, 1, keepdims=False) for array in (att_keys, att_values)])
    far = lax.ppermute(own, "tokens", swap)
    attended, attended_peer = [], []
    for part in range(2):
        queries = (att_queries, part, 2)
        attended.append(attention(core[None], queries, own, far, attended))
        attended_peer.append(lax.ppermute(attended[-1], "tokens", swap))
    both = jnp.concatenate(
        [jnp.concatenate(attended, axis=1), jnp.concatenate(attended_peer, axis=1)], axis=0
    )

    made = {}

    def make(k, after=(), arrivals=()):
        made[k, 0], outgoing = project(info, k, 1, 0, both, out_weight, residual.shape[1], after)
        if arrivals:
            outgoing = hold(outgoing, arrivals)
        made[k, 1] = lax.ppermute(outgoing, "tokens", swap)

    def partial_sum(q):
        return choose(info[2 * half + q + half - 1], [made[key] for key in sum_choices(q, half)]).astype(F32)

    arrived = {}

    def send(way, step, previous):
        q = half - step + 1 if way == "long" else step - half
        value = partial_sum(q)
        if step > 1:
            before = arrived[way]
            if (way, step) == ("short", 2):
                before = hold(before, [arrived["long"]])
            value = value + lax.optimization_barrier((before, previous))[0].astype(F32)
        value = value.astype(BF16)
        arrived[way] = lax.ppermute(value, devices, long_way if way == "long" else short_way)
        return value

    make(0)
    make(1)
    long_value = send("long", 1, None)
    for k in range(half - 1, half // 2, -1):
        make(k, [long_value], [arrived["long"]])
    short_value = send("short", 1, long_value)
    value = send("long", 2, short_value)
    for k in range(2, half // 2 + 1):
        make(k, [short_value, value])
    for step in range(2, half):
        value = send("short", step, value)
        value = send("long", step + 1, value)

    arrived["short"] = hold(arrived["short"], [])
    mixed = residual.astype(F32) + partial_sum(0) + arrived["long"].astype(F32) + arrived["short"].astype(F32)
    resid_out = mixed.astype(BF16)
    scaled = (mixed * norm_gain.astype(F32)).astype(BF16)
    squares = jnp.sum(mixed * mixed, axis=1)[None]

    scaled_peer = lax.ppermute(scaled, "tokens", swap)
    held = {0: scaled}
    groups = {}
    for k in range(1, half):
        groups.setdefault(max(k, half - k), []).append(k)
    reach = 1
    acc, after = (), ()
    for step in range(1, half):
        held[-step] = lax.ppermute(held[1 - step], devices, long_way)
        held[step] = lax.ppermute(held[step - 1], devices, short_way)
        if reach < n:
            more = lax.ppermute(squares, "tensor", [(c, c ^ reach) for c in range(n)])
            squares, (held[-step],) = add_in_step(squares, more, [held[-step]], after)
            reach *= 2
        pairs = groups.get(step, [])
        if pairs:
            wanted = {k: [[held[q]] for q in block_choices(k, half)] for k in pairs}
            others = [[wanted[k][index ^ 1] for index in range(len(wanted[k]))] for k in pairs]
            outgoing = pick(info, [half + k for k in pairs], others, after)
            far = [lax.ppermute(block, "tokens", swap) for block in outgoing]
            blocks = [(k, wanted[k], [[block]]) for k, block in zip(pairs, far)]
            acc = query_block(info, half, blocks, next_weight, acc, False)
            after = acc[:1]
    while reach < n:
        squares = squares + lax.ppermute(squares, "tensor", [(c, c ^ reach) for c in range(n)])
        reach *= 2
    meets = {b: ring[(p + half) % n] // half for p, b in enumerate(ring)}
    last_hop = [
        lax.ppermute(held[1 - half], devices, [(2 * a, 2 * b + meets[b]) for a, b in up]),
        lax.ppermute(held[1 - half], devices, [(2 * b + 1, 2 * a + meets[a]) for a, b in up]),
    ]
    own = [[scaled], *[[block] for block in last_hop]]
    far = [[scaled_peer], *[[block] for block in reversed(last_hop)]]
    acc = query_block(info, half, [(0, own, far)], next_weight, acc, True)
    query_sum = acc[0] + lax.ppermute(acc[1], "tokens", swap).astype(F32)
    factor = 1.0 / jnp.sqrt(squares[0] / D + EPS_NORM)
    return (resid_out, (query_sum * factor[:, None]).astype(BF16))


def on_mesh(n, att_queries, att_keys, att_values, out_weight, residual, norm_gain, next_weight):
    rows, width = att_queries.shape
    swap = [(0, 1), (1, 0)]
    chip = lax.axis_index("tensor")
    core = lax.axis_index("tokens")
    kv_head = chip * (width // HD) // (H // KVH)
    own = jnp.stack([lax.dynamic_index_in_dim(array, kv_head, 1, keepdims=False) for array in (att_keys, att_values)])
    far = lax.ppermute(own, "tokens", swap)
    attended = attention(core[None], (att_queries, 0, 1), own, far)
    both = lax.all_gather(attended, "tokens", axis=0, tiled=True)
    partial = dot(both, out_weight).astype(BF16)
    partial = lax.all_to_all(partial, "tokens", split_axis=0, concat_axis=1, tiled=True)
    attn_out = lax.psum_scatter(partial.astype(F32), "tensor", scatter_dimension=1, tiled=True)
    mixed = residual.astype(F32) + attn_out
    total_squares = lax.psum(jnp.sum(mixed * mixed, axis=1), "tensor")
    factor = 1.0 / jnp.sqrt(total_squares / D + EPS_NORM)
    normed = (mixed * factor[:, None] * norm_gain.astype(F32)).astype(BF16)
    gathered = lax.all_gather(normed, "tensor", axis=1, tiled=True)
    halves = lax.all_to_all(gathered, "tokens", split_axis=1, concat_axis=0, tiled=True)
    query_sum = lax.psum_scatter(dot(halves, next_weight), "tokens", scatter_dimension=0, tiled=True)
    return (mixed.astype(BF16), query_sum.astype(BF16))


def solution(mesh):
    n = mesh.shape["tensor"]
    in_specs = (
        P(("groups", "tokens"), "tensor"),
        P(("groups", "tokens"), None, None),
        P(("groups", "tokens"), None, None),
        P("tensor", "tokens"),
        P(("groups", "tokens"), "tensor"),
        P("tensor"),
        P("tokens", "tensor"),
    )
    out_specs = (P(("groups", "tokens"), "tensor"), P(("groups", "tokens"), "tensor"))
    body = functools.partial(on_ring if n <= RING_LIMIT else on_mesh, n)
    return jax.shard_map(body, mesh=mesh, in_specs=in_specs, out_specs=out_specs, check_vma=False)
```
